256 devices in a mesh: slot: 64 (over y_lo, z, x), head: 4 (over y_hi, core).
Axes of the slice: x: 4, y: 4 (y_hi: 2, y_lo: 2; y = y_hi * 2 + y_lo), z: 8, core: 2. Of those that a mesh axis runs over, the one named last changes fastest.
Arguments:
- queries: bfloat16 [4096, 6144], P('slot', 'head'), may hold values from -4.5 to 4.5
- keys: bfloat16 [4096, 1024], P('slot', 'head'), may hold values from -4.5 to 4.5
- values: bfloat16 [4096, 1024], P('slot', 'head'), may hold values from -4.5 to 4.5
- cache_keys: bfloat16 [16384, 1024], P('slot', 'head'), may hold values from -4.5 to 4.5
- cache_values: bfloat16 [16384, 1024], P('slot', 'head'), may hold values from -4.5 to 4.5
- cache_count: int32 [64], P('slot'), may hold values from 1 to 240
- span_section: int32 [4], replicated, may hold values from 0 to 3, each once
- norm_gain: float32 [6144], P('head'), may hold values from 0.5 to 1.5
Outputs:
- attended: float32 [4096, 6144], P('slot', 'head')
- new_cache_keys: bfloat16 [16384, 1024], P('slot', 'head')
- new_cache_values: bfloat16 [16384, 1024], P('slot', 'head')
The draws below stay inside these ranges and needn't reach their ends.
Inputs may be any that keep to these rules, and one draw needn't show every extreme that they name: `span_section`: the noise section of each group; 0 marks the span that retires.
All inputs are finite; a program needn't handle non-finite values.
Results may differ from the reference program's by a relative error of at most 0.0085.
Values may be sent and summed in bfloat16 or wider, within the bound.
A program may use at most 64 MiB of HBM per device.

```python
import jax
import jax.numpy as jnp
from jax import lax

HEADS = 48
KV_HEADS = 8
HEAD = 128
TOK_DEV = 64
CACHE_DEV = 256
D = 6144
KVW = 1024
RATIO = 6
GROUP_SIZE = 16
SPAN_TOK = 1024
TOKENS = 4096
CACHE_ROWS = 16384
RETIRE_ROWS = 16
N_SLOT = 64


def shared_pattern(key):
    width = KV_HEADS * HEAD
    signs = jnp.where(jax.random.bernoulli(key, 0.5, (TOKENS, width)), 1.0, -1.0)
    rows = jnp.arange(TOKENS)
    strength = 3.5 + 0.5 * (rows // TOK_DEV % 3).astype(jnp.float32)
    return signs * strength[:, None]


def column_scale(key, width):
    cols = jnp.arange(width).astype(jnp.float32)
    rough = jax.random.uniform(key, (width,), jnp.float32, 0.8, 1.2)
    return (0.6 + 1.2 * cols / (width - 1)) * rough


def draw_queries(key, part):
    pattern = shared_pattern(key)
    widened = jnp.repeat(pattern.reshape(TOKENS, KV_HEADS, 1, HEAD), HEADS // KV_HEADS, axis=2)
    widened = widened.reshape(TOKENS, HEADS * HEAD)
    key = jax.random.fold_in(key, 11)
    base = jax.random.truncated_normal(key, -4.5, 4.5, widened.shape, jnp.float32)
    return base.astype(jnp.bfloat16)


def draw_keys(key, part):
    pattern = shared_pattern(key)
    key = jax.random.fold_in(key, 12)
    base = jax.random.truncated_normal(key, -4.5, 4.5, pattern.shape, jnp.float32)
    return base.astype(jnp.bfloat16)


def draw_values(key, part):
    key = jax.random.fold_in(key, 13)
    width = KV_HEADS * HEAD
    scale = column_scale(jax.random.fold_in(key, 1), width)
    base = jax.random.truncated_normal(jax.random.fold_in(key, 2), -2.0, 2.0, (TOKENS, width), jnp.float32)
    return (base * scale[None, :]).astype(jnp.bfloat16)


def draw_cache_values(key, part):
    key = jax.random.fold_in(key, 14)
    width = KV_HEADS * HEAD
    scale = column_scale(jax.random.fold_in(key, 1), width)
    base = jax.random.truncated_normal(jax.random.fold_in(key, 2), -2.0, 2.0, (CACHE_ROWS, width), jnp.float32)
    return (base * scale[None, :]).astype(jnp.bfloat16)


def draw_cache_count(key, part):
    key = jax.random.fold_in(key, 17)
    most = CACHE_DEV - RETIRE_ROWS
    counts = jax.random.randint(jax.random.fold_in(key, 1), (N_SLOT,), 1, most + 1, jnp.int32)
    chosen = jax.random.randint(jax.random.fold_in(key, 2), (), 0, N_SLOT, jnp.int32)
    return counts.at[chosen].set(most)


def block_scale(own_key, dims, split, smallest, top_value):
    level = 1.0
    for position, blocks in split:
        steps = jax.random.uniform(jax.random.fold_in(jax.random.fold_in(own_key, 6), position), (blocks,), jnp.float32, smallest / len(split), top_value / len(split))
        level = level * jnp.repeat(jnp.exp(steps), dims[position] // blocks).reshape((-1,) + (1,) * (len(dims) - 1 - position))
    return level


def scatter_about(rng, dims, scale, reach, cuts=(), kind=jnp.bfloat16):
    result = scale * jax.random.normal(rng, dims, jnp.float32)
    if cuts:
        result = result * block_scale(rng, dims, cuts, -0.22, 0.18)
    return jnp.clip(result, -reach, reach).astype(kind)


def setup_inputs(seed: int = 0) -> dict:
    key_of = jax.random.split(jax.random.key(seed), 9)
    return {
        "queries": draw_queries(jax.random.fold_in(key_of[8], 71), 0),
        "keys": draw_keys(jax.random.fold_in(key_of[8], 71), 0),
        "values": draw_values(jax.random.fold_in(key_of[8], 71), 0),
        "cache_keys": scatter_about(key_of[3], (CACHE_ROWS, KVW), 1.0, 4.5, ((0, 64), (1, 4))),
        "cache_values": draw_cache_values(jax.random.fold_in(key_of[8], 71), 0),
        "cache_count": draw_cache_count(jax.random.fold_in(key_of[8], 71), 0),
        "span_section": jax.random.permutation(key_of[6], 4).astype(jnp.int32),
        "norm_gain": jnp.clip(1.0 + 0.1 * jax.random.normal(key_of[7], (D,), jnp.float32), 0.5, 1.5),
    }


def head_attention(query_h, key_h, value_h, visible):
    score = jnp.dot(query_h, key_h.T, preferred_element_type=jnp.float32) * HEAD ** (-0.5)
    score = jnp.where(visible[None, :], score, -1e+30)
    top = lax.optimization_barrier(jnp.max(score, axis=1))
    expo = jnp.where(visible[None, :], jnp.exp(score - top[:, None]), 0.0)
    total = lax.optimization_barrier(jnp.sum(expo, axis=1))
    mixed = jnp.dot(expo.astype(jnp.bfloat16), value_h, preferred_element_type=jnp.float32)
    return mixed / total[:, None]

def split_kv(array):
    return array.reshape(array.shape[0], KV_HEADS, HEAD).transpose(1, 0, 2)

def reference(queries, keys, values, cache_keys, cache_values, cache_count, span_section, norm_gain):
    token_rows = jnp.arange(TOKENS, dtype=jnp.int32)
    row_group = token_rows // SPAN_TOK
    cache_index = jnp.arange(CACHE_ROWS, dtype=jnp.int32)
    cache_live = cache_index % CACHE_DEV < cache_count[cache_index // CACHE_DEV]
    all_keys = split_kv(jnp.concatenate([keys, cache_keys], axis=0))
    all_values = split_kv(jnp.concatenate([values, cache_values], axis=0))
    blocks = []
    for group in range(4):
        section = span_section[group]
        visible = jnp.concatenate([span_section[row_group] <= section, cache_live])
        group_queries = queries[group * SPAN_TOK:(group + 1) * SPAN_TOK]
        group_queries = group_queries.reshape(SPAN_TOK, KV_HEADS, RATIO, HEAD).transpose(1, 2, 0, 3)

        def kv_step(items):
            return lax.map(lambda query_h: head_attention(query_h, items[1], items[2], visible), items[0])
        per_head = lax.map(kv_step, (group_queries, all_keys, all_values))
        blocks.append(per_head.transpose(2, 0, 1, 3).reshape(SPAN_TOK, HEADS * HEAD))
    mixed = jnp.concatenate(blocks, axis=0)
    meansq = lax.optimization_barrier(jnp.mean(mixed * mixed, axis=1))
    attended = mixed * lax.rsqrt(meansq + 1e-06)[:, None] * norm_gain[None, :]
    retiring = jnp.sum(jnp.arange(4, dtype=jnp.int32) * (span_section == 0).astype(jnp.int32)).astype(jnp.int32)
    start = (retiring * SPAN_TOK).astype(jnp.int32)

    def retire(source, cache):
        span = lax.dynamic_slice_in_dim(source, start, SPAN_TOK, 0)
        span = span.reshape(GROUP_SIZE, 4, RETIRE_ROWS, KVW).transpose(1, 0, 2, 3)
        span = span.reshape(N_SLOT, RETIRE_ROWS, KVW)
        shards = cache.reshape(N_SLOT, CACHE_DEV, KVW)
        placed = jax.vmap(lambda shard, rows, count: lax.dynamic_update_slice(shard, rows, (count.astype(jnp.int32), jnp.zeros((), jnp.int32))))(shards, span, cache_count)
        return placed.reshape(CACHE_ROWS, KVW)
    return (attended, retire(keys, cache_keys), retire(values, cache_values))
```

```python
import functools

import jax
import jax.numpy as jnp
from jax import lax
from jax.experimental import pallas as pl
from jax.experimental.pallas import tpu as pltpu
from jax.sharding import PartitionSpec as P

MESH = pl.DeviceIdType.MESH
F32 = jnp.float32
BF16 = jnp.bfloat16

HEADS = 48
HEAD = 128
TOK = 64
CACHE = 256
KEYS = TOK + CACHE
KROWS = KEYS + 16
KCUT = 176
VCUT = 160
HERE = 12
SHARE = 6
W = HERE * HEAD
HALF = TOK // 2
LOG2E = 1.4426950408889634
C = HEAD ** -0.5 * LOG2E
NEG = -1e30
NZ, NX = 8, 4


def kernel(
    q_ref, k_ref, v_ref, ck_ref, cv_ref, gain_ref, count_ref, section_ref,
    out_ref, nck_ref, ncv_ref,
    qg, kbuf, vbuf, rbuf, bias, o_a, l_a, o_cur, l_cur, sbuf, mbuf, sq_s, sq_r,
    q_send, q_recv, k_send, k_recv, v_send, v_recv, r_send, r_recv, o_send, o_recv, s_send, s_recv,
):
    slot = lax.axis_index("slot")
    head = lax.axis_index("head")
    y = slot // 32
    z = slot // 4 % 8
    x = slot % 4

    def at(y_, z_, x_):
        return (y_ * 32 + z_ * 4 + x_, head)

    z_dev = (at(y, (z + 1) % NZ, x), at(y, (z + 7) % NZ, x))
    x_dev = (at(y, z, (x + 1) % NX), at(y, z, (x + 3) % NX))
    y_dev = at(1 - y, z, x)
    col_dev = (y_dev, at(y, (z + 4) % NZ, x), at(1 - y, (z + 4) % NZ, x))
    head_dev = tuple((slot, (head // 2 * 2 + (1 - head % 2), (head + 2) % 4, (head + 2) % 4 // 2 * 2 + (1 - head % 2))[i]) for i in range(3))

    barrier = pltpu.get_barrier_semaphore()
    peers = z_dev + x_dev + col_dev + head_dev
    for peer in peers:
        pl.semaphore_signal(barrier, inc=1, device_id=peer, device_id_type=MESH)

    qg[0] = q_ref[...]
    kbuf[0, 0, 0:TOK] = k_ref[...]
    kbuf[0, 0, TOK:KEYS] = ck_ref[...]
    kbuf[0, 0, KEYS:KROWS] = jnp.full((16, 256), count_ref[0].astype(F32), F32).astype(BF16)
    vbuf[0, 0, 0:TOK] = v_ref[...]
    vbuf[0, 0, TOK:KEYS] = cv_ref[...]
    pl.semaphore_wait(barrier, len(peers))

    def remote(src, dst, send, recv, dev):
        return pltpu.make_async_remote_copy(
            src_ref=src, dst_ref=dst, send_sem=send, recv_sem=recv, device_id=dev, device_id_type=MESH
        )

    def q_rows(ref, e, p):
        return ref.at[e, p * HALF:(p + 1) * HALF]

    def q_copy(d, step, p):
        src = (-step if d == 0 else step) % NZ
        dst = (-step - 1 if d == 0 else step + 1) % NZ
        return remote(q_rows(qg, src, p), q_rows(qg, dst, p), q_send.at[d, step, p], q_recv.at[d, step, p], z_dev[d])

    def k_copies():
        full = lambda h, s: kbuf.at[h, s]
        lo = lambda h, s: kbuf.at[h, s, 0:KCUT]
        hi = lambda h, s: kbuf.at[h, s, KCUT:KROWS]
        table = {
            "own_up": (full(0, 0), full(0, 1), x_dev[0]),
            "own_down": (full(0, 0), full(0, 2), x_dev[1]),
            "own_y": (full(0, 0), full(0, 3), y_dev),
            "fwd_up": (lo(0, 1), lo(1, 0), x_dev[0]),
            "fwd_down": (hi(0, 2), hi(1, 0), x_dev[1]),
            "y_up": (full(0, 3), full(1, 1), x_dev[0]),
            "y_down": (full(0, 3), full(1, 2), x_dev[1]),
            "yf_up": (lo(1, 1), lo(1, 3), x_dev[0]),
            "yf_down": (hi(1, 2), hi(1, 3), x_dev[1]),
        }
        return {n: remote(s, d, k_send.at[i], k_recv.at[i], dev) for i, (n, (s, d, dev)) in enumerate(table.items())}

    def v_copies():
        full = lambda h, s: vbuf.at[h, s]
        lo = lambda h, s: vbuf.at[h, s, 0:VCUT]
        hi = lambda h, s: vbuf.at[h, s, VCUT:KEYS]
        table = {
            "own_up": (full(0, 0), full(0, 1), x_dev[0]),
            "own_down": (full(0, 0), full(0, 2), x_dev[1]),
            "own_y": (full(0, 0), full(0, 3), y_dev),
            "fwd_up": (lo(0, 1), lo(1, 0), x_dev[0]),
            "fwd_down": (hi(0, 2), hi(1, 0), x_dev[1]),
            "y_1": (full(0, 1), full(1, 1), y_dev),
            "y_2": (full(0, 2), full(1, 2), y_dev),
            "y_3": (full(1, 0), full(1, 3), y_dev),
        }
        return {n: remote(s, d, v_send.at[i], v_recv.at[i], dev) for i, (n, (s, d, dev)) in enumerate(table.items())}

    kc, vc = k_copies(), v_copies()

    def retire_copies():
        out = []
        for i, dev in enumerate(col_dev):
            group = dev[0] // 16
            rows = pl.ds(pl.multiple_of(group * 16, 16), 16)
            out.append(remote(kbuf.at[0, 0, rows], rbuf.at[0, i], r_send.at[0, i], r_recv.at[0, i], dev))
            out.append(remote(vbuf.at[0, 0, rows], rbuf.at[1, i], r_send.at[1, i], r_recv.at[1, i], dev))
        return out

    rc = retire_copies()

    for p in (0, 1):
        for d in (0, 1):
            q_copy(d, 0, p if d == 0 else 1 - p).start()
            if p == 0:
                kc[("own_up", "own_down")[d]].start()
        if p == 0:
            kc["own_y"].start()
    vc["own_up"].start()
    vc["own_down"].start()
    vc["own_y"].start()
    for copy in rc:
        copy.start()

    def q_pass(step, first):
        for d in (0, 1):
            p = d if first else 1 - d
            q_copy(d, step, p).wait_recv()
            if step < 2 or (step == 2 and first):
                q_copy(d, step + 1, p).start()

    q_pass(0, True)
    q_pass(0, False)
    for n, f in (("own_up", "fwd_up"), ("own_down", "fwd_down")):
        kc[n].wait_recv()
        kc[f].start()
    kc["own_y"].wait_recv()
    kc["y_up"].start()
    kc["y_down"].start()
    q_pass(1, True)
    for n, f, t in (("own_up", "fwd_up", "y_1"), ("own_down", "fwd_down", "y_2")):
        vc[n].wait_recv()
        vc[f].start()
        vc[t].start()
    vc["own_y"].wait_recv()

    lane = lax.broadcasted_iota(jnp.int32, (1, 4 * KEYS), 1)

    def make_bias(half):
        for qhi in (0, 1):
            mine = section_ref[y * 2 + qhi]
            total = jnp.zeros((1, 4 * KEYS), F32)
            for s in range(4):
                other = (s == 3) if half == 0 else (s > 0)
                ky = 1 - y if other else y
                seen = section_ref[ky * 2 + z // 4] <= mine
                tok = jnp.where(seen, 0.0, NEG).astype(F32)
                live = kbuf[half, s, KEYS:KROWS, 0:128].astype(F32)[0:1, 0:1]
                row = lane - s * KEYS
                dead = jnp.where((row - TOK).astype(F32) >= live, NEG, 0.0)
                here = (row >= 0) & (row < KEYS)
                total = jnp.where(here, jnp.where(row < TOK, tok, dead), total)
            bias[half, qhi] = total

    ones = jnp.ones((4 * KEYS, HEAD), BF16)

    def attend(half, e, g):
        qhi = (z + e) % NZ // 4
        q = jnp.concatenate([qg[e, :, (g * SHARE + h) * HEAD:(g * SHARE + h + 1) * HEAD] for h in range(SHARE)], 0)
        k = jnp.concatenate([kbuf[half, s, 0:KEYS, g * HEAD:(g + 1) * HEAD] for s in range(4)], 0)
        v = jnp.concatenate([vbuf[half, s, :, g * HEAD:(g + 1) * HEAD] for s in range(4)], 0)
        score = lax.dot_general(q, k, (((1,), (1,)), ((), ())), preferred_element_type=F32)
        score = score + bias[half, qhi]
        top = jnp.max(score, axis=1, keepdims=True)
        weight = jnp.exp2((score - top) * C).astype(BF16)
        mixed = jnp.dot(weight, jnp.concatenate([v, ones], 1), preferred_element_type=F32)
        total = mixed[:, HEAD:]
        return mixed[:, :HEAD] / total, top * C + jnp.log2(total)

    def merge(o1, l1, o2, l2):
        top = jnp.maximum(l1, l2)
        w1 = jnp.exp2(l1 - top)
        w2 = jnp.exp2(l2 - top)
        total = w1 + w2
        return (o1 * w1 + o2 * w2) / total, top + jnp.log2(total)

    make_bias(0)

    def phase_a(i, carry):
        e = jnp.where(i % 2 == 1, NZ - (i + 1) // 2, i // 2)

        @pl.when(i == 1)
        def _():
            q_pass(1, False)

        @pl.when(i == 2)
        def _():
            q_pass(2, True)

        @pl.when(i == 3)
        def _():
            for n in ("fwd_up", "fwd_down"):
                kc[n].wait_recv()
                vc[n].wait_recv()
            vc["y_3"].start()

        @pl.when(i == 4)
        def _():
            for n, f in (("y_up", "yf_up"), ("y_down", "yf_down")):
                kc[n].wait_recv()
                kc[f].start()

        @pl.when(i == 5)
        def _():
            q_pass(2, False)

        @pl.when(i == 7)
        def _():
            q_pass(3, True)

        for g in (0, 1):
            o, l = attend(0, e, g)
            for h in range(SHARE):
                cols = slice((g * SHARE + h) * HEAD, (g * SHARE + h + 1) * HEAD)
                o_a[e, :, cols] = o[h * TOK:(h + 1) * TOK]
                l_a[e, :, cols] = l[h * TOK:(h + 1) * TOK]
        return carry

    lax.fori_loop(0, NZ, phase_a, 0)

    for n in ("yf_up", "yf_down"):
        kc[n].wait_recv()
    for n in ("y_1", "y_2", "y_3"):
        vc[n].wait_recv()
    make_bias(1)

    lane128 = lax.broadcasted_iota(jnp.int32, (HALF, HEAD), 1)

    def o_copy(d, step, p):
        rows = pl.ds(pl.multiple_of(p * HALF, HALF), HALF)
        dev = at(y, (z + 1 + 6 * d) % NZ, x)
        return remote(sbuf.at[d, step, rows], mbuf.at[d, step, rows], o_send.at[d, step, p], o_recv.at[d, step, p], dev)

    def read_message(d, step, p):
        o_copy(d, step, p).wait_recv()
        rows = pl.ds(pl.multiple_of(p * HALF, HALF), HALF)
        packed = mbuf[d, step, rows, W:W + HEAD].astype(F32)
        stat = packed + pltpu.roll(packed, HEAD - 16, 1) + pltpu.roll(packed, HEAD - 32, 1)
        return rows, stat

    def send_piece(d, step, p, combine):
        rows = pl.ds(pl.multiple_of(p * HALF, HALF), HALF)
        if combine:
            _, stat = read_message(d, step - 1, p)
        packed = jnp.zeros((HALF, HEAD), F32)
        for h in range(HERE):
            cols = slice(h * HEAD, (h + 1) * HEAD)
            o = o_cur[rows, cols]
            l = l_cur[rows, cols]
            if combine:
                o2 = mbuf[d, step - 1, rows, cols].astype(F32)
                l2 = jnp.broadcast_to(stat[:, h:h + 1], (HALF, HEAD))
                o, l = merge(o, l, o2, l2)
            sbuf[d, step, rows, cols] = o.astype(BF16)
            packed = jnp.where(lane128 % 16 == h, l, packed)
        first = packed.astype(BF16).astype(F32)
        rest = packed - first
        second = rest.astype(BF16).astype(F32)
        third = rest - second
        parts = jnp.where(lane128 < 16, first, jnp.where(lane128 < 32, second, third))
        parts = jnp.where(lane128 < 48, parts, 0.0)
        sbuf[d, step, rows, W:W + HEAD] = parts.astype(BF16)
        o_copy(d, step, p).start()

    def phase_b(i, carry):
        j = NZ - 1 - i
        e = jnp.where(j % 2 == 1, NZ - (j + 1) // 2, j // 2)
        for g in (0, 1):
            o, l = attend(1, e, g)
            for h in range(SHARE):
                cols = slice((g * SHARE + h) * HEAD, (g * SHARE + h + 1) * HEAD)
                part = slice(h * TOK, (h + 1) * TOK)
                o2, l2 = merge(o[part], l[part], o_a[e, :, cols], l_a[e, :, cols])
                o_cur[:, cols] = o2
                l_cur[:, cols] = l2

        d = 1 - i % 2
        step = (i + 1) // 2

        @pl.when(i == 0)
        def _():
            send_piece(0, 0, 0, False)
            send_piece(1, 0, 1, False)

        @pl.when((i > 0) & (i < 7))
        def _():
            send_piece(d, step, d, True)

        @pl.when((i > 0) & (i < 3))
        def _():
            send_piece(d, step, 1 - d, False)

        @pl.when((i > 2) & (i < 7))
        def _():
            send_piece(d, step, 1 - d, True)

        return carry

    lax.fori_loop(0, NZ, phase_b, 0)

    for p in (0, 1):
        rows = slice(p * HALF, (p + 1) * HALF)
        _, stat0 = read_message(0, 3, p)
        _, stat1 = read_message(1, 3, p)
        squares = jnp.zeros((HALF, HEAD), F32)
        for h in range(HERE):
            cols = slice(h * HEAD, (h + 1) * HEAD)
            o, l = o_cur[rows, cols], l_cur[rows, cols]
            for d, stat in ((0, stat0), (1, stat1)):
                l2 = jnp.broadcast_to(stat[:, h:h + 1], (HALF, HEAD))
                o, l = merge(o, l, mbuf[d, 3, rows, cols].astype(F32), l2)
            o_cur[rows, cols] = o
            squares = squares + o * o
        sq_s[rows, :] = jnp.broadcast_to(jnp.sum(squares, axis=1, keepdims=True), (HALF, HEAD))
    sc = [remote(sq_s, sq_r.at[i], s_send.at[i], s_recv.at[i], head_dev[i]) for i in range(3)]
    for copy in sc:
        copy.start()

    for copy in rc:
        copy.wait_recv()
    group = y * 2 + z // 4
    own_rows = pl.ds(pl.multiple_of(group * 16, 16), 16)
    own_group = section_ref[group] == 0
    spot = lax.broadcasted_iota(jnp.int32, (CACHE, 16), 0) - lax.broadcasted_iota(jnp.int32, (CACHE, 16), 1)
    pick = jnp.where(spot == count_ref[0], 1.0, 0.0).astype(BF16)
    row = lax.broadcasted_iota(jnp.int32, (CACHE, 256), 0) - count_ref[0]
    fresh = (row >= 0) & (row < 16)
    for i, (buf, old, new) in enumerate(((kbuf, ck_ref, nck_ref), (vbuf, cv_ref, ncv_ref))):
        got = jnp.where(own_group, buf[0, 0, own_rows].astype(F32), 0.0)
        for j, dev in enumerate(col_dev):
            got = jnp.where(section_ref[dev[0] // 16] == 0, rbuf[i, j].astype(F32), got)
        moved = jnp.dot(pick, got.astype(BF16), preferred_element_type=F32)
        new[...] = jnp.where(fresh, moved, old[...].astype(F32)).astype(BF16)

    total = sq_s[...]
    for i, copy in enumerate(sc):
        copy.wait_recv()
        total = total + sq_r[i]
    scale = lax.rsqrt(total / (HEADS * HEAD) + 1e-06)
    for h in range(HERE):
        cols = slice(h * HEAD, (h + 1) * HEAD)
        out_ref[:, cols] = o_cur[:, cols] * scale * gain_ref[:, cols]

    for d in (0, 1):
        for step in range(4):
            for p in (0, 1):
                if step < 3 or p == d:
                    q_copy(d, step, p).wait_send()
                if step > 0 or p == d:
                    o_copy(d, step, p).wait_send()
    for copy in list(kc.values()) + list(vc.values()) + rc + sc:
        copy.wait_send()


def on_device(queries, keys, values, cache_keys, cache_values, cache_count, span_section, norm_gain):
    vmem = pl.BlockSpec(memory_space=pltpu.VMEM)
    smem = pl.BlockSpec(memory_space=pltpu.SMEM)
    dma = pltpu.SemaphoreType.DMA
    return pl.pallas_call(
        kernel,
        out_shape=[
            jax.ShapeDtypeStruct((TOK, W), F32),
            jax.ShapeDtypeStruct((CACHE, 256), BF16),
            jax.ShapeDtypeStruct((CACHE, 256), BF16),
        ],
        in_specs=[vmem] * 6 + [smem] * 2,
        out_specs=[vmem] * 3,
        scratch_shapes=[
            pltpu.VMEM((NZ, TOK, W), BF16),
            pltpu.VMEM((2, 4, KROWS, 256), BF16),
            pltpu.VMEM((2, 4, KEYS, 256), BF16),
            pltpu.VMEM((2, 3, 16, 256), BF16),
            pltpu.VMEM((2, 2, 1, 4 * KEYS), F32),
            pltpu.VMEM((NZ, TOK, W), F32),
            pltpu.VMEM((NZ, TOK, W), F32),
            pltpu.VMEM((TOK, W), F32),
            pltpu.VMEM((TOK, W), F32),
            pltpu.VMEM((2, 4, TOK, W + HEAD), BF16),
            pltpu.VMEM((2, 4, TOK, W + HEAD), BF16),
            pltpu.VMEM((TOK, HEAD), F32),
            pltpu.VMEM((3, TOK, HEAD), F32),
            dma((2, 4, 2)), dma((2, 4, 2)),
            dma((9,)), dma((9,)),
            dma((8,)), dma((8,)),
            dma((2, 3)), dma((2, 3)),
            dma((2, 4, 2)), dma((2, 4, 2)),
            dma((3,)), dma((3,)),
        ],
        compiler_params=pltpu.CompilerParams(
            collective_id=0, has_side_effects=True, vmem_limit_bytes=56 * 2**20
        ),
    )(queries, keys, values, cache_keys, cache_values, norm_gain.reshape(1, W), cache_count, span_section)


def solution(mesh):
    placed = (
        P("slot", "head"),
        P("slot", "head"),
        P("slot", "head"),
        P("slot", "head"),
        P("slot", "head"),
        P("slot"),
        P(),
        P("head"),
    )
    return jax.shard_map(
        on_device,
        mesh=mesh,
        in_specs=placed,
        out_specs=(P("slot", "head"), P("slot", "head"), P("slot", "head")),
        check_vma=False,
    )
```

```python
import functools

import jax
import jax.numpy as jnp
from jax import lax
from jax.experimental import pallas as pl
from jax.experimental.pallas import tpu as pltpu
from jax.sharding import PartitionSpec as P

MESH = pl.DeviceIdType.MESH
F32 = jnp.float32
BF16 = jnp.bfloat16

HEADS = 48
HEAD = 128
TOK = 64
CACHE = 256
KEYS = TOK + CACHE
KVR = 2 * KEYS + 16
SHARE = 6
GW = SHARE * HEAD
MW = GW + HEAD
HALF = TOK // 2
PAIR = 2 * SHARE * TOK
SPAN = 4 * KEYS
TILE = 256
C = HEAD ** -0.5 * 1.4426950408889634
NEG = -1e30
NZ, NX = 8, 4
Z_ORDER = (0, 1, 7, 2, 6, 3, 5, 4)
G1_FIRST = (7, 5, 1, 3)
G1_SECOND = (4, 6, 2, 0)
MSG = {}
for _name, _rows in (
    ("y7", 32), ("y5", 32), ("y6", 32), ("y3", 32), ("x1u", 32), ("x1d", 32), ("xx1u", 16), ("xx1d", 16),
    ("x2u0", 32), ("x2u1", 32), ("x2d0", 32), ("x2d1", 32), ("xx2u", 32), ("xx2d", 32), ("yf", 32),
):
    MSG[_name] = (len(MSG), sum(r for _, _, r in MSG.values()), _rows)
MSG_ROWS = sum(r for _, _, r in MSG.values())


def kernel(
    q_ref, k_ref, v_ref, ck_ref, cv_ref, gain_ref, count_ref, section_ref,
    out_ref, nck_ref, ncv_ref,
    qg, kv, bias, acc, l_st, m_st, s0, s1, mx0, mx1, al0, al1,
    sb0, mb0, sb1, mb1, rt_s, rt_y, rz_s, rz_r, sq_s, sq_r,
    zq_send, zq_recv, zk_send, zk_recv, xk_send, xk_recv, xq_send, xq_recv,
    r_send, r_recv, o_send, o_recv, p_send, p_recv, h_send, h_recv,
):
    slot = lax.axis_index("slot")
    head = lax.axis_index("head")
    y = slot // 32
    z = slot // 4 % 8
    x = slot % 4
    zhi = z // 4

    def at(y_, z_, x_):
        return (y_ * 32 + z_ * 4 + x_, head)

    z_dev = (at(y, (z + 1) % NZ, x), at(y, (z + 7) % NZ, x))
    x_dev = (at(y, z, (x + 1) % NX), at(y, z, (x + 3) % NX))
    y_dev = at(1 - y, z, x)
    far_dev = at(y, (z + 4) % NZ, x)
    pair_core = 1 - head % 2
    head_dev = ((slot, head // 2 * 2 + pair_core), (slot, (head + 2) % 4), (slot, (head + 2) % 4 // 2 * 2 + pair_core))

    barrier = pltpu.get_barrier_semaphore()
    peers = z_dev + x_dev + (y_dev,) + head_dev
    for peer in peers:
        pl.semaphore_signal(barrier, inc=1, device_id=peer, device_id_type=MESH)

    for g in (0, 1):
        cols = slice(g * HEAD, (g + 1) * HEAD)
        qg[g, 0] = q_ref[:, g * GW:(g + 1) * GW]
        kv[2 * g, 0, 0:TOK] = k_ref[:, cols]
        kv[2 * g, 0, TOK:KEYS] = ck_ref[:, cols]
        kv[2 * g, 0, KEYS:KEYS + TOK] = v_ref[:, cols]
        kv[2 * g, 0, KEYS + TOK:2 * KEYS] = cv_ref[:, cols]
        kv[2 * g, 0, 2 * KEYS:KVR] = jnp.full((16, HEAD), count_ref[0].astype(F32), F32).astype(BF16)

    def tokens(ref, group):
        return ref[pl.ds(pl.multiple_of(group * 16, 16), 16)]

    for i, group in enumerate(((1 - y) * 2 + zhi, (1 - y) * 2 + 1 - zhi)):
        rt_s[32 * i:32 * i + 16] = tokens(k_ref, group)
        rt_s[32 * i + 16:32 * i + 32] = tokens(v_ref, group)
    m_st[...] = jnp.full(m_st.shape, NEG, F32)
    l_st[...] = jnp.zeros(l_st.shape, F32)
    acc[...] = jnp.zeros(acc.shape, F32)
    pl.semaphore_wait(barrier, len(peers))

    def remote(src, dst, send, recv, dev):
        return pltpu.make_async_remote_copy(
            src_ref=src, dst_ref=dst, send_sem=send, recv_sem=recv, device_id=dev, device_id_type=MESH
        )

    def zq_view(e, p):
        return qg.at[0, e, p * HALF:(p + 1) * HALF]

    def zk_view(e, p):
        spot = Z_ORDER.index(e)
        rows = slice(0, KEYS) if p == 0 else slice(KEYS, KVR)
        return kv.at[2 + spot // 4, spot % 4, rows]

    def z_copy(kind, d, step, p):
        view, send, recv = ((zq_view, zq_send, zq_recv), (zk_view, zk_send, zk_recv))[kind]
        src = (-step if d == 0 else step) % NZ
        dst = (-step - 1 if d == 0 else step + 1) % NZ
        return remote(view(src, p), view(dst, p), send.at[d, step, p], recv.at[d, step, p], z_dev[d])

    def z_begin(kind, first):
        for d in (0, 1):
            z_copy(kind, d, 0, d if first else 1 - d).start()

    def z_pass(kind, step, first):
        for d in (0, 1):
            p = d if first else 1 - d
            z_copy(kind, d, step, p).wait_recv()
            if step < 2 or (step == 2 and first):
                z_copy(kind, d, step + 1, p).start()

    def xy_copies(view, cut, quarter, end, send, recv):
        table = {
            "own_up": (0, 1, 0, end, x_dev[0]),
            "own_down": (0, 2, 0, end, x_dev[1]),
            "own_y": (0, 3, 0, end, y_dev),
            "fwd_up": (1, 4, 0, cut, x_dev[0]),
            "fwd_down": (2, 4, cut, end, x_dev[1]),
            "y_up": (3, 5, 0, cut, x_dev[0]),
            "y_down": (3, 6, 0, cut, x_dev[1]),
            "yf_up": (5, 7, 0, quarter, x_dev[0]),
            "yf_down": (6, 7, quarter, cut, x_dev[1]),
            "y_1": (1, 5, cut, end, y_dev),
            "y_2": (2, 6, cut, end, y_dev),
            "y_3": (4, 7, cut, end, y_dev),
        }
        return {
            n: remote(view(s, a, b), view(t, a, b), send.at[i], recv.at[i], dev)
            for i, (n, (s, t, a, b, dev)) in enumerate(table.items())
        }

    xk = xy_copies(lambda s, a, b: kv.at[s // 4, s % 4, a:b], KEYS, KEYS // 2, KVR, xk_send, xk_recv)
    xq = xy_copies(lambda s, a, b: qg.at[1, s, a:b], HALF, HALF // 2, TOK, xq_send, xq_recv)

    def xy_begin(c):
        for n in ("own_up", "own_down", "own_y"):
            c[n].start()

    def xy_pass1(c):
        for n in ("own_up", "own_down"):
            c[n].wait_recv()
        c["fwd_up"].start()
        c["fwd_down"].start()
        c["y_1"].start()
        c["y_2"].start()
        c["own_y"].wait_recv()
        c["y_up"].start()
        c["y_down"].start()

    def xy_pass2(c):
        for n in ("fwd_up", "fwd_down"):
            c[n].wait_recv()
        c["y_3"].start()
        for n in ("y_up", "y_down"):
            c[n].wait_recv()
        c["yf_up"].start()
        c["yf_down"].start()

    def xy_pass3(c):
        for n in ("y_1", "y_2", "y_3", "yf_up", "yf_down"):
            c[n].wait_recv()

    rt_copy = remote(rt_s, rt_y, r_send.at[0], r_recv.at[0], y_dev)
    rz_copy = remote(rz_s, rz_r, r_send.at[1], r_recv.at[1], far_dev)

    def far_retire():
        group = y * 2 + 1 - zhi
        rz_s[0:16] = tokens(k_ref, group)
        rz_s[16:32] = tokens(v_ref, group)
        rt_copy.wait_recv()
        rz_s[32:64] = rt_y[32:64]
        rz_copy.start()

    lane = lax.broadcasted_iota(jnp.int32, (1, SPAN), 1)

    def make_bias(ph):
        for sel in (0, 1):
            if ph < 2:
                mine = section_ref[y * 2 + sel]
            else:
                mine = section_ref[(y + sel) % 2 * 2 + zhi]
            total = jnp.zeros((1, SPAN), F32)
            for s in range(4):
                if ph < 2:
                    block = ph * 4 + s
                    key_group = (y if block in (0, 1, 2, 4) else 1 - y) * 2 + zhi
                else:
                    key_group = y * 2 + (z + Z_ORDER[(ph - 2) * 4 + s]) % NZ // 4
                seen = section_ref[key_group] <= mine
                tok = jnp.where(seen, 0.0, NEG).astype(F32)
                live = kv[ph, s, 2 * KEYS:KVR, :].astype(F32)[0:1, 0:1]
                row = lane - s * KEYS
                dead = jnp.where((row - TOK).astype(F32) >= live, NEG, 0.0)
                here = (row >= 0) & (row < KEYS)
                total = jnp.where(here, jnp.where(row < TOK, tok, dead), total)
            bias[ph, sel] = total

    def pick(j, table):
        if isinstance(j, int):
            return table[j]
        return jnp.where(j == 0, table[0], jnp.where(j == 1, table[1], jnp.where(j == 2, table[2], table[3])))

    def unit(u):
        ph, j = u // 4, u % 4
        g = ph // 2
        if isinstance(u, int):
            where = lambda c, a, b: a if c else b
        else:
            where = jnp.where
        far = where(ph == 0, j + 1, 4 - j)
        c1 = where(g == 0, far, pick(j, G1_FIRST))
        c2 = where(g == 0, where(far == 4, 0, NZ - far), pick(j, G1_SECOND))
        sel = lambda c: where(g == 0, (z + c) % NZ // 4, where((c == 3) | (c > 4), 1, 0))
        return ph, g, c1, c2, sel(c1), sel(c2)

    scores, tops, alphas = (s0, s1), (mx0, mx1), (al0, al1)
    ones = jnp.ones((TILE, HEAD), BF16)

    def key_tile(ph, t, base):
        parts, a = [], t * TILE
        while a < (t + 1) * TILE:
            s = a // KEYS
            b = min((t + 1) * TILE, (s + 1) * KEYS)
            parts.append(kv[ph, s, base + a - s * KEYS:base + b - s * KEYS])
            a = b
        return jnp.concatenate(parts, 0) if len(parts) > 1 else parts[0]

    def stacked(ref, g, c1, c2):
        return jnp.concatenate([ref[g, c, :, h * HEAD:(h + 1) * HEAD] for c in (c1, c2) for h in range(SHARE)], 0)

    def unstack(ref, g, c1, c2, value):
        for i, c in enumerate((c1, c2)):
            for h in range(SHARE):
                r = (i * SHARE + h) * TOK
                ref[g, c, :, h * HEAD:(h + 1) * HEAD] = value[r:r + TOK]

    def score_tile(ctx, buf, t, top):
        (ph, g, c1, c2, b1, b2), q = ctx
        s = lax.dot_general(q, key_tile(ph, t, 0), (((1,), (1,)), ((), ())), preferred_element_type=F32)
        cols = slice(t * TILE, (t + 1) * TILE)
        s = jnp.concatenate(
            [s[:PAIR // 2] + bias[ph, b1, :, cols], s[PAIR // 2:] + bias[ph, b2, :, cols]], 0
        )
        scores[buf][:, cols] = s
        t2 = jnp.maximum(s[:, :HEAD], s[:, HEAD:])
        return t2 if top is None else jnp.maximum(top, t2)

    def score_begin(u):
        info = unit(u)
        return info, stacked(qg, info[1], info[2], info[3])

    def score_end(ctx, buf, top):
        _, g, c1, c2, _, _ = ctx[0]
        old = stacked(m_st, g, c1, c2)
        new = jnp.maximum(old, jnp.broadcast_to(jnp.max(top, axis=1, keepdims=True), (PAIR, HEAD)))
        tops[buf][...] = new
        alphas[buf][...] = jnp.exp2((old - new) * C)
        unstack(m_st, g, c1, c2, new)

    def step(u, buf, ahead):
        ph, g, c1, c2, _, _ = unit(u)
        if ahead:
            ctx = score_begin(u + 1)
        top = None
        new_top = tops[buf][...]
        total = None
        for t in range(SPAN // TILE):
            if ahead:
                top = score_tile(ctx, 1 - buf, t, top)
            s = scores[buf][:, t * TILE:(t + 1) * TILE]
            weight = jnp.concatenate(
                [jnp.exp2((s[:, :HEAD] - new_top) * C), jnp.exp2((s[:, HEAD:] - new_top) * C)], 1
            ).astype(BF16)
            v = jnp.concatenate([key_tile(ph, t, KEYS), ones], 1)
            mixed = jnp.dot(weight, v, preferred_element_type=F32)
            total = mixed if total is None else total + mixed
        alpha = alphas[buf][...]
        unstack(acc, g, c1, c2, stacked(acc, g, c1, c2) * alpha + total[:, :HEAD])
        unstack(l_st, g, c1, c2, stacked(l_st, g, c1, c2) * alpha + total[:, HEAD:])
        if ahead:
            score_end(ctx, 1 - buf, top)

    def gather_piece(g, c, r0, n, messages):
        rows = slice(r0, r0 + n)
        lanes = lax.broadcasted_iota(jnp.int32, (n, HEAD), 1)
        sums = jnp.ones((n, HEAD), F32)
        peak = jnp.zeros((n, HEAD), F32)
        for h in range(SHARE):
            cols = slice(h * HEAD, (h + 1) * HEAD)
            sums = jnp.where(lanes % 16 == h, l_st[g, c, rows, cols], sums)
            peak = jnp.where(lanes % 16 == h, m_st[g, c, rows, cols], peak)
        logs = [peak * C + jnp.log2(sums)]
        for ref, a in messages:
            p = ref[a:a + n, GW:MW].astype(F32)
            logs.append(p + pltpu.roll(p, 16, 1) + pltpu.roll(p, 32, 1) + pltpu.roll(p, 48, 1))
        top = functools.reduce(jnp.maximum, logs)
        weights = [jnp.exp2(item - top) for item in logs]
        total = functools.reduce(jnp.add, weights)
        share = 1.0 / total
        factors = [w * share for w in weights]
        factors[0] = factors[0] / sums
        out = []
        for h in range(SHARE):
            cols = slice(h * HEAD, (h + 1) * HEAD)
            spread = [jnp.broadcast_to(f[:, h:h + 1], (n, HEAD)) for f in factors]
            o = acc[g, c, rows, cols] * spread[0]
            for (ref, a), f in zip(messages, spread[1:]):
                o = o + ref[a:a + n, cols].astype(F32) * f
            out.append(o)
        return out, top + jnp.log2(total)

    def write_piece(dst, a, n, out, logs):
        for h in range(SHARE):
            dst[a:a + n, h * HEAD:(h + 1) * HEAD] = out[h].astype(BF16)
        lanes = lax.broadcasted_iota(jnp.int32, (n, HEAD), 1) // 16 % 4
        first = logs.astype(BF16).astype(F32)
        rest = logs - first
        second = rest.astype(BF16).astype(F32)
        third = rest - second
        parts = jnp.where(lanes == 0, first, jnp.where(lanes == 1, second, jnp.where(lanes == 2, third, 0.0)))
        dst[a:a + n, GW:MW] = parts.astype(BF16)

    def o_copy(d, hop, p):
        rows = slice(p * HALF, (p + 1) * HALF)
        return remote(
            sb0.at[d, hop, rows], mb0.at[d, hop, rows], o_send.at[d, hop, p], o_recv.at[d, hop, p], z_dev[d]
        )

    def ring(hop, first):
        for d in (0, 1):
            p = d if first else 1 - d
            messages = []
            if hop > 1 or (hop == 1 and first):
                o_copy(d, hop - 1, p).wait_recv()
                messages = [(mb0.at[d, hop - 1], p * HALF)]
            c = (4 - hop) if d == 0 else (4 + hop)
            write_piece(sb0.at[d, hop], p * HALF, HALF, *gather_piece(0, c, p * HALF, HALF, messages))
            o_copy(d, hop, p).start()

    def p_copy(name):
        i, a, n = MSG[name]
        dev = y_dev if name[0] == "y" else x_dev[0 if "u" in name else 1]
        return remote(sb1.at[a:a + n], mb1.at[a:a + n], p_send.at[i], p_recv.at[i], dev)

    def arrived(name, skip=0):
        return (mb1, MSG[name][1] + skip)

    def tree(name, c, r0, n, *needs):
        _, a, _ = MSG[name]
        write_piece(sb1, a, n, *gather_piece(1, c, r0, n, [arrived(*need) for need in needs]))
        p_copy(name).start()

    def wait_for(*names):
        for name in names:
            p_copy(name).wait_recv()

    def tree_12():
        tree("y7", 7, 32, 32)
        tree("xx1u", 7, 0, 16)
        tree("xx1d", 7, 16, 16)
        tree("x1u", 4, 0, 32)

    def split(name, c, parts):
        _, a, _ = MSG[name]
        for r0, needs in parts:
            write_piece(sb1, a + r0, 16, *gather_piece(1, c, r0, 16, needs))
        p_copy(name).start()

    def tree_13():
        tree("y5", 5, 32, 32)
        tree("y6", 6, 32, 32)
        wait_for("xx1u", "xx1d")
        split("xx2u", 6, ((0, [arrived("xx1u")]), (16, [])))
        split("xx2d", 5, ((0, []), (16, [arrived("xx1d")])))
        wait_for("y7")
        tree("x1d", 4, 32, 32, ("y7",))

    def tree_14():
        tree("x2d0", 1, 0, 32)
        wait_for("x1u")
        tree("x2u0", 2, 0, 32, ("x1u",))
        wait_for("y6")
        tree("x2u1", 2, 32, 32, ("y6",))
        wait_for("y5", "x1d")
        tree("x2d1", 1, 32, 32, ("y5",), ("x1d",))

    def tree_15():
        wait_for("xx2u", "xx2d")
        tree("yf", 3, 0, 32, ("xx2u",), ("xx2d",))
        tree("y3", 3, 32, 32)

    def finish(g, p, messages):
        out, _ = gather_piece(g, 0, p * HALF, HALF, messages)
        squares = jnp.zeros((HALF, HEAD), F32)
        for h in range(SHARE):
            acc[g, 0, p * HALF:(p + 1) * HALF, h * HEAD:(h + 1) * HEAD] = out[h]
            squares = squares + out[h] * out[h]
        rows = slice(p * HALF, (p + 1) * HALF)
        if g == 0:
            sq_s[rows, :] = squares
        else:
            total = jnp.sum(squares + sq_s[rows, :], axis=1, keepdims=True)
            sq_s[rows, :] = jnp.broadcast_to(total, (HALF, HEAD))

    def finish0():
        for p in (0, 1):
            for d in (0, 1):
                o_copy(d, 3, p).wait_recv()
            finish(0, p, [(mb0.at[d, 3], p * HALF) for d in (0, 1)])

    def retire():
        rz_copy.wait_recv()
        group = y * 2 + zhi
        spot = lax.broadcasted_iota(jnp.int32, (CACHE, 16), 0) - lax.broadcasted_iota(jnp.int32, (CACHE, 16), 1)
        chosen = jnp.where(spot == count_ref[0], 1.0, 0.0).astype(BF16)
        row = lax.broadcasted_iota(jnp.int32, (CACHE, 256), 0) - count_ref[0]
        fresh = (row >= 0) & (row < 16)
        for i, (own, old, new) in enumerate(((k_ref, ck_ref, nck_ref), (v_ref, cv_ref, ncv_ref))):
            got = jnp.where(section_ref[group] == 0, tokens(own, group).astype(F32), 0.0)
            for source, ref, a in (
                ((1 - y) * 2 + zhi, rt_y, 0),
                (y * 2 + 1 - zhi, rz_r, 0),
                ((1 - y) * 2 + 1 - zhi, rz_r, 32),
            ):
                got = jnp.where(section_ref[source] == 0, ref[a + 16 * i:a + 16 * i + 16].astype(F32), got)
            moved = jnp.dot(chosen, got.astype(BF16), preferred_element_type=F32)
            new[...] = jnp.where(fresh, moved, old[...].astype(F32)).astype(BF16)

    def z0(*passes):
        def run():
            for args in passes:
                z_pass(*args)
        return run

    before = {
        1: [z0((0, 2, True), (0, 2, False)), lambda: z_begin(1, False), lambda: xy_begin(xq)],
        2: [z0((0, 3, True)), lambda: xy_pass2(xk)],
        3: [lambda: xy_pass3(xk), lambda: make_bias(1), z0((1, 0, True))],
        4: [z0((1, 0, False)), lambda: xy_pass1(xq)],
        5: [z0((1, 1, True)), far_retire],
        6: [z0((1, 1, False)), lambda: xy_pass2(xq)],
        7: [lambda: xy_pass3(xq), lambda: make_bias(2)],
        8: [z0((1, 2, True))],
        9: [z0((1, 2, False))],
        11: [z0((1, 3, True)), lambda: make_bias(3)],
    }
    after = {
        4: [lambda: ring(0, True)],
        5: [lambda: ring(1, False)],
        6: [lambda: ring(1, True)],
        8: [lambda: ring(2, True), lambda: ring(2, False)],
        10: [lambda: ring(3, True), lambda: ring(3, False), retire],
        12: [tree_12],
        13: [tree_13, finish0],
        14: [tree_14],
        15: [tree_15],
    }

    def events(table, u, parity):
        if isinstance(u, int):
            for event in table.get(u, ()):
                event()
            return
        for at_unit, items in table.items():
            if at_unit % 2 == parity and at_unit < 14:
                @pl.when(u == at_unit)
                def _(items=items):
                    for event in items:
                        event()

    z_begin(0, True)
    xy_begin(xk)
    z_begin(0, False)
    rt_copy.start()
    z_pass(0, 0, True)
    z_pass(0, 0, False)
    z_pass(0, 1, True)
    z_begin(1, True)
    xy_pass1(xk)
    make_bias(0)
    ctx = score_begin(0)
    top = None
    for t in range(SPAN // TILE):
        top = score_tile(ctx, 0, t, top)
    score_end(ctx, 0, top)
    z_pass(0, 1, False)

    def two(i, carry):
        for parity in (0, 1):
            u = 2 * i + parity
            events(before, u, parity)
            step(u, parity, True)
            events(after, u, parity)
        return carry

    lax.fori_loop(0, 7, two, 0)
    events(before, 14, 0)
    step(14, 0, True)
    events(after, 14, 0)
    step(15, 1, False)
    events(after, 15, 1)

    wait_for("x2u0", "x2u1", "x2d0", "x2d1", "y3", "yf")
    for p in (0, 1):
        finish(1, p, [arrived(f"x2u{p}"), arrived(f"x2d{p}"), arrived("yf" if p == 0 else "y3")])
    sc = [remote(sq_s, sq_r.at[i], h_send.at[i], h_recv.at[i], head_dev[i]) for i in range(3)]
    for copy in sc:
        copy.start()
    total = sq_s[...]
    for i, copy in enumerate(sc):
        copy.wait_recv()
        total = total + sq_r[i]
    scale = lax.rsqrt(total / (HEADS * HEAD) + 1e-06)
    for g in (0, 1):
        for h in range(SHARE):
            cols = slice(h * HEAD, (h + 1) * HEAD)
            here = slice(g * GW + h * HEAD, g * GW + (h + 1) * HEAD)
            out_ref[:, here] = acc[g, 0, :, cols] * scale * gain_ref[here].reshape(1, HEAD)

    for d in (0, 1):
        for hop in range(4):
            for p in (0, 1):
                if hop < 3 or p == d:
                    z_copy(0, d, hop, p).wait_send()
                    z_copy(1, d, hop, p).wait_send()
                if hop > 0 or p == d:
                    o_copy(d, hop, p).wait_send()
    for copy in list(xk.values()) + list(xq.values()) + [rt_copy, rz_copy] + sc + [p_copy(n) for n in MSG]:
        copy.wait_send()


def on_device(queries, keys, values, cache_keys, cache_values, cache_count, span_section, norm_gain):
    vmem = pl.BlockSpec(memory_space=pltpu.VMEM)
    smem = pl.BlockSpec(memory_space=pltpu.SMEM)
    dma = pltpu.SemaphoreType.DMA
    state = pltpu.VMEM((2, NZ, TOK, GW), F32)
    return pl.pallas_call(
        kernel,
        out_shape=[
            jax.ShapeDtypeStruct((TOK, 2 * GW), F32),
            jax.ShapeDtypeStruct((CACHE, 256), BF16),
            jax.ShapeDtypeStruct((CACHE, 256), BF16),
        ],
        in_specs=[vmem] * 6 + [smem] * 2,
        out_specs=[vmem] * 3,
        scratch_shapes=[
            pltpu.VMEM((2, NZ, TOK, GW), BF16),
            pltpu.VMEM((4, 4, KVR, HEAD), BF16),
            pltpu.VMEM((4, 2, 1, SPAN), F32),
            state, state, state,
            pltpu.VMEM((PAIR, SPAN), F32), pltpu.VMEM((PAIR, SPAN), F32),
            pltpu.VMEM((PAIR, HEAD), F32), pltpu.VMEM((PAIR, HEAD), F32),
            pltpu.VMEM((PAIR, HEAD), F32), pltpu.VMEM((PAIR, HEAD), F32),
            pltpu.VMEM((2, 4, TOK, MW), BF16), pltpu.VMEM((2, 4, TOK, MW), BF16),
            pltpu.VMEM((MSG_ROWS, MW), BF16), pltpu.VMEM((MSG_ROWS, MW), BF16),
            pltpu.VMEM((64, 256), BF16), pltpu.VMEM((64, 256), BF16),
            pltpu.VMEM((64, 256), BF16), pltpu.VMEM((64, 256), BF16),
            pltpu.VMEM((TOK, HEAD), F32),
            pltpu.VMEM((3, TOK, HEAD), F32),
            dma((2, 4, 2)), dma((2, 4, 2)), dma((2, 4, 2)), dma((2, 4, 2)),
            dma((12,)), dma((12,)), dma((12,)), dma((12,)),
            dma((2,)), dma((2,)),
            dma((2, 4, 2)), dma((2, 4, 2)),
            dma((len(MSG),)), dma((len(MSG),)),
            dma((3,)), dma((3,)),
        ],
        compiler_params=pltpu.CompilerParams(
            collective_id=0, has_side_effects=True, vmem_limit_bytes=56 * 2**20
        ),
    )(queries, keys, values, cache_keys, cache_values, norm_gain, cache_count, span_section)


def solution(mesh):
    placed = (
        P("slot", "head"),
        P("slot", "head"),
        P("slot", "head"),
        P("slot", "head"),
        P("slot", "head"),
        P("slot"),
        P(),
        P("head"),
    )
    return jax.shard_map(
        on_device,
        mesh=mesh,
        in_specs=placed,
        out_specs=(P("slot", "head"), P("slot", "head"), P("slot", "head")),
        check_vma=False,
    )
```

```python
import functools

import jax
import jax.numpy as jnp
from jax import lax
from jax.experimental import pallas as pl
from jax.experimental.pallas import tpu as pltpu
from jax.sharding import PartitionSpec as P

MESH = pl.DeviceIdType.MESH
F32 = jnp.float32
BF16 = jnp.bfloat16

HEADS = 48
HEAD = 128
TOK = 64
CACHE = 256
KEYS = TOK + CACHE
KVR = 2 * KEYS + 16
SHARE = 6
GW = SHARE * HEAD
MW = GW + HEAD
HALF = TOK // 2
PAIR = 2 * SHARE * TOK
SPAN = 4 * KEYS
TILE = 256
C = HEAD ** -0.5 * 1.4426950408889634
NEG = -1e30
NZ, NX = 8, 4
Z_ORDER = (0, 1, 7, 2, 6, 3, 5, 4)
G1_FIRST = (7, 5, 1, 3)
G1_SECOND = (4, 6, 2, 0)
MSG = {}
for _name, _rows in (
    ("y7", 32), ("y5", 32), ("y6", 32), ("y3", 32), ("x1u", 32), ("x1d", 32), ("xx1u", 16), ("xx1d", 16),
    ("x2u0", 32), ("x2u1", 32), ("x2d0", 32), ("x2d1", 32), ("xx2u", 32), ("xx2d", 32), ("yf", 32),
):
    MSG[_name] = (len(MSG), sum(r for _, _, r in MSG.values()), _rows)
MSG_ROWS = sum(r for _, _, r in MSG.values())


def kernel(
    q_hbm, k_hbm, v_hbm, ck_hbm, cv_hbm, gain_hbm, count_ref, section_ref,
    out_ref, nck_hbm, ncv_hbm,
    qg, kv, bias, acc, l_st, m_st, s0, s1, mx0, mx1, al0, al1,
    sb0, mb0, sb1, mb1, rt_s, rt_y, rz_s, rz_r, sq_s, sq_r, gain_ref, cache_s, in_sem, out_sem,
    zq_send, zq_recv, zk_send, zk_recv, xk_send, xk_recv, xq_send, xq_recv,
    r_send, r_recv, o_send, o_recv, p_send, p_recv, h_send, h_recv,
):
    slot = lax.axis_index("slot")
    head = lax.axis_index("head")
    y = slot // 32
    z = slot // 4 % 8
    x = slot % 4
    zhi = z // 4

    def at(y_, z_, x_):
        return (y_ * 32 + z_ * 4 + x_, head)

    z_dev = (at(y, (z + 1) % NZ, x), at(y, (z + 7) % NZ, x))
    x_dev = (at(y, z, (x + 1) % NX), at(y, z, (x + 3) % NX))
    y_dev = at(1 - y, z, x)
    far_dev = at(y, (z + 4) % NZ, x)
    pair_core = 1 - head % 2
    head_dev = ((slot, head // 2 * 2 + pair_core), (slot, (head + 2) % 4), (slot, (head + 2) % 4 // 2 * 2 + pair_core))

    barrier = pltpu.get_barrier_semaphore()
    peers = z_dev + x_dev + (y_dev,) + head_dev
    for peer in peers:
        pl.semaphore_signal(barrier, inc=1, device_id=peer, device_id_type=MESH)

    loads = []
    for g in (0, 1):
        cols = slice(g * HEAD, (g + 1) * HEAD)
        loads += [
            (q_hbm.at[:, g * GW:(g + 1) * GW], qg.at[g, 0]),
            (k_hbm.at[:, cols], kv.at[2 * g, 0, 0:TOK]),
            (ck_hbm.at[:, cols], kv.at[2 * g, 0, TOK:KEYS]),
            (v_hbm.at[:, cols], kv.at[2 * g, 0, KEYS:KEYS + TOK]),
            (cv_hbm.at[:, cols], kv.at[2 * g, 0, KEYS + TOK:2 * KEYS]),
        ]
    loads.append((gain_hbm, gain_ref))
    loads = [pltpu.make_async_copy(a, b, in_sem.at[i]) for i, (a, b) in enumerate(loads)]
    for copy in loads:
        copy.start()
    for g in (0, 1):
        kv[2 * g, 0, 2 * KEYS:KVR] = jnp.full((16, HEAD), count_ref[0].astype(F32), F32).astype(BF16)
    m_st[...] = jnp.full(m_st.shape, NEG, F32)
    for copy in loads:
        copy.wait()

    def tokens(kind, group):
        rows = pl.ds(pl.multiple_of(kind * KEYS + group * 16, 16), 16)
        return jnp.concatenate([kv[0, 0, rows], kv[2, 0, rows]], 1)

    for i, group in enumerate(((1 - y) * 2 + zhi, (1 - y) * 2 + 1 - zhi)):
        rt_s[32 * i:32 * i + 16] = tokens(0, group)
        rt_s[32 * i + 16:32 * i + 32] = tokens(1, group)
    pl.semaphore_wait(barrier, len(peers))

    def remote(src, dst, send, recv, dev):
        return pltpu.make_async_remote_copy(
            src_ref=src, dst_ref=dst, send_sem=send, recv_sem=recv, device_id=dev, device_id_type=MESH
        )

    def zq_view(e, p):
        return qg.at[0, e, p * HALF:(p + 1) * HALF]

    def zk_view(e, p):
        spot = Z_ORDER.index(e)
        rows = slice(0, KEYS) if p == 0 else slice(KEYS, KVR)
        return kv.at[2 + spot // 4, spot % 4, rows]

    def z_copy(kind, d, step, p):
        view, send, recv = ((zq_view, zq_send, zq_recv), (zk_view, zk_send, zk_recv))[kind]
        src = (-step if d == 0 else step) % NZ
        dst = (-step - 1 if d == 0 else step + 1) % NZ
        return remote(view(src, p), view(dst, p), send.at[d, step, p], recv.at[d, step, p], z_dev[d])

    def z_begin(kind, first):
        for d in (0, 1):
            z_copy(kind, d, 0, d if first else 1 - d).start()

    def z_pass(kind, step, first):
        for d in (0, 1):
            p = d if first else 1 - d
            z_copy(kind, d, step, p).wait_recv()
            if step < 2 or (step == 2 and first):
                z_copy(kind, d, step + 1, p).start()

    def xy_copies(view, cut, quarter, end, send, recv):
        table = {
            "own_up": (0, 1, 0, end, x_dev[0]),
            "own_down": (0, 2, 0, end, x_dev[1]),
            "own_y": (0, 3, 0, end, y_dev),
            "fwd_up": (1, 4, 0, cut, x_dev[0]),
            "fwd_down": (2, 4, cut, end, x_dev[1]),
            "y_up": (3, 5, 0, cut, x_dev[0]),
            "y_down": (3, 6, 0, cut, x_dev[1]),
            "yf_up": (5, 7, 0, quarter, x_dev[0]),
            "yf_down": (6, 7, quarter, cut, x_dev[1]),
            "y_1": (1, 5, cut, end, y_dev),
            "y_2": (2, 6, cut, end, y_dev),
            "y_3": (4, 7, cut, end, y_dev),
        }
        return {
            n: remote(view(s, a, b), view(t, a, b), send.at[i], recv.at[i], dev)
            for i, (n, (s, t, a, b, dev)) in enumerate(table.items())
        }

    xk = xy_copies(lambda s, a, b: kv.at[s // 4, s % 4, a:b], KEYS, KEYS // 2, KVR, xk_send, xk_recv)
    xq = xy_copies(lambda s, a, b: qg.at[1, s, a:b], HALF, HALF // 2, TOK, xq_send, xq_recv)

    def xy_begin(c):
        for n in ("own_up", "own_down", "own_y"):
            c[n].start()

    def xy_pass(c, needs, then):
        for n in needs:
            c[n].wait_recv()
        for n in then:
            c[n].start()

    own_x = (("own_up", "own_down"), ("fwd_up", "fwd_down", "y_1", "y_2"))
    own_y = (("own_y",), ("y_up", "y_down"))
    two_x = (("fwd_up", "fwd_down"), ("y_3",))
    two_y = (("y_up", "y_down"), ("yf_up", "yf_down"))
    last = (("y_1", "y_2", "y_3", "yf_up", "yf_down"), ())

    rt_copy = remote(rt_s, rt_y, r_send.at[0], r_recv.at[0], y_dev)
    rz_copy = remote(rz_s, rz_r, r_send.at[1], r_recv.at[1], far_dev)

    cache_out = [pltpu.make_async_copy(cache_s.at[i], (nck_hbm, ncv_hbm)[i], out_sem.at[i]) for i in (0, 1)]

    def far_retire():
        group = y * 2 + 1 - zhi
        rz_s[0:16] = tokens(0, group)
        rz_s[16:32] = tokens(1, group)
        rt_copy.wait_recv()
        rz_s[32:64] = rt_y[32:64]
        rz_copy.start()

    lane = lax.broadcasted_iota(jnp.int32, (1, SPAN), 1)

    def make_bias(ph):
        for sel in (0, 1):
            if ph < 2:
                mine = section_ref[y * 2 + sel]
            else:
                mine = section_ref[(y + sel) % 2 * 2 + zhi]
            total = jnp.zeros((1, SPAN), F32)
            for s in range(4):
                if ph < 2:
                    block = ph * 4 + s
                    key_group = (y if block in (0, 1, 2, 4) else 1 - y) * 2 + zhi
                else:
                    key_group = y * 2 + (z + Z_ORDER[(ph - 2) * 4 + s]) % NZ // 4
                seen = section_ref[key_group] <= mine
                tok = jnp.where(seen, 0.0, NEG).astype(F32)
                live = kv[ph, s, 2 * KEYS:KVR, :].astype(F32)[0:1, 0:1]
                row = lane - s * KEYS
                dead = jnp.where((row - TOK).astype(F32) >= live, NEG, 0.0)
                here = (row >= 0) & (row < KEYS)
                total = jnp.where(here, jnp.where(row < TOK, tok, dead), total)
            bias[ph, sel] = total

    def pick(j, table):
        if isinstance(j, int):
            return table[j]
        return jnp.where(j == 0, table[0], jnp.where(j == 1, table[1], jnp.where(j == 2, table[2], table[3])))

    def unit(u):
        if isinstance(u, int):
            where = lambda c, a, b: a if c else b
        else:
            where = jnp.where
        g = u // 8
        ph = where(g == 0, u // 4, 2 + u % 2)
        j = where(g == 0, u % 4, u % 8 // 2)
        far = where(ph == 0, j + 1, 4 - j)
        c1 = where(g == 0, far, pick(j, G1_FIRST))
        c2 = where(g == 0, where(far == 4, 0, NZ - far), pick(j, G1_SECOND))
        sel = lambda c: where(g == 0, (z + c) % NZ // 4, where((c == 3) | (c > 4), 1, 0))
        return ph, g, c1, c2, sel(c1), sel(c2)

    scores, tops, alphas = (s0, s1), (mx0, mx1), (al0, al1)
    ones = jnp.ones((TILE, HEAD), BF16)

    def key_tile(ph, t, base):
        parts, a = [], t * TILE
        while a < (t + 1) * TILE:
            s = a // KEYS
            b = min((t + 1) * TILE, (s + 1) * KEYS)
            parts.append(kv[ph, s, base + a - s * KEYS:base + b - s * KEYS])
            a = b
        return jnp.concatenate(parts, 0) if len(parts) > 1 else parts[0]

    def stacked(ref, g, c1, c2):
        return jnp.concatenate([ref[g, c, :, h * HEAD:(h + 1) * HEAD] for c in (c1, c2) for h in range(SHARE)], 0)

    def unstack(ref, g, c1, c2, value):
        for i, c in enumerate((c1, c2)):
            for h in range(SHARE):
                r = (i * SHARE + h) * TOK
                ref[g, c, :, h * HEAD:(h + 1) * HEAD] = value[r:r + TOK]

    def score_tile(ctx, buf, t, top):
        (ph, g, c1, c2, b1, b2), q = ctx
        s = lax.dot_general(q, key_tile(ph, t, 0), (((1,), (1,)), ((), ())), preferred_element_type=F32)
        cols = slice(t * TILE, (t + 1) * TILE)
        s = jnp.concatenate(
            [s[:PAIR // 2] + bias[ph, b1, :, cols], s[PAIR // 2:] + bias[ph, b2, :, cols]], 0
        )
        scores[buf][:, cols] = s
        t2 = jnp.maximum(s[:, :HEAD], s[:, HEAD:])
        return t2 if top is None else jnp.maximum(top, t2)

    def score_begin(u):
        info = unit(u)
        return info, stacked(qg, info[1], info[2], info[3])

    def score_end(ctx, buf, top):
        _, g, c1, c2, _, _ = ctx[0]
        old = stacked(m_st, g, c1, c2)
        new = jnp.maximum(old, jnp.broadcast_to(jnp.max(top, axis=1, keepdims=True), (PAIR, HEAD)))
        tops[buf][...] = new
        alphas[buf][...] = jnp.exp2((old - new) * C)
        unstack(m_st, g, c1, c2, new)

    def step(u, buf, ahead):
        ph, g, c1, c2, _, _ = unit(u)
        if ahead:
            ctx = score_begin(u + 1)
        top = None
        new_top = tops[buf][...]
        total = None
        for t in range(SPAN // TILE):
            if ahead:
                top = score_tile(ctx, 1 - buf, t, top)
            s = scores[buf][:, t * TILE:(t + 1) * TILE]
            weight = jnp.concatenate(
                [jnp.exp2((s[:, :HEAD] - new_top) * C), jnp.exp2((s[:, HEAD:] - new_top) * C)], 1
            ).astype(BF16)
            v = jnp.concatenate([key_tile(ph, t, KEYS), ones], 1)
            mixed = jnp.dot(weight, v, preferred_element_type=F32)
            total = mixed if total is None else total + mixed
        alpha = alphas[buf][...]
        unstack(acc, g, c1, c2, stacked(acc, g, c1, c2) * alpha + total[:, :HEAD])
        unstack(l_st, g, c1, c2, stacked(l_st, g, c1, c2) * alpha + total[:, HEAD:])
        if ahead:
            score_end(ctx, 1 - buf, top)

    def gather_piece(g, c, r0, n, messages):
        rows = slice(r0, r0 + n)
        lanes = lax.broadcasted_iota(jnp.int32, (n, HEAD), 1)
        sums = jnp.ones((n, HEAD), F32)
        peak = jnp.zeros((n, HEAD), F32)
        for h in range(SHARE):
            cols = slice(h * HEAD, (h + 1) * HEAD)
            sums = jnp.where(lanes % 16 == h, l_st[g, c, rows, cols], sums)
            peak = jnp.where(lanes % 16 == h, m_st[g, c, rows, cols], peak)
        logs = [peak * C + jnp.log2(sums)]
        for ref, a in messages:
            p = ref[a:a + n, GW:MW].astype(F32)
            logs.append(p + pltpu.roll(p, 16, 1) + pltpu.roll(p, 32, 1) + pltpu.roll(p, 48, 1))
        top = functools.reduce(jnp.maximum, logs)
        weights = [jnp.exp2(item - top) for item in logs]
        total = functools.reduce(jnp.add, weights)
        share = 1.0 / total
        factors = [w * share for w in weights]
        factors[0] = factors[0] / sums
        out = []
        for h in range(SHARE):
            cols = slice(h * HEAD, (h + 1) * HEAD)
            spread = [jnp.broadcast_to(f[:, h:h + 1], (n, HEAD)) for f in factors]
            o = acc[g, c, rows, cols] * spread[0]
            for (ref, a), f in zip(messages, spread[1:]):
                o = o + ref[a:a + n, cols].astype(F32) * f
            out.append(o)
        return out, top + jnp.log2(total)

    def write_piece(dst, a, n, out, logs):
        for h in range(SHARE):
            dst[a:a + n, h * HEAD:(h + 1) * HEAD] = out[h].astype(BF16)
        lanes = lax.broadcasted_iota(jnp.int32, (n, HEAD), 1) // 16 % 4
        first = logs.astype(BF16).astype(F32)
        rest = logs - first
        second = rest.astype(BF16).astype(F32)
        third = rest - second
        parts = jnp.where(lanes == 0, first, jnp.where(lanes == 1, second, jnp.where(lanes == 2, third, 0.0)))
        dst[a:a + n, GW:MW] = parts.astype(BF16)

    def o_copy(d, hop, p):
        rows = slice(p * HALF, (p + 1) * HALF)
        return remote(
            sb0.at[d, hop, rows], mb0.at[d, hop, rows], o_send.at[d, hop, p], o_recv.at[d, hop, p], z_dev[d]
        )

    def ring(hop, first):
        for d in (0, 1):
            p = d if first else 1 - d
            messages = []
            if hop > 1 or (hop == 1 and first):
                o_copy(d, hop - 1, p).wait_recv()
                messages = [(mb0.at[d, hop - 1], p * HALF)]
            c = (4 - hop) if d == 0 else (4 + hop)
            write_piece(sb0.at[d, hop], p * HALF, HALF, *gather_piece(0, c, p * HALF, HALF, messages))
            o_copy(d, hop, p).start()

    def p_copy(name):
        i, a, n = MSG[name]
        dev = y_dev if name[0] == "y" else x_dev[0 if "u" in name else 1]
        return remote(sb1.at[a:a + n], mb1.at[a:a + n], p_send.at[i], p_recv.at[i], dev)

    def arrived(name, skip=0):
        return (mb1, MSG[name][1] + skip)

    def tree(name, c, r0, n, *needs):
        _, a, _ = MSG[name]
        write_piece(sb1, a, n, *gather_piece(1, c, r0, n, [arrived(*need) for need in needs]))
        p_copy(name).start()

    def wait_for(*names):
        for name in names:
            p_copy(name).wait_recv()

    def split(name, c, parts):
        _, a, _ = MSG[name]
        for r0, needs in parts:
            write_piece(sb1, a + r0, 16, *gather_piece(1, c, r0, 16, needs))
        p_copy(name).start()

    def tree_far():
        tree("y7", 7, 32, 32)
        tree("xx1u", 7, 0, 16)
        tree("xx1d", 7, 16, 16)
        tree("x1u", 4, 0, 32)

    def tree_y():
        tree("y5", 5, 32, 32)
        tree("y6", 6, 32, 32)

    def tree_x():
        wait_for("xx1u", "xx1d", "y7")
        tree("x1d", 4, 32, 32, ("y7",))
        split("xx2u", 6, ((0, [arrived("xx1u")]), (16, [])))
        split("xx2d", 5, ((0, []), (16, [arrived("xx1d")])))

    def tree_near():
        tree("x2d0", 1, 0, 32)
        wait_for("x1u")
        tree("x2u0", 2, 0, 32, ("x1u",))

    def tree_near2():
        wait_for("y6")
        tree("x2u1", 2, 32, 32, ("y6",))

    def tree_last():
        wait_for("xx2u", "xx2d")
        tree("yf", 3, 0, 32, ("xx2u",), ("xx2d",))
        tree("y3", 3, 32, 32)
        wait_for("y5", "x1d")
        tree("x2d1", 1, 32, 32, ("y5",), ("x1d",))

    def finish(g, p, messages):
        out, _ = gather_piece(g, 0, p * HALF, HALF, messages)
        squares = jnp.zeros((HALF, HEAD), F32)
        for h in range(SHARE):
            acc[g, 0, p * HALF:(p + 1) * HALF, h * HEAD:(h + 1) * HEAD] = out[h]
            squares = squares + out[h] * out[h]
        rows = slice(p * HALF, (p + 1) * HALF)
        if g == 0:
            sq_s[rows, :] = squares
        else:
            total = jnp.sum(squares + sq_s[rows, :], axis=1, keepdims=True)
            sq_s[rows, :] = jnp.broadcast_to(total, (HALF, HEAD))

    def finish0():
        for p in (0, 1):
            for d in (0, 1):
                o_copy(d, 3, p).wait_recv()
            finish(0, p, [(mb0.at[d, 3], p * HALF) for d in (0, 1)])

    def retire():
        rz_copy.wait_recv()
        group = y * 2 + zhi
        spot = lax.broadcasted_iota(jnp.int32, (CACHE, 16), 0) - lax.broadcasted_iota(jnp.int32, (CACHE, 16), 1)
        chosen = jnp.where(spot == count_ref[0], 1.0, 0.0).astype(BF16)
        row = lax.broadcasted_iota(jnp.int32, (CACHE, 256), 0) - count_ref[0]
        fresh = (row >= 0) & (row < 16)
        for i in (0, 1):
            got = jnp.where(section_ref[group] == 0, tokens(i, group).astype(F32), 0.0)
            for source, ref, a in (
                ((1 - y) * 2 + zhi, rt_y, 0),
                (y * 2 + 1 - zhi, rz_r, 0),
                ((1 - y) * 2 + 1 - zhi, rz_r, 32),
            ):
                got = jnp.where(section_ref[source] == 0, ref[a + 16 * i:a + 16 * i + 16].astype(F32), got)
            moved = jnp.dot(chosen, got.astype(BF16), preferred_element_type=F32)
            rows = slice(i * KEYS + TOK, (i + 1) * KEYS)
            old = jnp.concatenate([kv[0, 0, rows], kv[2, 0, rows]], 1)
            cache_s[i] = jnp.where(fresh, moved, old.astype(F32)).astype(BF16)
        for copy in cache_out:
            copy.start()

    def z0(*passes):
        def run():
            for args in passes:
                z_pass(*args)
        return run

    def xy(c, *passes):
        def run():
            for args in passes:
                xy_pass(c, *args)
        return run

    before = {
        1: [z0((1, 1, True), (0, 2, True)), xy(xk, two_x, two_y), xy(xq, two_x, two_y), z0((0, 2, False))],
        2: [z0((1, 1, False), (0, 3, True))],
        3: [z0((1, 2, True)), xy(xk, last), lambda: make_bias(1)],
        4: [far_retire],
        7: [z0((1, 2, False)), xy(xq, last), lambda: make_bias(2)],
        8: [z0((1, 3, True)), lambda: make_bias(3)],
    }
    after = {
        4: [lambda: ring(0, True)],
        5: [lambda: ring(1, False)],
        7: [lambda: ring(1, True)],
        8: [lambda: ring(2, False)],
        9: [tree_far],
        10: [lambda: ring(2, True)],
        11: [lambda: ring(3, False), tree_y],
        12: [tree_x],
        13: [lambda: ring(3, True), tree_near],
        14: [tree_near2],
        15: [tree_last, finish0, retire],
    }

    def events(table, u, parity):
        if isinstance(u, int):
            for event in table.get(u, ()):
                event()
            return
        for at_unit, items in table.items():
            if at_unit % 2 == parity and at_unit < 14:
                @pl.when(u == at_unit)
                def _(items=items):
                    for event in items:
                        event()

    z_begin(0, True)
    xy_begin(xk)
    rt_copy.start()
    l_st[...] = jnp.zeros(l_st.shape, F32)
    z_begin(0, False)
    acc[...] = jnp.zeros(acc.shape, F32)
    z_begin(1, True)
    z_pass(0, 0, True)
    xy_begin(xq)
    z_begin(1, False)
    z_pass(0, 0, False)
    xy_pass(xk, *own_x)
    xy_pass(xk, *own_y)
    z_pass(1, 0, True)
    make_bias(0)
    ctx = score_begin(0)
    top = None
    for t in range(SPAN // TILE):
        top = score_tile(ctx, 0, t, top)
    score_end(ctx, 0, top)
    xy_pass(xq, *own_x)
    xy_pass(xq, *own_y)
    z_pass(0, 1, True)
    z_pass(1, 0, False)
    z_pass(0, 1, False)

    def two(i, carry):
        for parity in (0, 1):
            u = 2 * i + parity
            events(before, u, parity)
            step(u, parity, True)
            events(after, u, parity)
        return carry

    lax.fori_loop(0, 7, two, 0)
    events(before, 14, 0)
    step(14, 0, True)
    events(after, 14, 0)
    step(15, 1, False)
    events(after, 15, 1)

    wait_for("x2u0", "x2u1", "x2d0", "x2d1", "y3", "yf")
    for p in (0, 1):
        finish(1, p, [arrived(f"x2u{p}"), arrived(f"x2d{p}"), arrived("yf" if p == 0 else "y3")])
    sc = [remote(sq_s, sq_r.at[i], h_send.at[i], h_recv.at[i], head_dev[i]) for i in range(3)]
    for copy in sc:
        copy.start()
    total = sq_s[...]
    for i, copy in enumerate(sc):
        copy.wait_recv()
        total = total + sq_r[i]
    scale = lax.rsqrt(total / (HEADS * HEAD) + 1e-06)
    for g in (0, 1):
        for h in range(SHARE):
            cols = slice(h * HEAD, (h + 1) * HEAD)
            here = slice(g * GW + h * HEAD, g * GW + (h + 1) * HEAD)
            out_ref[:, here] = acc[g, 0, :, cols] * scale * gain_ref[here].reshape(1, HEAD)

    for copy in cache_out:
        copy.wait()
    for d in (0, 1):
        for hop in range(4):
            for p in (0, 1):
                if hop < 3 or p == d:
                    z_copy(0, d, hop, p).wait_send()
                    z_copy(1, d, hop, p).wait_send()
                if hop > 0 or p == d:
                    o_copy(d, hop, p).wait_send()
    for copy in list(xk.values()) + list(xq.values()) + [rt_copy, rz_copy] + sc + [p_copy(n) for n in MSG]:
        copy.wait_send()


def on_device(queries, keys, values, cache_keys, cache_values, cache_count, span_section, norm_gain):
    vmem = pl.BlockSpec(memory_space=pltpu.VMEM)
    smem = pl.BlockSpec(memory_space=pltpu.SMEM)
    hbm = pl.BlockSpec(memory_space=pl.ANY)
    dma = pltpu.SemaphoreType.DMA
    state = pltpu.VMEM((2, NZ, TOK, GW), F32)
    return pl.pallas_call(
        kernel,
        out_shape=[
            jax.ShapeDtypeStruct((TOK, 2 * GW), F32),
            jax.ShapeDtypeStruct((CACHE, 256), BF16),
            jax.ShapeDtypeStruct((CACHE, 256), BF16),
        ],
        in_specs=[hbm] * 6 + [smem] * 2,
        out_specs=[vmem, hbm, hbm],
        scratch_shapes=[
            pltpu.VMEM((2, NZ, TOK, GW), BF16),
            pltpu.VMEM((4, 4, KVR, HEAD), BF16),
            pltpu.VMEM((4, 2, 1, SPAN), F32),
            state, state, state,
            pltpu.VMEM((PAIR, SPAN), F32), pltpu.VMEM((PAIR, SPAN), F32),
            pltpu.VMEM((PAIR, HEAD), F32), pltpu.VMEM((PAIR, HEAD), F32),
            pltpu.VMEM((PAIR, HEAD), F32), pltpu.VMEM((PAIR, HEAD), F32),
            pltpu.VMEM((2, 4, TOK, MW), BF16), pltpu.VMEM((2, 4, TOK, MW), BF16),
            pltpu.VMEM((MSG_ROWS, MW), BF16), pltpu.VMEM((MSG_ROWS, MW), BF16),
            pltpu.VMEM((64, 256), BF16), pltpu.VMEM((64, 256), BF16),
            pltpu.VMEM((64, 256), BF16), pltpu.VMEM((64, 256), BF16),
            pltpu.VMEM((TOK, HEAD), F32),
            pltpu.VMEM((3, TOK, HEAD), F32),
            pltpu.VMEM((2 * GW,), F32),
            pltpu.VMEM((2, CACHE, 256), BF16),
            dma((11,)), dma((2,)),
            dma((2, 4, 2)), dma((2, 4, 2)), dma((2, 4, 2)), dma((2, 4, 2)),
            dma((12,)), dma((12,)), dma((12,)), dma((12,)),
            dma((2,)), dma((2,)),
            dma((2, 4, 2)), dma((2, 4, 2)),
            dma((len(MSG),)), dma((len(MSG),)),
            dma((3,)), dma((3,)),
        ],
        compiler_params=pltpu.CompilerParams(
            collective_id=0, has_side_effects=True, vmem_limit_bytes=56 * 2**20
        ),
    )(queries, keys, values, cache_keys, cache_values, norm_gain, cache_count, span_section)


def solution(mesh):
    placed = (
        P("slot", "head"),
        P("slot", "head"),
        P("slot", "head"),
        P("slot", "head"),
        P("slot", "head"),
        P("slot"),
        P(),
        P("head"),
    )
    return jax.shard_map(
        on_device,
        mesh=mesh,
        in_specs=placed,
        out_specs=(P("slot", "head"), P("slot", "head"), P("slot", "head")),
        check_vma=False,
    )
```

```python
import functools

import jax
import jax.numpy as jnp
from jax import lax
from jax.experimental import pallas as pl
from jax.experimental.pallas import tpu as pltpu
from jax.sharding import PartitionSpec as P

MESH = pl.DeviceIdType.MESH
F32 = jnp.float32
BF16 = jnp.bfloat16

HEADS = 48
HEAD = 128
TOK = 64
CACHE = 256
KEYS = TOK + CACHE
KVR = 2 * KEYS + 16
SHARE = 6
GW = SHARE * HEAD
MW = GW + HEAD
HALF = TOK // 2
PAIR = 2 * SHARE * TOK
SPAN = 4 * KEYS
TILE = 256
C = HEAD ** -0.5 * 1.4426950408889634
NEG = -1e30
NZ, NX = 8, 4
Z_ORDER = (0, 1, 7, 2, 6, 3, 5, 4)
G1_FIRST = (7, 5, 1, 3)
G1_SECOND = (4, 6, 2, 0)
MSG = {}
for _name, _rows in (
    ("y7", 32), ("y5", 32), ("y6", 32), ("y3", 32), ("x1u", 32), ("x1d", 32), ("xx1u", 16), ("xx1d", 16),
    ("x2u0", 32), ("x2u1", 32), ("x2d0", 32), ("x2d1", 32), ("xx2u", 32), ("xx2d", 32), ("yf", 32),
):
    MSG[_name] = (len(MSG), sum(r for _, _, r in MSG.values()), _rows)
MSG_ROWS = sum(r for _, _, r in MSG.values())


def kernel(
    q_hbm, k_hbm, v_hbm, ck_hbm, cv_hbm, count_ref, section_ref,
    o_ref, total_ref, fresh_ref,
    qg, kv, bias, acc, l_st, m_st, s0, s1, mx0, mx1, al0, al1,
    sb0, mb0, sb1, mb1, rt_s, rt_y, rz_s, rz_r, sq_p, sq_s, sq_r, in_sem,
    sent, zq_recv, zk_recv, xk_recv, xq_recv, r_recv, o_recv, p_recv, h_recv,
):
    slot = lax.axis_index("slot")
    head = lax.axis_index("head")
    y = slot // 32
    z = slot // 4 % 8
    x = slot % 4
    zhi = z // 4

    def at(y_, z_, x_):
        return (y_ * 32 + z_ * 4 + x_, head)

    z_dev = (at(y, (z + 1) % NZ, x), at(y, (z + 7) % NZ, x))
    x_dev = (at(y, z, (x + 1) % NX), at(y, z, (x + 3) % NX))
    y_dev = at(1 - y, z, x)
    far_dev = at(y, (z + 4) % NZ, x)
    pair_core = 1 - head % 2
    head_dev = ((slot, head // 2 * 2 + pair_core), (slot, (head + 2) % 4), (slot, (head + 2) % 4 // 2 * 2 + pair_core))

    barrier = pltpu.get_barrier_semaphore()
    peers = z_dev + x_dev + (y_dev,) + head_dev
    for peer in peers:
        pl.semaphore_signal(barrier, inc=1, device_id=peer, device_id_type=MESH)

    loads = []
    for g in (0, 1):
        cols = slice(g * HEAD, (g + 1) * HEAD)
        loads += [
            (q_hbm.at[:, g * GW:(g + 1) * GW], qg.at[g, 0]),
            (k_hbm.at[:, cols], kv.at[2 * g, 0, 0:TOK]),
            (ck_hbm.at[:, cols], kv.at[2 * g, 0, TOK:KEYS]),
            (v_hbm.at[:, cols], kv.at[2 * g, 0, KEYS:KEYS + TOK]),
            (cv_hbm.at[:, cols], kv.at[2 * g, 0, KEYS + TOK:2 * KEYS]),
        ]
    loads = [pltpu.make_async_copy(a, b, in_sem.at[i]) for i, (a, b) in enumerate(loads)]
    for copy in loads:
        copy.start()
    for g in (0, 1):
        kv[2 * g, 0, 2 * KEYS:KVR] = jnp.full((16, HEAD), count_ref[0].astype(F32), F32).astype(BF16)
    m_st[...] = jnp.full(m_st.shape, NEG, F32)
    for copy in loads:
        copy.wait()

    def tokens(kind, group):
        rows = pl.ds(pl.multiple_of(kind * KEYS + group * 16, 16), 16)
        return jnp.concatenate([kv[0, 0, rows], kv[2, 0, rows]], 1)

    for i, group in enumerate(((1 - y) * 2 + zhi, (1 - y) * 2 + 1 - zhi)):
        rt_s[32 * i:32 * i + 16] = tokens(0, group)
        rt_s[32 * i + 16:32 * i + 32] = tokens(1, group)
    pl.semaphore_wait(barrier, len(peers))

    def remote(src, dst, send, recv, dev):
        return pltpu.make_async_remote_copy(
            src_ref=src, dst_ref=dst, send_sem=send, recv_sem=recv, device_id=dev, device_id_type=MESH
        )

    def zq_view(e, p):
        return qg.at[0, e, p * HALF:(p + 1) * HALF]

    def zk_view(e, p):
        spot = Z_ORDER.index(e)
        rows = slice(0, KEYS) if p == 0 else slice(KEYS, KVR)
        return kv.at[2 + spot // 4, spot % 4, rows]

    def z_copy(kind, d, step, p):
        view, send, recv = ((zq_view, sent.at[0], zq_recv), (zk_view, sent.at[1], zk_recv))[kind]
        src = (-step if d == 0 else step) % NZ
        dst = (-step - 1 if d == 0 else step + 1) % NZ
        return remote(view(src, p), view(dst, p), send, recv.at[d, step, p], z_dev[d])

    def z_begin(kind, first):
        for d in (0, 1):
            z_copy(kind, d, 0, d if first else 1 - d).start()

    def z_pass(kind, step, first):
        for d in (0, 1):
            p = d if first else 1 - d
            z_copy(kind, d, step, p).wait_recv()
            if step < 2 or (step == 2 and first):
                z_copy(kind, d, step + 1, p).start()

    def xy_copies(view, cut, quarter, end, send, recv):
        table = {
            "own_up": (0, 1, 0, end, x_dev[0]),
            "own_down": (0, 2, 0, end, x_dev[1]),
            "own_y": (0, 3, 0, end, y_dev),
            "fwd_up": (1, 4, 0, cut, x_dev[0]),
            "fwd_down": (2, 4, cut, end, x_dev[1]),
            "y_up": (3, 5, 0, cut, x_dev[0]),
            "y_down": (3, 6, 0, cut, x_dev[1]),
            "yf_up": (5, 7, 0, quarter, x_dev[0]),
            "yf_down": (6, 7, quarter, cut, x_dev[1]),
            "y_1": (1, 5, cut, end, y_dev),
            "y_2": (2, 6, cut, end, y_dev),
            "y_3": (4, 7, cut, end, y_dev),
        }
        return {
            n: remote(view(s, a, b), view(t, a, b), send, recv.at[i], dev)
            for i, (n, (s, t, a, b, dev)) in enumerate(table.items())
        }

    xk = xy_copies(lambda s, a, b: kv.at[s // 4, s % 4, a:b], KEYS, KEYS // 2, KVR, sent.at[2], xk_recv)
    xq = xy_copies(lambda s, a, b: qg.at[1, s, a:b], HALF, HALF // 2, TOK, sent.at[3], xq_recv)

    def xy_begin(c):
        for n in ("own_up", "own_down", "own_y"):
            c[n].start()

    def xy_pass(c, needs, then):
        for n in needs:
            c[n].wait_recv()
        for n in then:
            c[n].start()

    own_x = (("own_up", "own_down"), ("fwd_up", "fwd_down", "y_1", "y_2"))
    own_y = (("own_y",), ("y_up", "y_down"))
    two_x = (("fwd_up", "fwd_down"), ("y_3",))
    two_y = (("y_up", "y_down"), ("yf_up", "yf_down"))
    last = (("y_1", "y_2", "y_3", "yf_up", "yf_down"), ())

    rt_copy = remote(rt_s, rt_y, sent.at[4], r_recv.at[0], y_dev)
    rz_copy = remote(rz_s, rz_r, sent.at[5], r_recv.at[1], far_dev)

    def far_retire():
        group = y * 2 + 1 - zhi
        rz_s[0:16] = tokens(0, group)
        rz_s[16:32] = tokens(1, group)
        rt_copy.wait_recv()
        rz_s[32:64] = rt_y[32:64]
        rz_copy.start()

    lane = lax.broadcasted_iota(jnp.int32, (1, SPAN), 1)

    def make_bias(ph):
        for sel in (0, 1):
            if ph < 2:
                mine = section_ref[y * 2 + sel]
            else:
                mine = section_ref[(y + sel) % 2 * 2 + zhi]
            total = jnp.zeros((1, SPAN), F32)
            for s in range(4):
                if ph < 2:
                    block = ph * 4 + s
                    key_group = (y if block in (0, 1, 2, 4) else 1 - y) * 2 + zhi
                else:
                    key_group = y * 2 + (z + Z_ORDER[(ph - 2) * 4 + s]) % NZ // 4
                seen = section_ref[key_group] <= mine
                tok = jnp.where(seen, 0.0, NEG).astype(F32)
                live = kv[ph, s, 2 * KEYS:KVR, :].astype(F32)[0:1, 0:1]
                row = lane - s * KEYS
                dead = jnp.where((row - TOK).astype(F32) >= live, NEG, 0.0)
                here = (row >= 0) & (row < KEYS)
                total = jnp.where(here, jnp.where(row < TOK, tok, dead), total)
            bias[ph, sel] = total

    def pick(j, table):
        if isinstance(j, int):
            return table[j]
        return jnp.where(j == 0, table[0], jnp.where(j == 1, table[1], jnp.where(j == 2, table[2], table[3])))

    def unit(u):
        if isinstance(u, int):
            where = lambda c, a, b: a if c else b
        else:
            where = jnp.where
        g = u // 8
        ph = where(g == 0, u // 4, 2 + u % 2)
        j = where(g == 0, u % 4, u % 8 // 2)
        far = where(ph == 0, j + 1, 4 - j)
        c1 = where(g == 0, far, pick(j, G1_FIRST))
        c2 = where(g == 0, where(far == 4, 0, NZ - far), pick(j, G1_SECOND))
        sel = lambda c: where(g == 0, (z + c) % NZ // 4, where((c == 3) | (c > 4), 1, 0))
        return ph, g, c1, c2, sel(c1), sel(c2)

    scores, tops, alphas = (s0, s1), (mx0, mx1), (al0, al1)
    ones = jnp.ones((TILE, HEAD), BF16)

    def key_tile(ph, t, base):
        parts, a = [], t * TILE
        while a < (t + 1) * TILE:
            s = a // KEYS
            b = min((t + 1) * TILE, (s + 1) * KEYS)
            parts.append(kv[ph, s, base + a - s * KEYS:base + b - s * KEYS])
            a = b
        return jnp.concatenate(parts, 0) if len(parts) > 1 else parts[0]

    def stacked(ref, g, c1, c2):
        return jnp.concatenate([ref[g, c, :, h * HEAD:(h + 1) * HEAD] for c in (c1, c2) for h in range(SHARE)], 0)

    def unstack(ref, g, c1, c2, value):
        for i, c in enumerate((c1, c2)):
            for h in range(SHARE):
                r = (i * SHARE + h) * TOK
                ref[g, c, :, h * HEAD:(h + 1) * HEAD] = value[r:r + TOK]

    def score_tile(ctx, buf, t, top):
        (ph, g, c1, c2, b1, b2), q = ctx
        s = lax.dot_general(q, key_tile(ph, t, 0), (((1,), (1,)), ((), ())), preferred_element_type=F32)
        cols = slice(t * TILE, (t + 1) * TILE)
        s = jnp.concatenate(
            [s[:PAIR // 2] + bias[ph, b1, :, cols], s[PAIR // 2:] + bias[ph, b2, :, cols]], 0
        )
        scores[buf][:, cols] = s
        t2 = jnp.maximum(s[:, :HEAD], s[:, HEAD:])
        return t2 if top is None else jnp.maximum(top, t2)

    def score_begin(u):
        info = unit(u)
        return info, stacked(qg, info[1], info[2], info[3])

    def score_end(ctx, buf, top):
        _, g, c1, c2, _, _ = ctx[0]
        old = stacked(m_st, g, c1, c2)
        new = jnp.maximum(old, jnp.broadcast_to(jnp.max(top, axis=1, keepdims=True), (PAIR, HEAD)))
        tops[buf][...] = new
        alphas[buf][...] = jnp.exp2((old - new) * C)
        unstack(m_st, g, c1, c2, new)

    def step(u, buf, ahead):
        ph, g, c1, c2, _, _ = unit(u)
        if ahead:
            ctx = score_begin(u + 1)
        top = None
        new_top = tops[buf][...]
        total = None
        for t in range(SPAN // TILE):
            if ahead:
                top = score_tile(ctx, 1 - buf, t, top)
            s = scores[buf][:, t * TILE:(t + 1) * TILE]
            weight = jnp.concatenate(
                [jnp.exp2((s[:, :HEAD] - new_top) * C), jnp.exp2((s[:, HEAD:] - new_top) * C)], 1
            ).astype(BF16)
            v = jnp.concatenate([key_tile(ph, t, KEYS), ones], 1)
            mixed = jnp.dot(weight, v, preferred_element_type=F32)
            total = mixed if total is None else total + mixed
        alpha = alphas[buf][...]
        unstack(acc, g, c1, c2, stacked(acc, g, c1, c2) * alpha + total[:, :HEAD])
        unstack(l_st, g, c1, c2, stacked(l_st, g, c1, c2) * alpha + total[:, HEAD:])
        if ahead:
            score_end(ctx, 1 - buf, top)

    def gather_piece(g, c, r0, n, messages):
        rows = slice(r0, r0 + n)
        lanes = lax.broadcasted_iota(jnp.int32, (n, HEAD), 1)
        sums = jnp.ones((n, HEAD), F32)
        peak = jnp.zeros((n, HEAD), F32)
        for h in range(SHARE):
            cols = slice(h * HEAD, (h + 1) * HEAD)
            sums = jnp.where(lanes % 16 == h, l_st[g, c, rows, cols], sums)
            peak = jnp.where(lanes % 16 == h, m_st[g, c, rows, cols], peak)
        logs = [peak * C + jnp.log2(sums)]
        for ref, a in messages:
            p = ref[a:a + n, GW:MW].astype(F32)
            logs.append(p + pltpu.roll(p, 16, 1) + pltpu.roll(p, 32, 1) + pltpu.roll(p, 48, 1))
        top = functools.reduce(jnp.maximum, logs)
        weights = [jnp.exp2(item - top) for item in logs]
        total = functools.reduce(jnp.add, weights)
        share = 1.0 / total
        factors = [w * share for w in weights]
        factors[0] = factors[0] / sums
        out = []
        for h in range(SHARE):
            cols = slice(h * HEAD, (h + 1) * HEAD)
            spread = [jnp.broadcast_to(f[:, h:h + 1], (n, HEAD)) for f in factors]
            o = acc[g, c, rows, cols] * spread[0]
            for (ref, a), f in zip(messages, spread[1:]):
                o = o + ref[a:a + n, cols].astype(F32) * f
            out.append(o)
        return out, top + jnp.log2(total)

    def write_piece(dst, a, n, out, logs):
        for h in range(SHARE):
            dst[a:a + n, h * HEAD:(h + 1) * HEAD] = out[h].astype(BF16)
        lanes = lax.broadcasted_iota(jnp.int32, (n, HEAD), 1) // 16 % 4
        first = logs.astype(BF16).astype(F32)
        rest = logs - first
        second = rest.astype(BF16).astype(F32)
        third = rest - second
        parts = jnp.where(lanes == 0, first, jnp.where(lanes == 1, second, jnp.where(lanes == 2, third, 0.0)))
        dst[a:a + n, GW:MW] = parts.astype(BF16)

    def o_copy(d, hop, p):
        rows = slice(p * HALF, (p + 1) * HALF)
        return remote(
            sb0.at[d, hop, rows], mb0.at[d, hop, rows], sent.at[6], o_recv.at[d, hop, p], z_dev[d]
        )

    def ring(hop, first):
        todo = []
        for d in (0, 1):
            p = d if first else 1 - d
            messages = []
            if hop > 1 or (hop == 1 and first):
                o_copy(d, hop - 1, p).wait_recv()
                messages = [(mb0.at[d, hop - 1], p * HALF)]
            todo.append((d, p, (4 - hop) if d == 0 else (4 + hop), messages))
        pieces = [gather_piece(0, c, p * HALF, HALF, messages) for d, p, c, messages in todo]
        for (d, p, _, _), piece in zip(todo, pieces):
            write_piece(sb0.at[d, hop], p * HALF, HALF, *piece)
        for d, p, _, _ in todo:
            o_copy(d, hop, p).start()

    def p_copy(name):
        i, a, n = MSG[name]
        dev = y_dev if name[0] == "y" else x_dev[0 if "u" in name else 1]
        return remote(sb1.at[a:a + n], mb1.at[a:a + n], sent.at[7], p_recv.at[i], dev)

    def arrived(name, skip=0):
        return (mb1, MSG[name][1] + skip)

    def tree(name, c, r0, n, *needs):
        _, a, _ = MSG[name]
        write_piece(sb1, a, n, *gather_piece(1, c, r0, n, [arrived(*need) for need in needs]))
        p_copy(name).start()

    def wait_for(*names):
        for name in names:
            p_copy(name).wait_recv()

    def split(name, c, parts):
        _, a, _ = MSG[name]
        for r0, needs in parts:
            write_piece(sb1, a + r0, 16, *gather_piece(1, c, r0, 16, needs))
        p_copy(name).start()

    def tree_far():
        tree("y7", 7, 32, 32)
        tree("xx1u", 7, 0, 16)
        tree("xx1d", 7, 16, 16)
        tree("x1u", 4, 0, 32)

    def tree_y():
        tree("y5", 5, 32, 32)
        tree("y6", 6, 32, 32)

    def tree_x():
        wait_for("xx1u", "xx1d", "y7")
        tree("x1d", 4, 32, 32, ("y7",))
        split("xx2u", 6, ((0, [arrived("xx1u")]), (16, [])))
        split("xx2d", 5, ((0, []), (16, [arrived("xx1d")])))

    def tree_near():
        tree("x2d0", 1, 0, 32)
        wait_for("x1u")
        tree("x2u0", 2, 0, 32, ("x1u",))

    def tree_near2():
        wait_for("y6")
        tree("x2u1", 2, 32, 32, ("y6",))

    def tree_last():
        wait_for("xx2u", "xx2d")
        tree("yf", 3, 0, 32, ("xx2u",), ("xx2d",))
        tree("y3", 3, 32, 32)
        wait_for("y5", "x1d")
        tree("x2d1", 1, 32, 32, ("y5",), ("x1d",))

    def finish(g, p, messages):
        out, _ = gather_piece(g, 0, p * HALF, HALF, messages)
        squares = jnp.zeros((HALF, HEAD), F32)
        for h in range(SHARE):
            o_ref[p * HALF:(p + 1) * HALF, g * GW + h * HEAD:g * GW + (h + 1) * HEAD] = out[h]
            squares = squares + out[h] * out[h]
        rows = slice(p * HALF, (p + 1) * HALF)
        if g == 0:
            sq_p[rows, :] = squares
        else:
            total = jnp.sum(squares + sq_p[rows, :], axis=1, keepdims=True)
            sq_p[rows, :] = jnp.broadcast_to(total, (HALF, HEAD))

    def finish0():
        for p in (0, 1):
            for d in (0, 1):
                o_copy(d, 3, p).wait_recv()
            finish(0, p, [(mb0.at[d, 3], p * HALF) for d in (0, 1)])

    def retire():
        rz_copy.wait_recv()
        group = y * 2 + zhi
        for i in (0, 1):
            got = jnp.where(section_ref[group] == 0, tokens(i, group).astype(F32), 0.0)
            for source, ref, a in (
                ((1 - y) * 2 + zhi, rt_y, 0),
                (y * 2 + 1 - zhi, rz_r, 0),
                ((1 - y) * 2 + 1 - zhi, rz_r, 32),
            ):
                got = jnp.where(section_ref[source] == 0, ref[a + 16 * i:a + 16 * i + 16].astype(F32), got)
            fresh_ref[i] = got.astype(BF16)

    def z0(*passes):
        def run():
            for args in passes:
                z_pass(*args)
        return run

    def xy(c, *passes):
        def run():
            for args in passes:
                xy_pass(c, *args)
        return run

    before = {
        1: [z0((1, 1, True), (0, 2, True)), xy(xk, two_x, two_y), xy(xq, two_x, two_y), z0((0, 2, False))],
        2: [z0((1, 1, False), (0, 3, True))],
        3: [z0((1, 2, True)), xy(xk, last), lambda: make_bias(1)],
        4: [far_retire],
        7: [z0((1, 2, False)), xy(xq, last), lambda: make_bias(2)],
        8: [z0((1, 3, True)), lambda: make_bias(3)],
    }
    after = {
        4: [lambda: ring(0, True)],
        5: [lambda: ring(1, False)],
        7: [lambda: ring(1, True)],
        8: [lambda: ring(2, False)],
        9: [tree_far],
        10: [lambda: ring(2, True)],
        11: [lambda: ring(3, False), tree_y],
        12: [tree_x],
        13: [lambda: ring(3, True), tree_near],
        14: [tree_near2],
        15: [tree_last, finish0, retire],
    }

    def events(table, u, parity):
        if isinstance(u, int):
            for event in table.get(u, ()):
                event()
            return
        for at_unit, items in table.items():
            if at_unit % 2 == parity and at_unit < 14:
                @pl.when(u == at_unit)
                def _(items=items):
                    for event in items:
                        event()

    z_begin(0, True)
    xy_begin(xk)
    rt_copy.start()
    l_st[...] = jnp.zeros(l_st.shape, F32)
    z_begin(0, False)
    acc[...] = jnp.zeros(acc.shape, F32)
    z_begin(1, True)
    z_pass(0, 0, True)
    xy_begin(xq)
    z_begin(1, False)
    z_pass(0, 0, False)
    xy_pass(xk, *own_x)
    xy_pass(xk, *own_y)
    z_pass(1, 0, True)
    make_bias(0)
    ctx = score_begin(0)
    top = None
    for t in range(SPAN // TILE):
        top = score_tile(ctx, 0, t, top)
    score_end(ctx, 0, top)
    xy_pass(xq, *own_x)
    xy_pass(xq, *own_y)
    z_pass(0, 1, True)
    z_pass(1, 0, False)
    z_pass(0, 1, False)

    def two(i, carry):
        for parity in (0, 1):
            u = 2 * i + parity
            events(before, u, parity)
            step(u, parity, True)
            events(after, u, parity)
        return carry

    lax.fori_loop(0, 7, two, 0)
    events(before, 14, 0)
    step(14, 0, True)
    events(after, 14, 0)
    step(15, 1, False)
    events(after, 15, 1)

    wait_for("x2u0", "x2u1", "x2d0", "x2d1", "y3", "yf")
    for p in (0, 1):
        finish(1, p, [arrived(f"x2u{p}"), arrived(f"x2d{p}"), arrived("yf" if p == 0 else "y3")])
    rows = jnp.concatenate([sq_p[...], jnp.zeros((HEAD - TOK, HEAD), F32)], 0)
    sq_s[...] = rows.T[0:8]
    sc = [remote(sq_s, sq_r.at[i], sent.at[8], h_recv.at[i], head_dev[i]) for i in range(3)]
    for copy in sc:
        copy.start()
    total = sq_s[...]
    for i, copy in enumerate(sc):
        copy.wait_recv()
        total = total + sq_r[i]
    total_ref[...] = jnp.concatenate([total] * 16, 0).T[0:TOK]

    for i, refs in enumerate((
        (qg.at[0, 0:7],),
        (kv.at[0], kv.at[1, 0:3]),
        (kv.at[0], kv.at[1, 0:3]),
        (qg.at[0, 0:7],),
        (rt_s,),
        (rz_s,),
        (sb0.at[0], sb0.at[1, 0:3]),
        (sb1,),
        (sq_r,),
    )):
        for ref in refs:
            pltpu.make_async_copy(ref, ref, sent.at[i]).wait()


def finish_kernel(count_ref, o_ref, total_ref, gain_ref, ck_ref, cv_ref, fresh_ref, out_ref, nck_ref, ncv_ref):
    scale = lax.rsqrt(total_ref[...] / (HEADS * HEAD) + 1e-06)
    for h in range(2 * SHARE):
        cols = slice(h * HEAD, (h + 1) * HEAD)
        out_ref[:, cols] = o_ref[:, cols] * scale * gain_ref[cols].reshape(1, HEAD)
    spot = lax.broadcasted_iota(jnp.int32, (CACHE, 16), 0) - lax.broadcasted_iota(jnp.int32, (CACHE, 16), 1)
    chosen = jnp.where(spot == count_ref[0], 1.0, 0.0).astype(BF16)
    row = lax.broadcasted_iota(jnp.int32, (CACHE, 256), 0) - count_ref[0]
    fresh = (row >= 0) & (row < 16)
    for i, (old, new) in enumerate(((ck_ref, nck_ref), (cv_ref, ncv_ref))):
        moved = jnp.dot(chosen, fresh_ref[i], preferred_element_type=F32)
        new[...] = jnp.where(fresh, moved, old[...].astype(F32)).astype(BF16)


def on_device(queries, keys, values, cache_keys, cache_values, cache_count, span_section, norm_gain):
    vmem = pl.BlockSpec(memory_space=pltpu.VMEM)
    smem = pl.BlockSpec(memory_space=pltpu.SMEM)
    hbm = pl.BlockSpec(memory_space=pl.ANY)
    dma = pltpu.SemaphoreType.DMA
    state = pltpu.VMEM((2, NZ, TOK, GW), F32)
    o, total, fresh = pl.pallas_call(
        kernel,
        out_shape=[
            jax.ShapeDtypeStruct((TOK, 2 * GW), F32),
            jax.ShapeDtypeStruct((TOK, HEAD), F32),
            jax.ShapeDtypeStruct((2, 16, 256), BF16),
        ],
        in_specs=[hbm] * 5 + [smem] * 2,
        out_specs=[vmem] * 3,
        scratch_shapes=[
            pltpu.VMEM((2, NZ, TOK, GW), BF16),
            pltpu.VMEM((4, 4, KVR, HEAD), BF16),
            pltpu.VMEM((4, 2, 1, SPAN), F32),
            state, state, state,
            pltpu.VMEM((PAIR, SPAN), F32), pltpu.VMEM((PAIR, SPAN), F32),
            pltpu.VMEM((PAIR, HEAD), F32), pltpu.VMEM((PAIR, HEAD), F32),
            pltpu.VMEM((PAIR, HEAD), F32), pltpu.VMEM((PAIR, HEAD), F32),
            pltpu.VMEM((2, 4, TOK, MW), BF16), pltpu.VMEM((2, 4, TOK, MW), BF16),
            pltpu.VMEM((MSG_ROWS, MW), BF16), pltpu.VMEM((MSG_ROWS, MW), BF16),
            pltpu.VMEM((64, 256), BF16), pltpu.VMEM((64, 256), BF16),
            pltpu.VMEM((64, 256), BF16), pltpu.VMEM((64, 256), BF16),
            pltpu.VMEM((TOK, HEAD), F32),
            pltpu.VMEM((8, HEAD), F32),
            pltpu.VMEM((3, 8, HEAD), F32),
            dma((10,)),
            dma((9,)), dma((2, 4, 2)), dma((2, 4, 2)), dma((12,)), dma((12,)), dma((2,)), dma((2, 4, 2)), dma((len(MSG),)),
            dma((3,)),
        ],
        compiler_params=pltpu.CompilerParams(
            collective_id=0, has_side_effects=True, vmem_limit_bytes=56 * 2**20
        ),
    )(queries, keys, values, cache_keys, cache_values, cache_count, span_section)
    return pl.pallas_call(
        finish_kernel,
        out_shape=[
            jax.ShapeDtypeStruct((TOK, 2 * GW), F32),
            jax.ShapeDtypeStruct((CACHE, 256), BF16),
            jax.ShapeDtypeStruct((CACHE, 256), BF16),
        ],
        in_specs=[smem] + [vmem] * 6,
        out_specs=[vmem] * 3,
        compiler_params=pltpu.CompilerParams(vmem_limit_bytes=56 * 2**20),
    )(cache_count, o, total, norm_gain, cache_keys, cache_values, fresh)


def solution(mesh):
    placed = (
        P("slot", "head"),
        P("slot", "head"),
        P("slot", "head"),
        P("slot", "head"),
        P("slot", "head"),
        P("slot"),
        P(),
        P("head"),
    )
    return jax.shard_map(
        on_device,
        mesh=mesh,
        in_specs=placed,
        out_specs=(P("slot", "head"), P("slot", "head"), P("slot", "head")),
        check_vma=False,
    )
```

```python
import functools

import jax
import jax.numpy as jnp
from jax import lax
from jax.experimental import pallas as pl
from jax.experimental.pallas import tpu as pltpu
from jax.sharding import PartitionSpec as P

MESH = pl.DeviceIdType.MESH
F32 = jnp.float32
BF16 = jnp.bfloat16

HEADS = 48
HEAD = 128
TOK = 64
CACHE = 256
KEYS = TOK + CACHE
KVR = 2 * KEYS + 16
SHARE = 6
GW = SHARE * HEAD
MW = GW + HEAD
HALF = TOK // 2
PAIR = 2 * SHARE * TOK
SPAN = 4 * KEYS
TILE = 256
C = HEAD ** -0.5 * 1.4426950408889634
NEG = -1e30
NZ, NX = 8, 4
Z_ORDER = (0, 1, 7, 2, 6, 3, 5, 4)
G0_PAIRS = ((1, 7), (2, 6), (3, 5), (4, 0))
G1_PAIRS = ((7, 4), (5, 6), (1, 2), (3, 0))
UNITS = (
    (0, 0, 0), (0, 0, 1), (0, 0, 2), (1, 0, 2),
    (1, 0, 3), (0, 0, 3), (0, 1, 3), (1, 0, 0),
    (1, 1, 0), (0, 1, 2), (1, 0, 1), (1, 1, 1),
    (0, 1, 1), (1, 1, 2), (0, 1, 0), (1, 1, 3),
)
PLAN = (
    "zq0T", "xkown_x", "xkown_y", "rt", "clear_l", "zq0F", "clear_acc", "zk0T", "xqown_x", "xqown_y",
    "zq1T", "zk0F", "zq1F", "xkfwd", "xky12", "xkyx", "S", "zk1T", "P", "xqfwd",
    "xqy12", "xqyx", "zq2T", "zq2F", "S", "zk1F", "P", "zk2T", "zq3T", "xky3",
    "xkyf", "S", "xqyf", "xqy3", "P", "zk2F", "S", "PS", "zk3T", "PS",
    "PS", "PS", "o0T", "PS", "far", "PS", "y7", "xx1", "PS", "o1T",
    "o1F", "PS", "PS", "x1", "y56", "xx2", "PS", "o2T", "o2F", "PS",
    "PS", "x2", "P", "yf", "o3T", "o3F", "y3",
)
MSG = {}
for _name, _rows in (
    ("y7", 32), ("y5", 32), ("y6", 32), ("y3", 32), ("x1u", 32), ("x1d", 32), ("xx1u", 16), ("xx1d", 16),
    ("x2u0", 32), ("x2u1", 32), ("x2d0", 32), ("x2d1", 32), ("xx2u", 32), ("xx2d", 32), ("yf", 32),
):
    MSG[_name] = (len(MSG), sum(r for _, _, r in MSG.values()), _rows)
MSG_ROWS = sum(r for _, _, r in MSG.values())


def kernel(
    q_hbm, k_hbm, v_hbm, ck_hbm, cv_hbm, count_ref, section_ref,
    o_ref, total_ref, fresh_ref,
    qg, kv, bias, acc, l_st, m_st, s0, s1, mx0, mx1, al0, al1,
    sb0, mb0, sb1, mb1, rt_s, rt_y, rz_s, rz_r, sq_p, sq_s, sq_r, in_sem,
    sent, zq_recv, zk_recv, xk_recv, xq_recv, r_recv, o_recv, p_recv, h_recv,
):
    slot = lax.axis_index("slot")
    head = lax.axis_index("head")
    y = slot // 32
    z = slot // 4 % 8
    x = slot % 4
    zhi = z // 4

    def at(y_, z_, x_):
        return (y_ * 32 + z_ * 4 + x_, head)

    z_dev = (at(y, (z + 1) % NZ, x), at(y, (z + 7) % NZ, x))
    x_dev = (at(y, z, (x + 1) % NX), at(y, z, (x + 3) % NX))
    y_dev = at(1 - y, z, x)
    far_dev = at(y, (z + 4) % NZ, x)
    pair_core = 1 - head % 2
    head_dev = ((slot, head // 2 * 2 + pair_core), (slot, (head + 2) % 4), (slot, (head + 2) % 4 // 2 * 2 + pair_core))

    barrier = pltpu.get_barrier_semaphore()
    peers = z_dev + x_dev + (y_dev,) + head_dev
    for peer in peers:
        pl.semaphore_signal(barrier, inc=1, device_id=peer, device_id_type=MESH)

    loads = []
    for g in (0, 1):
        cols = slice(g * HEAD, (g + 1) * HEAD)
        loads += [
            (q_hbm.at[:, g * GW:(g + 1) * GW], qg.at[g, 0]),
            (k_hbm.at[:, cols], kv.at[2 * g, 0, 0:TOK]),
            (ck_hbm.at[:, cols], kv.at[2 * g, 0, TOK:KEYS]),
            (v_hbm.at[:, cols], kv.at[2 * g, 0, KEYS:KEYS + TOK]),
            (cv_hbm.at[:, cols], kv.at[2 * g, 0, KEYS + TOK:2 * KEYS]),
        ]
    loads = [pltpu.make_async_copy(a, b, in_sem.at[i]) for i, (a, b) in enumerate(loads)]
    for copy in loads:
        copy.start()
    for g in (0, 1):
        kv[2 * g, 0, 2 * KEYS:KVR] = jnp.full((16, HEAD), count_ref[0].astype(F32), F32).astype(BF16)
    for copy in loads:
        copy.wait()

    def tokens(kind, group):
        rows = pl.ds(pl.multiple_of(kind * KEYS + group * 16, 16), 16)
        return jnp.concatenate([kv[0, 0, rows], kv[2, 0, rows]], 1)

    for i, group in enumerate(((1 - y) * 2 + zhi, (1 - y) * 2 + 1 - zhi)):
        rt_s[32 * i:32 * i + 16] = tokens(0, group)
        rt_s[32 * i + 16:32 * i + 32] = tokens(1, group)
    pl.semaphore_wait(barrier, len(peers))

    def remote(src, dst, send, recv, dev):
        return pltpu.make_async_remote_copy(
            src_ref=src, dst_ref=dst, send_sem=send, recv_sem=recv, device_id=dev, device_id_type=MESH
        )

    def zq_view(e, p):
        return qg.at[0, e, p * HALF:(p + 1) * HALF]

    def zk_view(e, p):
        spot = Z_ORDER.index(e)
        rows = slice(0, KEYS) if p == 0 else slice(KEYS, KVR)
        return kv.at[2 + spot // 4, spot % 4, rows]

    def z_copy(kind, d, step, p):
        view, send, recv = ((zq_view, sent.at[0], zq_recv), (zk_view, sent.at[1], zk_recv))[kind]
        src = (-step if d == 0 else step) % NZ
        dst = (-step - 1 if d == 0 else step + 1) % NZ
        return remote(view(src, p), view(dst, p), send, recv.at[d, step, p], z_dev[d])

    def xy_copies(view, cut, quarter, end, send, recv):
        table = {
            "own_up": (0, 1, 0, end, x_dev[0]),
            "own_down": (0, 2, 0, end, x_dev[1]),
            "own_y": (0, 3, 0, end, y_dev),
            "fwd_up": (1, 4, 0, cut, x_dev[0]),
            "fwd_down": (2, 4, cut, end, x_dev[1]),
            "y_up": (3, 5, 0, cut, x_dev[0]),
            "y_down": (3, 6, 0, cut, x_dev[1]),
            "yf_up": (5, 7, 0, quarter, x_dev[0]),
            "yf_down": (6, 7, quarter, cut, x_dev[1]),
            "y_1": (1, 5, cut, end, y_dev),
            "y_2": (2, 6, cut, end, y_dev),
            "y_3": (4, 7, cut, end, y_dev),
        }
        return {
            n: remote(view(s, a, b), view(t, a, b), send, recv.at[i], dev)
            for i, (n, (s, t, a, b, dev)) in enumerate(table.items())
        }

    xk = xy_copies(lambda s, a, b: kv.at[s // 4, s % 4, a:b], KEYS, KEYS // 2, KVR, sent.at[2], xk_recv)
    xq = xy_copies(lambda s, a, b: qg.at[1, s, a:b], HALF, HALF // 2, TOK, sent.at[3], xq_recv)

    XY = {
        "own_x": ("own_up", "own_down"), "own_y": ("own_y",), "fwd": ("fwd_up", "fwd_down"), "y12": ("y_1", "y_2"),
        "yx": ("y_up", "y_down"), "yf": ("yf_up", "yf_down"), "y3": ("y_3",),
    }
    XY_NEEDS = {"fwd": "own_x", "y12": "own_x", "yx": "own_y", "yf": "yx", "y3": "fwd"}
    TREE = {
        "y7": ("y7",), "xx1": ("xx1u", "xx1d"), "x1": ("x1u", "x1d"), "y56": ("y5", "y6"), "xx2": ("xx2u", "xx2d"),
        "x2": ("x2u0", "x2u1", "x2d0", "x2d1"), "yf": ("yf",), "y3": ("y3",),
    }

    def copies(name):
        kind, rest = name[:2], name[2:]
        if kind in ("zq", "zk"):
            return [z_copy(kind == "zk", d, int(rest[0]), d if rest[1] == "T" else 1 - d) for d in (0, 1)]
        if kind in ("xk", "xq"):
            return [(xk if kind == "xk" else xq)[n] for n in XY[rest]]
        if name[0] == "o":
            return [o_copy(d, int(name[1]), d if name[2] == "T" else 1 - d) for d in (0, 1)]
        return [p_copy(n) for n in TREE[name]]

    have = set()

    def need(*names):
        for name in names:
            if name not in have:
                have.add(name)
                for copy in copies(name):
                    copy.wait_recv()

    def begin(name):
        kind, rest = name[:2], name[2:]
        if kind in ("zq", "zk"):
            if rest[0] != "0":
                need(kind + str(int(rest[0]) - 1) + rest[1])
        elif rest in XY_NEEDS:
            need(kind + XY_NEEDS[rest])
        for copy in copies(name):
            copy.start()

    rt_copy = remote(rt_s, rt_y, sent.at[4], r_recv.at[0], y_dev)
    rz_copy = remote(rz_s, rz_r, sent.at[5], r_recv.at[1], far_dev)

    def far_retire():
        group = y * 2 + 1 - zhi
        rz_s[0:16] = tokens(0, group)
        rz_s[16:32] = tokens(1, group)
        rt_copy.wait_recv()
        rz_s[32:64] = rt_y[32:64]
        rz_copy.start()

    lane = lax.broadcasted_iota(jnp.int32, (1, SPAN), 1)

    def make_bias(ph):
        for sel in (0, 1):
            if ph < 2:
                mine = section_ref[y * 2 + sel]
            else:
                mine = section_ref[(y + sel) % 2 * 2 + zhi]
            total = jnp.zeros((1, SPAN), F32)
            for s in range(4):
                if ph < 2:
                    block = ph * 4 + s
                    key_group = (y if block in (0, 1, 2, 4) else 1 - y) * 2 + zhi
                else:
                    key_group = y * 2 + (z + Z_ORDER[(ph - 2) * 4 + s]) % NZ // 4
                seen = section_ref[key_group] <= mine
                tok = jnp.where(seen, 0.0, NEG).astype(F32)
                live = kv[ph, s, 2 * KEYS:KVR, :].astype(F32)[0:1, 0:1]
                row = lane - s * KEYS
                dead = jnp.where((row - TOK).astype(F32) >= live, NEG, 0.0)
                here = (row >= 0) & (row < KEYS)
                total = jnp.where(here, jnp.where(row < TOK, tok, dead), total)
            bias[ph, sel] = total

    def unit(u):
        g, half, j = UNITS[u]
        if g == 0:
            c1, c2 = G0_PAIRS[j]
            sel = lambda c: (z + c) % NZ // 4
        else:
            c1, c2 = G1_PAIRS[j]
            sel = lambda c: 1 if c in (3, 5, 6, 7) else 0
        return 2 * g + half, g, c1, c2, sel(c1), sel(c2)

    scores, tops, alphas = (s0, s1), (mx0, mx1), (al0, al1)
    ones = jnp.ones((TILE, HEAD), BF16)

    def key_tile(ph, t, base):
        parts, a = [], t * TILE
        while a < (t + 1) * TILE:
            s = a // KEYS
            b = min((t + 1) * TILE, (s + 1) * KEYS)
            parts.append(kv[ph, s, base + a - s * KEYS:base + b - s * KEYS])
            a = b
        return jnp.concatenate(parts, 0) if len(parts) > 1 else parts[0]

    def stacked(ref, g, c1, c2):
        return jnp.concatenate([ref[g, c, :, h * HEAD:(h + 1) * HEAD] for c in (c1, c2) for h in range(SHARE)], 0)

    def unstack(ref, g, c1, c2, value):
        for i, c in enumerate((c1, c2)):
            for h in range(SHARE):
                r = (i * SHARE + h) * TOK
                ref[g, c, :, h * HEAD:(h + 1) * HEAD] = value[r:r + TOK]

    def score_tile(ctx, buf, t, top):
        (ph, g, c1, c2, b1, b2), q = ctx
        s = lax.dot_general(q, key_tile(ph, t, 0), (((1,), (1,)), ((), ())), preferred_element_type=F32)
        cols = slice(t * TILE, (t + 1) * TILE)
        s = jnp.concatenate(
            [s[:PAIR // 2] + bias[ph, b1, :, cols], s[PAIR // 2:] + bias[ph, b2, :, cols]], 0
        )
        scores[buf][:, cols] = s
        t2 = jnp.maximum(s[:, :HEAD], s[:, HEAD:])
        return t2 if top is None else jnp.maximum(top, t2)

    def score_begin(u):
        info = unit(u)
        return info, stacked(qg, info[1], info[2], info[3])

    def score_end(ctx, buf, top):
        _, g, c1, c2, _, _ = ctx[0]
        new = jnp.broadcast_to(jnp.max(top, axis=1, keepdims=True), (PAIR, HEAD))
        if ctx[0][0] % 2:
            old = stacked(m_st, g, c1, c2)
            new = jnp.maximum(old, new)
            alphas[buf][...] = jnp.exp2((old - new) * C)
        tops[buf][...] = new
        unstack(m_st, g, c1, c2, new)

    def score_alone(u):
        ctx = score_begin(u)
        top = None
        for t in range(SPAN // TILE):
            top = score_tile(ctx, u % 2, t, top)
        score_end(ctx, u % 2, top)

    def step(u, buf, ahead):
        ph, g, c1, c2, _, _ = unit(u)
        if ahead:
            ctx = score_begin(u + 1)
        top = None
        new_top = tops[buf][...]
        total = None
        for t in range(SPAN // TILE):
            if ahead:
                top = score_tile(ctx, 1 - buf, t, top)
            s = scores[buf][:, t * TILE:(t + 1) * TILE]
            weight = jnp.concatenate(
                [jnp.exp2((s[:, :HEAD] - new_top) * C), jnp.exp2((s[:, HEAD:] - new_top) * C)], 1
            ).astype(BF16)
            v = jnp.concatenate([key_tile(ph, t, KEYS), ones], 1)
            mixed = jnp.dot(weight, v, preferred_element_type=F32)
            total = mixed if total is None else total + mixed
        fresh_acc, fresh_sum = total[:, :HEAD], total[:, HEAD:]
        if ph % 2:
            alpha = alphas[buf][...]
            fresh_acc = stacked(acc, g, c1, c2) * alpha + fresh_acc
            fresh_sum = stacked(l_st, g, c1, c2) * alpha + fresh_sum
        unstack(acc, g, c1, c2, fresh_acc)
        unstack(l_st, g, c1, c2, fresh_sum)
        if ahead:
            score_end(ctx, 1 - buf, top)

    def gather_piece(g, c, r0, n, messages):
        rows = slice(r0, r0 + n)
        lanes = lax.broadcasted_iota(jnp.int32, (n, HEAD), 1)
        sums = jnp.ones((n, HEAD), F32)
        peak = jnp.zeros((n, HEAD), F32)
        for h in range(SHARE):
            cols = slice(h * HEAD, (h + 1) * HEAD)
            sums = jnp.where(lanes % 16 == h, l_st[g, c, rows, cols], sums)
            peak = jnp.where(lanes % 16 == h, m_st[g, c, rows, cols], peak)
        logs = [peak * C + jnp.log2(sums)]
        for ref, a in messages:
            p = ref[a:a + n, GW:MW].astype(F32)
            logs.append(p + pltpu.roll(p, 16, 1) + pltpu.roll(p, 32, 1) + pltpu.roll(p, 48, 1))
        top = functools.reduce(jnp.maximum, logs)
        weights = [jnp.exp2(item - top) for item in logs]
        total = functools.reduce(jnp.add, weights)
        share = 1.0 / total
        factors = [w * share for w in weights]
        factors[0] = factors[0] / sums
        out = []
        for h in range(SHARE):
            cols = slice(h * HEAD, (h + 1) * HEAD)
            spread = [jnp.broadcast_to(f[:, h:h + 1], (n, HEAD)) for f in factors]
            o = acc[g, c, rows, cols] * spread[0]
            for (ref, a), f in zip(messages, spread[1:]):
                o = o + ref[a:a + n, cols].astype(F32) * f
            out.append(o)
        return out, top + jnp.log2(total)

    def write_piece(dst, a, n, out, logs):
        for h in range(SHARE):
            dst[a:a + n, h * HEAD:(h + 1) * HEAD] = out[h].astype(BF16)
        lanes = lax.broadcasted_iota(jnp.int32, (n, HEAD), 1) // 16 % 4
        first = logs.astype(BF16).astype(F32)
        rest = logs - first
        second = rest.astype(BF16).astype(F32)
        third = rest - second
        parts = jnp.where(lanes == 0, first, jnp.where(lanes == 1, second, jnp.where(lanes == 2, third, 0.0)))
        dst[a:a + n, GW:MW] = parts.astype(BF16)

    def o_copy(d, hop, p):
        rows = slice(p * HALF, (p + 1) * HALF)
        return remote(
            sb0.at[d, hop, rows], mb0.at[d, hop, rows], sent.at[6], o_recv.at[d, hop, p], z_dev[d]
        )

    def ring(hop, first):
        todo = []
        for d in (0, 1):
            p = d if first else 1 - d
            messages = []
            if hop > 1 or (hop == 1 and first):
                need(f"o{hop - 1}{'T' if first else 'F'}")
                messages = [(mb0.at[d, hop - 1], p * HALF)]
            todo.append((d, p, (4 - hop) if d == 0 else (4 + hop), messages))
        pieces = [gather_piece(0, c, p * HALF, HALF, messages) for d, p, c, messages in todo]
        for (d, p, _, _), piece in zip(todo, pieces):
            write_piece(sb0.at[d, hop], p * HALF, HALF, *piece)
        for d, p, _, _ in todo:
            o_copy(d, hop, p).start()

    def p_copy(name):
        i, a, n = MSG[name]
        dev = y_dev if name[0] == "y" else x_dev[0 if "u" in name else 1]
        return remote(sb1.at[a:a + n], mb1.at[a:a + n], sent.at[7], p_recv.at[i], dev)

    def arrived(name, skip=0):
        return (mb1, MSG[name][1] + skip)

    def tree(name, c, r0, n, *needs):
        _, a, _ = MSG[name]
        write_piece(sb1, a, n, *gather_piece(1, c, r0, n, [arrived(*need) for need in needs]))
        p_copy(name).start()

    def split(name, c, parts):
        _, a, _ = MSG[name]
        for r0, needs in parts:
            write_piece(sb1, a + r0, 16, *gather_piece(1, c, r0, 16, needs))
        p_copy(name).start()

    def tree_y7():
        tree("y7", 7, 32, 32)

    def tree_xx1():
        tree("xx1u", 7, 0, 16)
        tree("xx1d", 7, 16, 16)

    def tree_x1():
        tree("x1u", 4, 0, 32)
        need("y7")
        tree("x1d", 4, 32, 32, ("y7",))

    def tree_y56():
        tree("y5", 5, 32, 32)
        tree("y6", 6, 32, 32)

    def tree_xx2():
        need("xx1")
        split("xx2u", 6, ((0, [arrived("xx1u")]), (16, [])))
        split("xx2d", 5, ((0, []), (16, [arrived("xx1d")])))

    def tree_x2():
        need("x1", "y56")
        tree("x2u0", 2, 0, 32, ("x1u",))
        tree("x2u1", 2, 32, 32, ("y6",))
        tree("x2d0", 1, 0, 32)
        tree("x2d1", 1, 32, 32, ("y5",), ("x1d",))

    def tree_yf():
        need("xx2")
        tree("yf", 3, 0, 32, ("xx2u",), ("xx2d",))

    def tree_y3():
        tree("y3", 3, 32, 32)

    trees = {
        "y7": tree_y7, "xx1": tree_xx1, "x1": tree_x1, "y56": tree_y56, "xx2": tree_xx2, "x2": tree_x2, "yf": tree_yf,
        "y3": tree_y3,
    }

    def finish(g, p, messages):
        out, _ = gather_piece(g, 0, p * HALF, HALF, messages)
        squares = jnp.zeros((HALF, HEAD), F32)
        for h in range(SHARE):
            o_ref[p * HALF:(p + 1) * HALF, g * GW + h * HEAD:g * GW + (h + 1) * HEAD] = out[h]
            squares = squares + out[h] * out[h]
        rows = slice(p * HALF, (p + 1) * HALF)
        if g == 0:
            sq_p[rows, :] = squares
        else:
            total = jnp.sum(squares + sq_p[rows, :], axis=1, keepdims=True)
            sq_p[rows, :] = jnp.broadcast_to(total, (HALF, HEAD))

    def finish0():
        need("o3T", "o3F")
        for p in (0, 1):
            finish(0, p, [(mb0.at[d, 3], p * HALF) for d in (0, 1)])

    def retire():
        rz_copy.wait_recv()
        group = y * 2 + zhi
        for i in (0, 1):
            got = jnp.where(section_ref[group] == 0, tokens(i, group).astype(F32), 0.0)
            for source, ref, a in (
                ((1 - y) * 2 + zhi, rt_y, 0),
                (y * 2 + 1 - zhi, rz_r, 0),
                ((1 - y) * 2 + 1 - zhi, rz_r, 32),
            ):
                got = jnp.where(section_ref[source] == 0, ref[a + 16 * i:a + 16 * i + 16].astype(F32), got)
            fresh_ref[i] = got.astype(BF16)

    ready = set()

    def unit_needs(u):
        g, half, j = UNITS[u]
        if g == 0:
            need(*[f"zq{k}{p}" for k in range(j + 1) for p in "TF" if k < 3 or p == "T"])
            need("xkown_x", "xkown_y")
            if half:
                need("xkfwd", "xky12", "xkyx", "xkyf", "xky3")
        else:
            need("xqown_x", "xqown_y")
            if j < 2:
                need("xqfwd", "xqy12", "xqyx", "xqyf", "xqy3")
            need(*[f"zk{k}{p}" for k in range(4 if half else 2) for p in "TF" if k < 3 or p == "T"])
        if 2 * g + half not in ready:
            ready.add(2 * g + half)
            make_bias(2 * g + half)

    scored = done = 0
    for op in PLAN:
        if op == "S":
            unit_needs(scored)
            score_alone(scored)
            scored += 1
        elif op == "P":
            step(done, done % 2, False)
            done += 1
        elif op == "PS":
            unit_needs(scored)
            step(done, done % 2, True)
            scored += 1
            done += 1
        elif op == "clear_l":
            l_st[...] = jnp.zeros(l_st.shape, F32)
        elif op == "clear_acc":
            acc[...] = jnp.zeros(acc.shape, F32)
        elif op == "rt":
            rt_copy.start()
        elif op == "far":
            need("zq3T")
            far_retire()
        elif op in trees:
            trees[op]()
        elif op[0] == "o":
            ring(int(op[1]), op[2] == "T")
        else:
            begin(op)
    finish0()
    retire()
    need("x2", "y3", "yf")
    for p in (0, 1):
        finish(1, p, [arrived(f"x2u{p}"), arrived(f"x2d{p}"), arrived("yf" if p == 0 else "y3")])
    rows = jnp.concatenate([sq_p[...], jnp.zeros((HEAD - TOK, HEAD), F32)], 0)
    sq_s[...] = rows.T[0:8]
    sc = [remote(sq_s, sq_r.at[i], sent.at[8], h_recv.at[i], head_dev[i]) for i in range(3)]
    for copy in sc:
        copy.start()
    total = sq_s[...]
    for i, copy in enumerate(sc):
        copy.wait_recv()
        total = total + sq_r[i]
    total_ref[...] = jnp.concatenate([total] * 16, 0).T[0:TOK]

    for i, refs in enumerate((
        (qg.at[0, 0:7],),
        (kv.at[0], kv.at[1, 0:3]),
        (kv.at[0], kv.at[1, 0:3]),
        (qg.at[0, 0:7],),
        (rt_s,),
        (rz_s,),
        (sb0.at[0], sb0.at[1, 0:3]),
        (sb1,),
        (sq_r,),
    )):
        for ref in refs:
            pltpu.make_async_copy(ref, ref, sent.at[i]).wait()


def finish_kernel(count_ref, o_ref, total_ref, gain_ref, ck_ref, cv_ref, fresh_ref, out_ref, nck_ref, ncv_ref):
    scale = lax.rsqrt(total_ref[...] / (HEADS * HEAD) + 1e-06)
    for h in range(2 * SHARE):
        cols = slice(h * HEAD, (h + 1) * HEAD)
        out_ref[:, cols] = o_ref[:, cols] * scale * gain_ref[cols].reshape(1, HEAD)
    spot = lax.broadcasted_iota(jnp.int32, (CACHE, 16), 0) - lax.broadcasted_iota(jnp.int32, (CACHE, 16), 1)
    chosen = jnp.where(spot == count_ref[0], 1.0, 0.0).astype(BF16)
    row = lax.broadcasted_iota(jnp.int32, (CACHE, 256), 0) - count_ref[0]
    fresh = (row >= 0) & (row < 16)
    for i, (old, new) in enumerate(((ck_ref, nck_ref), (cv_ref, ncv_ref))):
        moved = jnp.dot(chosen, fresh_ref[i], preferred_element_type=F32)
        new[...] = jnp.where(fresh, moved, old[...].astype(F32)).astype(BF16)


def on_device(queries, keys, values, cache_keys, cache_values, cache_count, span_section, norm_gain):
    vmem = pl.BlockSpec(memory_space=pltpu.VMEM)
    smem = pl.BlockSpec(memory_space=pltpu.SMEM)
    hbm = pl.BlockSpec(memory_space=pl.ANY)
    dma = pltpu.SemaphoreType.DMA
    state = pltpu.VMEM((2, NZ, TOK, GW), F32)
    o, total, fresh = pl.pallas_call(
        kernel,
        out_shape=[
            jax.ShapeDtypeStruct((TOK, 2 * GW), F32),
            jax.ShapeDtypeStruct((TOK, HEAD), F32),
            jax.ShapeDtypeStruct((2, 16, 256), BF16),
        ],
        in_specs=[hbm] * 5 + [smem] * 2,
        out_specs=[vmem] * 3,
        scratch_shapes=[
            pltpu.VMEM((2, NZ, TOK, GW), BF16),
            pltpu.VMEM((4, 4, KVR, HEAD), BF16),
            pltpu.VMEM((4, 2, 1, SPAN), F32),
            state, state, state,
            pltpu.VMEM((PAIR, SPAN), F32), pltpu.VMEM((PAIR, SPAN), F32),
            pltpu.VMEM((PAIR, HEAD), F32), pltpu.VMEM((PAIR, HEAD), F32),
            pltpu.VMEM((PAIR, HEAD), F32), pltpu.VMEM((PAIR, HEAD), F32),
            pltpu.VMEM((2, 4, TOK, MW), BF16), pltpu.VMEM((2, 4, TOK, MW), BF16),
            pltpu.VMEM((MSG_ROWS, MW), BF16), pltpu.VMEM((MSG_ROWS, MW), BF16),
            pltpu.VMEM((64, 256), BF16), pltpu.VMEM((64, 256), BF16),
            pltpu.VMEM((64, 256), BF16), pltpu.VMEM((64, 256), BF16),
            pltpu.VMEM((TOK, HEAD), F32),
            pltpu.VMEM((8, HEAD), F32),
            pltpu.VMEM((3, 8, HEAD), F32),
            dma((10,)),
            dma((9,)), dma((2, 4, 2)), dma((2, 4, 2)), dma((12,)), dma((12,)), dma((2,)), dma((2, 4, 2)), dma((len(MSG),)),
            dma((3,)),
        ],
        compiler_params=pltpu.CompilerParams(
            collective_id=0, has_side_effects=True, vmem_limit_bytes=56 * 2**20
        ),
    )(queries, keys, values, cache_keys, cache_values, cache_count, span_section)
    return pl.pallas_call(
        finish_kernel,
        out_shape=[
            jax.ShapeDtypeStruct((TOK, 2 * GW), F32),
            jax.ShapeDtypeStruct((CACHE, 256), BF16),
            jax.ShapeDtypeStruct((CACHE, 256), BF16),
        ],
        in_specs=[smem] + [vmem] * 6,
        out_specs=[vmem] * 3,
        compiler_params=pltpu.CompilerParams(vmem_limit_bytes=56 * 2**20),
    )(cache_count, o, total, norm_gain, cache_keys, cache_values, fresh)


def solution(mesh):
    placed = (
        P("slot", "head"),
        P("slot", "head"),
        P("slot", "head"),
        P("slot", "head"),
        P("slot", "head"),
        P("slot"),
        P(),
        P("head"),
    )
    return jax.shard_map(
        on_device,
        mesh=mesh,
        in_specs=placed,
        out_specs=(P("slot", "head"), P("slot", "head"), P("slot", "head")),
        check_vma=False,
    )
```

```python
import functools

import jax
import jax.numpy as jnp
from jax import lax
from jax.experimental import pallas as pl
from jax.experimental.pallas import tpu as pltpu
from jax.sharding import PartitionSpec as P

MESH = pl.DeviceIdType.MESH
F32 = jnp.float32
BF16 = jnp.bfloat16

HEADS = 48
HEAD = 128
TOK = 64
CACHE = 256
KEYS = TOK + CACHE
KVR = 2 * KEYS + 16
SHARE = 6
GW = SHARE * HEAD
MW = GW + HEAD
HALF = TOK // 2
PAIR = 2 * SHARE * TOK
SPAN = 4 * KEYS
TILE = 256
C = HEAD ** -0.5 * 1.4426950408889634
NEG = -1e30
NZ, NX = 8, 4
Z_ORDER = (0, 1, 7, 2, 6, 3, 5, 4)
G0_PAIRS = ((1, 7), (2, 6), (3, 5), (4, 0))
G1_PAIRS = ((7, 4), (5, 6), (1, 2), (3, 0))
UNITS = (
    (0, 0, 0), (0, 0, 1), (0, 0, 2), (1, 0, 2),
    (1, 0, 3), (0, 0, 3), (0, 1, 3), (1, 0, 0),
    (1, 1, 0), (0, 1, 2), (1, 0, 1), (1, 1, 1),
    (0, 1, 1), (1, 1, 2), (0, 1, 0), (1, 1, 3),
)
PLAN = (
    "zq0T", "xkown_x", "xkown_y", "rt", "clear_l", "zq0F", "clear_acc", "zk0T", "xqown_x", "xqown_y",
    "zq1T", "zk0F", "zq1F", "xkfwd", "xky12", "xkyx", "S", "zk1T", "P", "xqfwd",
    "xqy12", "xqyx", "zq2T", "zq2F", "S", "zk1F", "P", "zk2T", "zq3T", "xky3",
    "xkyf", "S", "xqyf", "xqy3", "P", "zk2F", "S", "PS", "zk3T", "PS",
    "PS", "PS", "o0T", "PS", "far", "PS", "y7", "xx1", "PS", "o1T",
    "o1F", "PS", "PS", "x1", "y56", "xx2", "PS", "o2T", "o2F", "PS",
    "PS", "x2", "P", "yf", "o3T", "o3F", "y3",
)
MSG = {}
for _name, _rows in (
    ("y7", 32), ("y5", 32), ("y6", 32), ("y3", 32), ("x1u", 32), ("x1d", 32), ("xx1u", 16), ("xx1d", 16),
    ("x2u0", 32), ("x2u1", 32), ("x2d0", 32), ("x2d1", 32), ("xx2u", 32), ("xx2d", 32), ("yf", 32),
):
    MSG[_name] = (len(MSG), sum(r for _, _, r in MSG.values()), _rows)
MSG_ROWS = sum(r for _, _, r in MSG.values())


def kernel(
    q_hbm, k_hbm, v_hbm, ck_hbm, cv_hbm, count_hbm, section_hbm,
    o_hbm, total_ref, fresh_ref,
    qg, kv, bias, acc, l_st, m_st, s0, s1, mx0, mx1, al0, al1,
    sb0, mb0, sb1, mb1, rt_s, rt_y, rz_s, rz_r, sq_p, sq_s, sq_r, o_ref, count_ref, section_ref, in_sem, out_sem,
    sent, zq_recv, zk_recv, xk_recv, xq_recv, r_recv, o_recv, p_recv, h_recv,
):
    slot = lax.axis_index("slot")
    head = lax.axis_index("head")
    y = slot // 32
    z = slot // 4 % 8
    x = slot % 4
    zhi = z // 4

    def at(y_, z_, x_):
        return (y_ * 32 + z_ * 4 + x_, head)

    z_dev = (at(y, (z + 1) % NZ, x), at(y, (z + 7) % NZ, x))
    x_dev = (at(y, z, (x + 1) % NX), at(y, z, (x + 3) % NX))
    y_dev = at(1 - y, z, x)
    far_dev = at(y, (z + 4) % NZ, x)
    pair_core = 1 - head % 2
    head_dev = ((slot, head // 2 * 2 + pair_core), (slot, (head + 2) % 4), (slot, (head + 2) % 4 // 2 * 2 + pair_core))

    barrier = pltpu.get_barrier_semaphore()
    peers = z_dev + x_dev + (y_dev,) + head_dev
    for peer in peers:
        pl.semaphore_signal(barrier, inc=1, device_id=peer, device_id_type=MESH)

    loads = []
    for g in (0, 1):
        cols = slice(g * HEAD, (g + 1) * HEAD)
        loads += [
            (q_hbm.at[:, g * GW:(g + 1) * GW], qg.at[g, 0]),
            (k_hbm.at[:, cols], kv.at[2 * g, 0, 0:TOK]),
            (ck_hbm.at[:, cols], kv.at[2 * g, 0, TOK:KEYS]),
            (v_hbm.at[:, cols], kv.at[2 * g, 0, KEYS:KEYS + TOK]),
            (cv_hbm.at[:, cols], kv.at[2 * g, 0, KEYS + TOK:2 * KEYS]),
        ]
    scalars = [(count_hbm, count_ref), (section_hbm, section_ref)]
    loads = [pltpu.make_async_copy(a, b, in_sem.at[i]) for i, (a, b) in enumerate(scalars + loads)]
    for copy in loads:
        copy.start()
    loads[0].wait()
    for g in (0, 1):
        kv[2 * g, 0, 2 * KEYS:KVR] = jnp.full((16, HEAD), count_ref[0].astype(F32), F32).astype(BF16)
    for copy in loads[1:]:
        copy.wait()

    def tokens(kind, group):
        rows = pl.ds(pl.multiple_of(kind * KEYS + group * 16, 16), 16)
        return jnp.concatenate([kv[0, 0, rows], kv[2, 0, rows]], 1)

    for i, group in enumerate(((1 - y) * 2 + zhi, (1 - y) * 2 + 1 - zhi)):
        rt_s[32 * i:32 * i + 16] = tokens(0, group)
        rt_s[32 * i + 16:32 * i + 32] = tokens(1, group)
    pl.semaphore_wait(barrier, len(peers))

    def remote(src, dst, send, recv, dev):
        return pltpu.make_async_remote_copy(
            src_ref=src, dst_ref=dst, send_sem=send, recv_sem=recv, device_id=dev, device_id_type=MESH
        )

    def zq_view(e, p):
        return qg.at[0, e, p * HALF:(p + 1) * HALF]

    def zk_view(e, p):
        spot = Z_ORDER.index(e)
        rows = slice(0, KEYS) if p == 0 else slice(KEYS, KVR)
        return kv.at[2 + spot // 4, spot % 4, rows]

    def z_copy(kind, d, step, p):
        view, send, recv = ((zq_view, sent.at[0], zq_recv), (zk_view, sent.at[1], zk_recv))[kind]
        src = (-step if d == 0 else step) % NZ
        dst = (-step - 1 if d == 0 else step + 1) % NZ
        return remote(view(src, p), view(dst, p), send, recv.at[d, step, p], z_dev[d])

    def xy_copies(view, cut, quarter, end, send, recv):
        table = {
            "own_up": (0, 1, 0, end, x_dev[0]),
            "own_down": (0, 2, 0, end, x_dev[1]),
            "own_y": (0, 3, 0, end, y_dev),
            "fwd_up": (1, 4, 0, cut, x_dev[0]),
            "fwd_down": (2, 4, cut, end, x_dev[1]),
            "y_up": (3, 5, 0, cut, x_dev[0]),
            "y_down": (3, 6, 0, cut, x_dev[1]),
            "yf_up": (5, 7, 0, quarter, x_dev[0]),
            "yf_down": (6, 7, quarter, cut, x_dev[1]),
            "y_1": (1, 5, cut, end, y_dev),
            "y_2": (2, 6, cut, end, y_dev),
            "y_3": (4, 7, cut, end, y_dev),
        }
        return {
            n: remote(view(s, a, b), view(t, a, b), send, recv.at[i], dev)
            for i, (n, (s, t, a, b, dev)) in enumerate(table.items())
        }

    xk = xy_copies(lambda s, a, b: kv.at[s // 4, s % 4, a:b], KEYS, KEYS // 2, KVR, sent.at[2], xk_recv)
    xq = xy_copies(lambda s, a, b: qg.at[1, s, a:b], HALF, HALF // 2, TOK, sent.at[3], xq_recv)

    XY = {
        "own_x": ("own_up", "own_down"), "own_y": ("own_y",), "fwd": ("fwd_up", "fwd_down"), "y12": ("y_1", "y_2"),
        "yx": ("y_up", "y_down"), "yf": ("yf_up", "yf_down"), "y3": ("y_3",),
    }
    XY_NEEDS = {"fwd": "own_x", "y12": "own_x", "yx": "own_y", "yf": "yx", "y3": "fwd"}
    TREE = {
        "y7": ("y7",), "xx1": ("xx1u", "xx1d"), "x1": ("x1u", "x1d"), "y56": ("y5", "y6"), "xx2": ("xx2u", "xx2d"),
        "x2": ("x2u0", "x2u1", "x2d0", "x2d1"), "yf": ("yf",), "y3": ("y3",),
    }

    def copies(name):
        kind, rest = name[:2], name[2:]
        if kind in ("zq", "zk"):
            return [z_copy(kind == "zk", d, int(rest[0]), d if rest[1] == "T" else 1 - d) for d in (0, 1)]
        if kind in ("xk", "xq"):
            return [(xk if kind == "xk" else xq)[n] for n in XY[rest]]
        if name[0] == "o":
            return [o_copy(d, int(name[1]), d if name[2] == "T" else 1 - d) for d in (0, 1)]
        return [p_copy(n) for n in TREE[name]]

    have = set()

    def need(*names):
        for name in names:
            if name not in have:
                have.add(name)
                for copy in copies(name):
                    copy.wait_recv()

    def begin(name):
        kind, rest = name[:2], name[2:]
        if kind in ("zq", "zk"):
            if rest[0] != "0":
                need(kind + str(int(rest[0]) - 1) + rest[1])
        elif rest in XY_NEEDS:
            need(kind + XY_NEEDS[rest])
        for copy in copies(name):
            copy.start()

    rt_copy = remote(rt_s, rt_y, sent.at[4], r_recv.at[0], y_dev)
    rz_copy = remote(rz_s, rz_r, sent.at[5], r_recv.at[1], far_dev)

    def far_retire():
        group = y * 2 + 1 - zhi
        rz_s[0:16] = tokens(0, group)
        rz_s[16:32] = tokens(1, group)
        rt_copy.wait_recv()
        rz_s[32:64] = rt_y[32:64]
        rz_copy.start()

    lane = lax.broadcasted_iota(jnp.int32, (1, SPAN), 1)

    def make_bias(ph):
        for sel in (0, 1):
            if ph < 2:
                mine = section_ref[y * 2 + sel]
            else:
                mine = section_ref[(y + sel) % 2 * 2 + zhi]
            total = jnp.zeros((1, SPAN), F32)
            for s in range(4):
                if ph < 2:
                    block = ph * 4 + s
                    key_group = (y if block in (0, 1, 2, 4) else 1 - y) * 2 + zhi
                else:
                    key_group = y * 2 + (z + Z_ORDER[(ph - 2) * 4 + s]) % NZ // 4
                seen = section_ref[key_group] <= mine
                tok = jnp.where(seen, 0.0, NEG).astype(F32)
                live = kv[ph, s, 2 * KEYS:KVR, :].astype(F32)[0:1, 0:1]
                row = lane - s * KEYS
                dead = jnp.where((row - TOK).astype(F32) >= live, NEG, 0.0)
                here = (row >= 0) & (row < KEYS)
                total = jnp.where(here, jnp.where(row < TOK, tok, dead), total)
            bias[ph, sel] = total

    def unit(u):
        g, half, j = UNITS[u]
        if g == 0:
            c1, c2 = G0_PAIRS[j]
            sel = lambda c: (z + c) % NZ // 4
        else:
            c1, c2 = G1_PAIRS[j]
            sel = lambda c: 1 if c in (3, 5, 6, 7) else 0
        return 2 * g + half, g, c1, c2, sel(c1), sel(c2)

    scores, tops, alphas = (s0, s1), (mx0, mx1), (al0, al1)
    ones = jnp.ones((TILE, HEAD), BF16)

    def key_tile(ph, t, base):
        parts, a = [], t * TILE
        while a < (t + 1) * TILE:
            s = a // KEYS
            b = min((t + 1) * TILE, (s + 1) * KEYS)
            parts.append(kv[ph, s, base + a - s * KEYS:base + b - s * KEYS])
            a = b
        return jnp.concatenate(parts, 0) if len(parts) > 1 else parts[0]

    def stacked(ref, g, c1, c2):
        return jnp.concatenate([ref[g, c, :, h * HEAD:(h + 1) * HEAD] for c in (c1, c2) for h in range(SHARE)], 0)

    def unstack(ref, g, c1, c2, value):
        for i, c in enumerate((c1, c2)):
            for h in range(SHARE):
                r = (i * SHARE + h) * TOK
                ref[g, c, :, h * HEAD:(h + 1) * HEAD] = value[r:r + TOK]

    def score_tile(ctx, buf, t, top):
        (ph, g, c1, c2, b1, b2), q = ctx
        s = lax.dot_general(q, key_tile(ph, t, 0), (((1,), (1,)), ((), ())), preferred_element_type=F32)
        cols = slice(t * TILE, (t + 1) * TILE)
        s = jnp.concatenate(
            [s[:PAIR // 2] + bias[ph, b1, :, cols], s[PAIR // 2:] + bias[ph, b2, :, cols]], 0
        )
        scores[buf][:, cols] = s
        t2 = jnp.maximum(s[:, :HEAD], s[:, HEAD:])
        return t2 if top is None else jnp.maximum(top, t2)

    def score_begin(u):
        info = unit(u)
        return info, stacked(qg, info[1], info[2], info[3])

    def score_end(ctx, buf, top):
        _, g, c1, c2, _, _ = ctx[0]
        new = jnp.broadcast_to(jnp.max(top, axis=1, keepdims=True), (PAIR, HEAD))
        if ctx[0][0] % 2:
            old = stacked(m_st, g, c1, c2)
            new = jnp.maximum(old, new)
            alphas[buf][...] = jnp.exp2((old - new) * C)
        tops[buf][...] = new
        unstack(m_st, g, c1, c2, new)

    def score_alone(u):
        ctx = score_begin(u)
        top = None
        for t in range(SPAN // TILE):
            top = score_tile(ctx, u % 2, t, top)
        score_end(ctx, u % 2, top)

    def step(u, buf, ahead):
        ph, g, c1, c2, _, _ = unit(u)
        if ahead:
            ctx = score_begin(u + 1)
        top = None
        new_top = tops[buf][...]
        total = None
        for t in range(SPAN // TILE):
            if ahead:
                top = score_tile(ctx, 1 - buf, t, top)
            s = scores[buf][:, t * TILE:(t + 1) * TILE]
            weight = jnp.concatenate(
                [jnp.exp2((s[:, :HEAD] - new_top) * C), jnp.exp2((s[:, HEAD:] - new_top) * C)], 1
            ).astype(BF16)
            v = jnp.concatenate([key_tile(ph, t, KEYS), ones], 1)
            mixed = jnp.dot(weight, v, preferred_element_type=F32)
            total = mixed if total is None else total + mixed
        fresh_acc, fresh_sum = total[:, :HEAD], total[:, HEAD:]
        if ph % 2:
            alpha = alphas[buf][...]
            fresh_acc = stacked(acc, g, c1, c2) * alpha + fresh_acc
            fresh_sum = stacked(l_st, g, c1, c2) * alpha + fresh_sum
        unstack(acc, g, c1, c2, fresh_acc)
        unstack(l_st, g, c1, c2, fresh_sum)
        if ahead:
            score_end(ctx, 1 - buf, top)

    def gather_piece(g, c, r0, n, messages):
        rows = slice(r0, r0 + n)
        lanes = lax.broadcasted_iota(jnp.int32, (n, HEAD), 1)
        sums = jnp.ones((n, HEAD), F32)
        peak = jnp.zeros((n, HEAD), F32)
        for h in range(SHARE):
            cols = slice(h * HEAD, (h + 1) * HEAD)
            sums = jnp.where(lanes % 16 == h, l_st[g, c, rows, cols], sums)
            peak = jnp.where(lanes % 16 == h, m_st[g, c, rows, cols], peak)
        logs = [peak * C + jnp.log2(sums)]
        for ref, a in messages:
            p = ref[a:a + n, GW:MW].astype(F32)
            logs.append(p + pltpu.roll(p, 16, 1) + pltpu.roll(p, 32, 1) + pltpu.roll(p, 48, 1))
        top = functools.reduce(jnp.maximum, logs)
        weights = [jnp.exp2(item - top) for item in logs]
        total = functools.reduce(jnp.add, weights)
        share = 1.0 / total
        factors = [w * share for w in weights]
        factors[0] = factors[0] / sums
        out = []
        for h in range(SHARE):
            cols = slice(h * HEAD, (h + 1) * HEAD)
            spread = [jnp.broadcast_to(f[:, h:h + 1], (n, HEAD)) for f in factors]
            o = acc[g, c, rows, cols] * spread[0]
            for (ref, a), f in zip(messages, spread[1:]):
                o = o + ref[a:a + n, cols].astype(F32) * f
            out.append(o)
        return out, top + jnp.log2(total)

    def write_piece(dst, a, n, out, logs):
        for h in range(SHARE):
            dst[a:a + n, h * HEAD:(h + 1) * HEAD] = out[h].astype(BF16)
        lanes = lax.broadcasted_iota(jnp.int32, (n, HEAD), 1) // 16 % 4
        first = logs.astype(BF16).astype(F32)
        rest = logs - first
        second = rest.astype(BF16).astype(F32)
        third = rest - second
        parts = jnp.where(lanes == 0, first, jnp.where(lanes == 1, second, jnp.where(lanes == 2, third, 0.0)))
        dst[a:a + n, GW:MW] = parts.astype(BF16)

    def o_copy(d, hop, p):
        rows = slice(p * HALF, (p + 1) * HALF)
        return remote(
            sb0.at[d, hop, rows], mb0.at[d, hop, rows], sent.at[6], o_recv.at[d, hop, p], z_dev[d]
        )

    def ring(hop, first):
        todo = []
        for d in (0, 1):
            p = d if first else 1 - d
            messages = []
            if hop > 1 or (hop == 1 and first):
                need(f"o{hop - 1}{'T' if first else 'F'}")
                messages = [(mb0.at[d, hop - 1], p * HALF)]
            todo.append((d, p, (4 - hop) if d == 0 else (4 + hop), messages))
        pieces = [gather_piece(0, c, p * HALF, HALF, messages) for d, p, c, messages in todo]
        for (d, p, _, _), piece in zip(todo, pieces):
            write_piece(sb0.at[d, hop], p * HALF, HALF, *piece)
        for d, p, _, _ in todo:
            o_copy(d, hop, p).start()

    def p_copy(name):
        i, a, n = MSG[name]
        dev = y_dev if name[0] == "y" else x_dev[0 if "u" in name else 1]
        return remote(sb1.at[a:a + n], mb1.at[a:a + n], sent.at[7], p_recv.at[i], dev)

    def arrived(name, skip=0):
        return (mb1, MSG[name][1] + skip)

    def tree(name, c, r0, n, *needs):
        _, a, _ = MSG[name]
        write_piece(sb1, a, n, *gather_piece(1, c, r0, n, [arrived(*need) for need in needs]))
        p_copy(name).start()

    def split(name, c, parts):
        _, a, _ = MSG[name]
        for r0, needs in parts:
            write_piece(sb1, a + r0, 16, *gather_piece(1, c, r0, 16, needs))
        p_copy(name).start()

    def tree_y7():
        tree("y7", 7, 32, 32)

    def tree_xx1():
        tree("xx1u", 7, 0, 16)
        tree("xx1d", 7, 16, 16)

    def tree_x1():
        tree("x1u", 4, 0, 32)
        need("y7")
        tree("x1d", 4, 32, 32, ("y7",))

    def tree_y56():
        tree("y5", 5, 32, 32)
        tree("y6", 6, 32, 32)

    def tree_xx2():
        need("xx1")
        split("xx2u", 6, ((0, [arrived("xx1u")]), (16, [])))
        split("xx2d", 5, ((0, []), (16, [arrived("xx1d")])))

    def tree_x2():
        need("x1", "y56")
        tree("x2u0", 2, 0, 32, ("x1u",))
        tree("x2u1", 2, 32, 32, ("y6",))
        tree("x2d0", 1, 0, 32)
        tree("x2d1", 1, 32, 32, ("y5",), ("x1d",))

    def tree_yf():
        need("xx2")
        tree("yf", 3, 0, 32, ("xx2u",), ("xx2d",))

    def tree_y3():
        tree("y3", 3, 32, 32)

    trees = {
        "y7": tree_y7, "xx1": tree_xx1, "x1": tree_x1, "y56": tree_y56, "xx2": tree_xx2, "x2": tree_x2, "yf": tree_yf,
        "y3": tree_y3,
    }

    def finish(g, p, messages):
        out, _ = gather_piece(g, 0, p * HALF, HALF, messages)
        squares = jnp.zeros((HALF, HEAD), F32)
        for h in range(SHARE):
            o_ref[p * HALF:(p + 1) * HALF, g * GW + h * HEAD:g * GW + (h + 1) * HEAD] = out[h]
            squares = squares + out[h] * out[h]
        rows = slice(p * HALF, (p + 1) * HALF)
        if g == 0:
            sq_p[rows, :] = squares
        else:
            total = jnp.sum(squares + sq_p[rows, :], axis=1, keepdims=True)
            sq_p[rows, :] = jnp.broadcast_to(total, (HALF, HEAD))

    def o_out(g):
        cols = slice(g * GW, (g + 1) * GW)
        return pltpu.make_async_copy(o_ref.at[:, cols], o_hbm.at[:, cols], out_sem.at[g])

    def finish0():
        need("o3T", "o3F")
        for p in (0, 1):
            finish(0, p, [(mb0.at[d, 3], p * HALF) for d in (0, 1)])

    def retire():
        rz_copy.wait_recv()
        group = y * 2 + zhi
        for i in (0, 1):
            got = jnp.where(section_ref[group] == 0, tokens(i, group).astype(F32), 0.0)
            for source, ref, a in (
                ((1 - y) * 2 + zhi, rt_y, 0),
                (y * 2 + 1 - zhi, rz_r, 0),
                ((1 - y) * 2 + 1 - zhi, rz_r, 32),
            ):
                got = jnp.where(section_ref[source] == 0, ref[a + 16 * i:a + 16 * i + 16].astype(F32), got)
            fresh_ref[i] = got.astype(BF16)

    ready = set()

    def unit_needs(u):
        g, half, j = UNITS[u]
        if g == 0:
            need(*[f"zq{k}{p}" for k in range(j + 1) for p in "TF" if k < 3 or p == "T"])
            need("xkown_x", "xkown_y")
            if half:
                need("xkfwd", "xky12", "xkyx", "xkyf", "xky3")
        else:
            need("xqown_x", "xqown_y")
            if j < 2:
                need("xqfwd", "xqy12", "xqyx", "xqyf", "xqy3")
            need(*[f"zk{k}{p}" for k in range(4 if half else 2) for p in "TF" if k < 3 or p == "T"])
        if 2 * g + half not in ready:
            ready.add(2 * g + half)
            make_bias(2 * g + half)

    scored = done = 0
    for op in PLAN:
        if op == "S":
            unit_needs(scored)
            score_alone(scored)
            scored += 1
        elif op == "P":
            step(done, done % 2, False)
            done += 1
        elif op == "PS":
            unit_needs(scored)
            step(done, done % 2, True)
            scored += 1
            done += 1
        elif op == "clear_l":
            l_st[...] = jnp.zeros(l_st.shape, F32)
        elif op == "clear_acc":
            acc[...] = jnp.zeros(acc.shape, F32)
        elif op == "rt":
            rt_copy.start()
        elif op == "far":
            need("zq3T")
            far_retire()
        elif op in trees:
            trees[op]()
        elif op[0] == "o":
            ring(int(op[1]), op[2] == "T")
        else:
            begin(op)
    finish0()
    o_out(0).start()
    retire()
    need("x2", "y3", "yf")
    for p in (0, 1):
        finish(1, p, [arrived(f"x2u{p}"), arrived(f"x2d{p}"), arrived("yf" if p == 0 else "y3")])
    o_out(1).start()
    rows = jnp.concatenate([sq_p[...], jnp.zeros((HEAD - TOK, HEAD), F32)], 0)
    sq_s[...] = rows.T[0:8]
    sc = [remote(sq_s, sq_r.at[i], sent.at[8], h_recv.at[i], head_dev[i]) for i in range(3)]
    for copy in sc:
        copy.start()
    total = sq_s[...]
    for i, copy in enumerate(sc):
        copy.wait_recv()
        total = total + sq_r[i]
    total_ref[...] = total
    for g in (0, 1):
        o_out(g).wait()

    for i, refs in enumerate((
        (qg.at[0, 0:7],),
        (kv.at[0], kv.at[1, 0:3]),
        (kv.at[0], kv.at[1, 0:3]),
        (qg.at[0, 0:7],),
        (rt_s,),
        (rz_s,),
        (sb0.at[0], sb0.at[1, 0:3]),
        (sb1,),
        (sq_r,),
    )):
        for ref in refs:
            pltpu.make_async_copy(ref, ref, sent.at[i]).wait()


def finish_kernel(count_ref, o_ref, total_ref, gain_ref, ck_ref, cv_ref, fresh_ref, out_ref, nck_ref, ncv_ref):
    total = jnp.concatenate([total_ref[...]] * 16, 0).T[0:TOK]
    scale = lax.rsqrt(total / (HEADS * HEAD) + 1e-06)
    for h in range(2 * SHARE):
        cols = slice(h * HEAD, (h + 1) * HEAD)
        out_ref[:, cols] = o_ref[:, cols] * scale * gain_ref[cols].reshape(1, HEAD)
    spot = lax.broadcasted_iota(jnp.int32, (CACHE, 16), 0) - lax.broadcasted_iota(jnp.int32, (CACHE, 16), 1)
    chosen = jnp.where(spot == count_ref[0], 1.0, 0.0).astype(BF16)
    row = lax.broadcasted_iota(jnp.int32, (CACHE, 256), 0) - count_ref[0]
    fresh = (row >= 0) & (row < 16)
    for i, (old, new) in enumerate(((ck_ref, nck_ref), (cv_ref, ncv_ref))):
        moved = jnp.dot(chosen, fresh_ref[i], preferred_element_type=F32)
        new[...] = jnp.where(fresh, moved, old[...].astype(F32)).astype(BF16)


def on_device(queries, keys, values, cache_keys, cache_values, cache_count, span_section, norm_gain):
    vmem = pl.BlockSpec(memory_space=pltpu.VMEM)
    smem = pl.BlockSpec(memory_space=pltpu.SMEM)
    hbm = pl.BlockSpec(memory_space=pl.ANY)
    dma = pltpu.SemaphoreType.DMA
    state = pltpu.VMEM((2, NZ, TOK, GW), F32)
    o, total, fresh = pl.pallas_call(
        kernel,
        out_shape=[
            jax.ShapeDtypeStruct((TOK, 2 * GW), F32),
            jax.ShapeDtypeStruct((8, HEAD), F32),
            jax.ShapeDtypeStruct((2, 16, 256), BF16),
        ],
        in_specs=[hbm] * 7,
        out_specs=[hbm, vmem, vmem],
        scratch_shapes=[
            pltpu.VMEM((2, NZ, TOK, GW), BF16),
            pltpu.VMEM((4, 4, KVR, HEAD), BF16),
            pltpu.VMEM((4, 2, 1, SPAN), F32),
            state, state, state,
            pltpu.VMEM((PAIR, SPAN), F32), pltpu.VMEM((PAIR, SPAN), F32),
            pltpu.VMEM((PAIR, HEAD), F32), pltpu.VMEM((PAIR, HEAD), F32),
            pltpu.VMEM((PAIR, HEAD), F32), pltpu.VMEM((PAIR, HEAD), F32),
            pltpu.VMEM((2, 4, TOK, MW), BF16), pltpu.VMEM((2, 4, TOK, MW), BF16),
            pltpu.VMEM((MSG_ROWS, MW), BF16), pltpu.VMEM((MSG_ROWS, MW), BF16),
            pltpu.VMEM((64, 256), BF16), pltpu.VMEM((64, 256), BF16),
            pltpu.VMEM((64, 256), BF16), pltpu.VMEM((64, 256), BF16),
            pltpu.VMEM((TOK, HEAD), F32),
            pltpu.VMEM((8, HEAD), F32),
            pltpu.VMEM((3, 8, HEAD), F32),
            pltpu.VMEM((TOK, 2 * GW), F32),
            pltpu.SMEM((1,), jnp.int32),
            pltpu.SMEM((4,), jnp.int32),
            dma((12,)), dma((2,)),
            dma((9,)), dma((2, 4, 2)), dma((2, 4, 2)), dma((12,)), dma((12,)), dma((2,)), dma((2, 4, 2)), dma((len(MSG),)),
            dma((3,)),
        ],
        compiler_params=pltpu.CompilerParams(
            collective_id=0, has_side_effects=True, vmem_limit_bytes=56 * 2**20
        ),
    )(queries, keys, values, cache_keys, cache_values, cache_count, span_section)
    return pl.pallas_call(
        finish_kernel,
        out_shape=[
            jax.ShapeDtypeStruct((TOK, 2 * GW), F32),
            jax.ShapeDtypeStruct((CACHE, 256), BF16),
            jax.ShapeDtypeStruct((CACHE, 256), BF16),
        ],
        in_specs=[smem] + [vmem] * 6,
        out_specs=[vmem] * 3,
        compiler_params=pltpu.CompilerParams(vmem_limit_bytes=56 * 2**20),
    )(cache_count, o, total, norm_gain, cache_keys, cache_values, fresh)


def solution(mesh):
    placed = (
        P("slot", "head"),
        P("slot", "head"),
        P("slot", "head"),
        P("slot", "head"),
        P("slot", "head"),
        P("slot"),
        P(),
        P("head"),
    )
    return jax.shard_map(
        on_device,
        mesh=mesh,
        in_specs=placed,
        out_specs=(P("slot", "head"), P("slot", "head"), P("slot", "head")),
        check_vma=False,
    )
```

```python
import functools

import jax
import jax.numpy as jnp
from jax import lax
from jax.experimental import pallas as pl
from jax.experimental.pallas import tpu as pltpu
from jax.sharding import PartitionSpec as P

MESH = pl.DeviceIdType.MESH
F32 = jnp.float32
BF16 = jnp.bfloat16

HEADS = 48
HEAD = 128
TOK = 64
CACHE = 256
KEYS = TOK + CACHE
KVR = 2 * KEYS + 16
SHARE = 6
GW = SHARE * HEAD
MW = GW + HEAD
HALF = TOK // 2
PAIR = 2 * SHARE * TOK
SPAN = 4 * KEYS
TILE = 256
C = HEAD ** -0.5 * 1.4426950408889634
NEG = -1e30
NZ, NX = 8, 4
Z_ORDER = (0, 1, 7, 2, 6, 3, 5, 4)
G0_PAIRS = ((1, 7), (2, 6), (3, 5), (4, 0))
G1_PAIRS = ((7, 4), (5, 6), (1, 2), (3, 0))
UNITS = (
    (0, 0, 1), (0, 0, 0), (0, 0, 2), (1, 0, 3),
    (1, 0, 2), (0, 0, 3), (0, 1, 3), (1, 0, 0),
    (1, 1, 0), (0, 1, 2), (1, 0, 1), (1, 1, 1),
    (0, 1, 1), (1, 1, 2), (0, 1, 0), (1, 1, 3),
)
PLAN = (
    "zq0T", "xkown_x", "xkown_y", "rt", "clear_l", "zq0F", "clear_acc", "zk0T", "xqown_x", "xqown_y",
    "zq1T", "zk0F", "zq1F", "xkfwd", "xky12", "xkyx", "zk1T", "xqfwd", "xqy12", "xqyx",
    "zq2T", "zq2F", "S", "zk1F", "PS", "zk2T", "P", "xky3", "zq3T", "xkyf",
    "xqy3", "xqyf", "S", "P", "zk2F", "S", "PS", "zk3T", "PS", "PS",
    "PS", "o0T", "PS", "far", "PS", "y7", "xx1", "PS", "o1T", "o1F",
    "PS", "PS", "x1", "y56", "xx2", "PS", "o2T", "o2F", "PS", "PS",
    "x2", "P", "yf", "y3", "o3T", "o3F",
)
MSG = {}
for _name, _rows in (
    ("y7", 32), ("y5", 32), ("y6", 32), ("y3", 32), ("x1u", 32), ("x1d", 32), ("xx1u", 16), ("xx1d", 16),
    ("x2u0", 32), ("x2u1", 32), ("x2d0", 32), ("x2d1", 32), ("xx2u", 32), ("xx2d", 32), ("yf", 32),
):
    MSG[_name] = (len(MSG), sum(r for _, _, r in MSG.values()), _rows)
MSG_ROWS = sum(r for _, _, r in MSG.values())


def kernel(
    q_hbm, k_hbm, v_hbm, ck_hbm, cv_hbm, count_hbm, section_hbm,
    o_hbm, total_ref, fresh_ref,
    qg, kv, bias, acc, l_st, m_st, s0, s1, mx0, mx1, al0, al1,
    sb0, mb0, sb1, mb1, rt_s, rt_y, rz_s, rz_r, sq_p, sq_s, sq_r, o_ref, count_ref, section_ref, in_sem, out_sem,
    sent, zq_recv, zk_recv, xk_recv, xq_recv, r_recv, o_recv, p_recv, h_recv,
):
    slot = lax.axis_index("slot")
    head = lax.axis_index("head")
    y = slot // 32
    z = slot // 4 % 8
    x = slot % 4
    zhi = z // 4

    def at(y_, z_, x_):
        return (y_ * 32 + z_ * 4 + x_, head)

    z_dev = (at(y, (z + 1) % NZ, x), at(y, (z + 7) % NZ, x))
    x_dev = (at(y, z, (x + 1) % NX), at(y, z, (x + 3) % NX))
    y_dev = at(1 - y, z, x)
    far_dev = at(y, (z + 4) % NZ, x)
    pair_core = 1 - head % 2
    head_dev = ((slot, head // 2 * 2 + pair_core), (slot, (head + 2) % 4), (slot, (head + 2) % 4 // 2 * 2 + pair_core))

    barrier = pltpu.get_barrier_semaphore()
    peers = z_dev + x_dev + (y_dev,) + head_dev
    for peer in peers:
        pl.semaphore_signal(barrier, inc=1, device_id=peer, device_id_type=MESH)

    loads = []
    for g in (0, 1):
        cols = slice(g * HEAD, (g + 1) * HEAD)
        loads += [
            (q_hbm.at[:, g * GW:(g + 1) * GW], qg.at[g, 0]),
            (k_hbm.at[:, cols], kv.at[2 * g, 0, 0:TOK]),
            (ck_hbm.at[:, cols], kv.at[2 * g, 0, TOK:KEYS]),
            (v_hbm.at[:, cols], kv.at[2 * g, 0, KEYS:KEYS + TOK]),
            (cv_hbm.at[:, cols], kv.at[2 * g, 0, KEYS + TOK:2 * KEYS]),
        ]
    scalars = [(count_hbm, count_ref), (section_hbm, section_ref)]
    loads = [pltpu.make_async_copy(a, b, in_sem.at[i]) for i, (a, b) in enumerate(scalars + loads)]
    for copy in loads:
        copy.start()
    loads[0].wait()
    for g in (0, 1):
        kv[2 * g, 0, 2 * KEYS:KVR] = jnp.full((16, HEAD), count_ref[0].astype(F32), F32).astype(BF16)
    for copy in loads[1:]:
        copy.wait()

    def tokens(kind, group):
        rows = pl.ds(pl.multiple_of(kind * KEYS + group * 16, 16), 16)
        return jnp.concatenate([kv[0, 0, rows], kv[2, 0, rows]], 1)

    for i, group in enumerate(((1 - y) * 2 + zhi, (1 - y) * 2 + 1 - zhi)):
        rt_s[32 * i:32 * i + 16] = tokens(0, group)
        rt_s[32 * i + 16:32 * i + 32] = tokens(1, group)
    pl.semaphore_wait(barrier, len(peers))

    def remote(src, dst, send, recv, dev):
        return pltpu.make_async_remote_copy(
            src_ref=src, dst_ref=dst, send_sem=send, recv_sem=recv, device_id=dev, device_id_type=MESH
        )

    def zq_view(e, p):
        return qg.at[0, e, p * HALF:(p + 1) * HALF]

    def zk_view(e, p):
        spot = Z_ORDER.index(e)
        rows = slice(0, KEYS) if p == 0 else slice(KEYS, KVR)
        return kv.at[2 + spot // 4, spot % 4, rows]

    def z_copy(kind, d, step, p):
        view, send, recv = ((zq_view, sent.at[0], zq_recv), (zk_view, sent.at[1], zk_recv))[kind]
        src = (-step if d == 0 else step) % NZ
        dst = (-step - 1 if d == 0 else step + 1) % NZ
        return remote(view(src, p), view(dst, p), send, recv.at[d, step, p], z_dev[d])

    def xy_copies(view, cut, quarter, end, send, recv):
        table = {
            "own_up": (0, 1, 0, end, x_dev[0]),
            "own_down": (0, 2, 0, end, x_dev[1]),
            "own_y": (0, 3, 0, end, y_dev),
            "fwd_up": (1, 4, 0, cut, x_dev[0]),
            "fwd_down": (2, 4, cut, end, x_dev[1]),
            "y_up": (3, 5, 0, cut, x_dev[0]),
            "y_down": (3, 6, 0, cut, x_dev[1]),
            "yf_up": (5, 7, 0, quarter, x_dev[0]),
            "yf_down": (6, 7, quarter, cut, x_dev[1]),
            "y_1": (1, 5, cut, end, y_dev),
            "y_2": (2, 6, cut, end, y_dev),
            "y_3": (4, 7, cut, end, y_dev),
        }
        return {
            n: remote(view(s, a, b), view(t, a, b), send, recv.at[i], dev)
            for i, (n, (s, t, a, b, dev)) in enumerate(table.items())
        }

    xk = xy_copies(lambda s, a, b: kv.at[s // 4, s % 4, a:b], KEYS, KEYS // 2, KVR, sent.at[2], xk_recv)
    xq = xy_copies(lambda s, a, b: qg.at[1, s, a:b], HALF, HALF // 2, TOK, sent.at[3], xq_recv)

    XY = {
        "own_x": ("own_up", "own_down"), "own_y": ("own_y",), "fwd": ("fwd_up", "fwd_down"), "y12": ("y_1", "y_2"),
        "yx": ("y_up", "y_down"), "yf": ("yf_up", "yf_down"), "y3": ("y_3",),
    }
    XY_NEEDS = {"fwd": "own_x", "y12": "own_x", "yx": "own_y", "yf": "yx", "y3": "fwd"}
    TREE = {
        "y7": ("y7",), "xx1": ("xx1u", "xx1d"), "x1": ("x1u", "x1d"), "y56": ("y5", "y6"), "xx2": ("xx2u", "xx2d"),
        "x2": ("x2u0", "x2u1", "x2d0", "x2d1"), "yf": ("yf",), "y3": ("y3",),
    }

    def copies(name):
        kind, rest = name[:2], name[2:]
        if kind in ("zq", "zk"):
            return [z_copy(kind == "zk", d, int(rest[0]), d if rest[1] == "T" else 1 - d) for d in (0, 1)]
        if kind in ("xk", "xq"):
            return [(xk if kind == "xk" else xq)[n] for n in XY[rest]]
        if name[0] == "o":
            return [o_copy(d, int(name[1]), d if name[2] == "T" else 1 - d) for d in (0, 1)]
        return [p_copy(n) for n in TREE[name]]

    have = set()

    def need(*names):
        for name in names:
            if name not in have:
                have.add(name)
                for copy in copies(name):
                    copy.wait_recv()

    def begin(name):
        kind, rest = name[:2], name[2:]
        if kind in ("zq", "zk"):
            if rest[0] != "0":
                need(kind + str(int(rest[0]) - 1) + rest[1])
        elif rest in XY_NEEDS:
            need(kind + XY_NEEDS[rest])
        for copy in copies(name):
            copy.start()

    rt_copy = remote(rt_s, rt_y, sent.at[4], r_recv.at[0], y_dev)
    rz_copy = remote(rz_s, rz_r, sent.at[5], r_recv.at[1], far_dev)

    def far_retire():
        group = y * 2 + 1 - zhi
        rz_s[0:16] = tokens(0, group)
        rz_s[16:32] = tokens(1, group)
        rt_copy.wait_recv()
        rz_s[32:64] = rt_y[32:64]
        rz_copy.start()

    lane = lax.broadcasted_iota(jnp.int32, (1, SPAN), 1)

    def make_bias(ph):
        for sel in (0, 1):
            if ph < 2:
                mine = section_ref[y * 2 + sel]
            else:
                mine = section_ref[(y + sel) % 2 * 2 + zhi]
            total = jnp.zeros((1, SPAN), F32)
            for s in range(4):
                if ph < 2:
                    block = ph * 4 + s
                    key_group = (y if block in (0, 1, 2, 4) else 1 - y) * 2 + zhi
                else:
                    key_group = y * 2 + (z + Z_ORDER[(ph - 2) * 4 + s]) % NZ // 4
                seen = section_ref[key_group] <= mine
                tok = jnp.where(seen, 0.0, NEG).astype(F32)
                live = kv[ph, s, 2 * KEYS:KVR, :].astype(F32)[0:1, 0:1]
                row = lane - s * KEYS
                dead = jnp.where((row - TOK).astype(F32) >= live, NEG, 0.0)
                here = (row >= 0) & (row < KEYS)
                total = jnp.where(here, jnp.where(row < TOK, tok, dead), total)
            bias[ph, sel] = total

    def unit(u):
        g, half, j = UNITS[u]
        if g == 0:
            c1, c2 = G0_PAIRS[j]
            sel = lambda c: (z + c) % NZ // 4
        else:
            c1, c2 = G1_PAIRS[j]
            sel = lambda c: 1 if c in (3, 5, 6, 7) else 0
        return 2 * g + half, g, c1, c2, sel(c1), sel(c2)

    scores, tops, alphas = (s0, s1), (mx0, mx1), (al0, al1)
    ones = jnp.ones((TILE, HEAD), BF16)

    def key_tile(ph, t, base):
        parts, a = [], t * TILE
        while a < (t + 1) * TILE:
            s = a // KEYS
            b = min((t + 1) * TILE, (s + 1) * KEYS)
            parts.append(kv[ph, s, base + a - s * KEYS:base + b - s * KEYS])
            a = b
        return jnp.concatenate(parts, 0) if len(parts) > 1 else parts[0]

    def stacked(ref, g, c1, c2):
        return jnp.concatenate([ref[g, c, :, h * HEAD:(h + 1) * HEAD] for c in (c1, c2) for h in range(SHARE)], 0)

    def unstack(ref, g, c1, c2, value):
        for i, c in enumerate((c1, c2)):
            for h in range(SHARE):
                r = (i * SHARE + h) * TOK
                ref[g, c, :, h * HEAD:(h + 1) * HEAD] = value[r:r + TOK]

    def score_tile(ctx, buf, t, top):
        (ph, g, c1, c2, b1, b2), q = ctx
        s = lax.dot_general(q, key_tile(ph, t, 0), (((1,), (1,)), ((), ())), preferred_element_type=F32)
        cols = slice(t * TILE, (t + 1) * TILE)
        s = jnp.concatenate(
            [s[:PAIR // 2] + bias[ph, b1, :, cols], s[PAIR // 2:] + bias[ph, b2, :, cols]], 0
        )
        scores[buf][:, cols] = s
        t2 = jnp.maximum(s[:, :HEAD], s[:, HEAD:])
        return t2 if top is None else jnp.maximum(top, t2)

    def score_begin(u):
        info = unit(u)
        return info, stacked(qg, info[1], info[2], info[3])

    def score_end(ctx, buf, top):
        _, g, c1, c2, _, _ = ctx[0]
        new = jnp.broadcast_to(jnp.max(top, axis=1, keepdims=True), (PAIR, HEAD))
        if ctx[0][0] % 2:
            old = stacked(m_st, g, c1, c2)
            new = jnp.maximum(old, new)
            alphas[buf][...] = jnp.exp2((old - new) * C)
        tops[buf][...] = new
        unstack(m_st, g, c1, c2, new)

    def score_alone(u):
        ctx = score_begin(u)
        top = None
        for t in range(SPAN // TILE):
            top = score_tile(ctx, u % 2, t, top)
        score_end(ctx, u % 2, top)

    def step(u, buf, ahead):
        ph, g, c1, c2, _, _ = unit(u)
        if ahead:
            ctx = score_begin(u + 1)
        top = None
        new_top = tops[buf][...]
        total = None
        for t in range(SPAN // TILE):
            if ahead:
                top = score_tile(ctx, 1 - buf, t, top)
            s = scores[buf][:, t * TILE:(t + 1) * TILE]
            weight = jnp.concatenate(
                [jnp.exp2((s[:, :HEAD] - new_top) * C), jnp.exp2((s[:, HEAD:] - new_top) * C)], 1
            ).astype(BF16)
            v = jnp.concatenate([key_tile(ph, t, KEYS), ones], 1)
            mixed = jnp.dot(weight, v, preferred_element_type=F32)
            total = mixed if total is None else total + mixed
        fresh_acc, fresh_sum = total[:, :HEAD], total[:, HEAD:]
        if ph % 2:
            alpha = alphas[buf][...]
            fresh_acc = stacked(acc, g, c1, c2) * alpha + fresh_acc
            fresh_sum = stacked(l_st, g, c1, c2) * alpha + fresh_sum
        unstack(acc, g, c1, c2, fresh_acc)
        unstack(l_st, g, c1, c2, fresh_sum)
        if ahead:
            score_end(ctx, 1 - buf, top)

    def gather_piece(g, c, r0, n, messages):
        rows = slice(r0, r0 + n)
        lanes = lax.broadcasted_iota(jnp.int32, (n, HEAD), 1)
        sums = jnp.ones((n, HEAD), F32)
        peak = jnp.zeros((n, HEAD), F32)
        for h in range(SHARE):
            cols = slice(h * HEAD, (h + 1) * HEAD)
            sums = jnp.where(lanes % 16 == h, l_st[g, c, rows, cols], sums)
            peak = jnp.where(lanes % 16 == h, m_st[g, c, rows, cols], peak)
        logs = [peak * C + jnp.log2(sums)]
        for ref, a in messages:
            p = ref[a:a + n, GW:MW].astype(F32)
            logs.append(p + pltpu.roll(p, 16, 1) + pltpu.roll(p, 32, 1) + pltpu.roll(p, 48, 1))
        top = functools.reduce(jnp.maximum, logs)
        weights = [jnp.exp2(item - top) for item in logs]
        total = functools.reduce(jnp.add, weights)
        share = 1.0 / total
        factors = [w * share for w in weights]
        factors[0] = factors[0] / sums
        out = []
        for h in range(SHARE):
            cols = slice(h * HEAD, (h + 1) * HEAD)
            spread = [jnp.broadcast_to(f[:, h:h + 1], (n, HEAD)) for f in factors]
            o = acc[g, c, rows, cols] * spread[0]
            for (ref, a), f in zip(messages, spread[1:]):
                o = o + ref[a:a + n, cols].astype(F32) * f
            out.append(o)
        return out, top + jnp.log2(total)

    def write_piece(dst, a, n, out, logs):
        for h in range(SHARE):
            dst[a:a + n, h * HEAD:(h + 1) * HEAD] = out[h].astype(BF16)
        lanes = lax.broadcasted_iota(jnp.int32, (n, HEAD), 1) // 16 % 4
        first = logs.astype(BF16).astype(F32)
        rest = logs - first
        second = rest.astype(BF16).astype(F32)
        third = rest - second
        parts = jnp.where(lanes == 0, first, jnp.where(lanes == 1, second, jnp.where(lanes == 2, third, 0.0)))
        dst[a:a + n, GW:MW] = parts.astype(BF16)

    def o_copy(d, hop, p):
        rows = slice(p * HALF, (p + 1) * HALF)
        return remote(
            sb0.at[d, hop, rows], mb0.at[d, hop, rows], sent.at[6], o_recv.at[d, hop, p], z_dev[d]
        )

    def ring(hop, first):
        todo = []
        for d in (0, 1):
            p = d if first else 1 - d
            messages = []
            if hop > 1 or (hop == 1 and first):
                need(f"o{hop - 1}{'T' if first else 'F'}")
                messages = [(mb0.at[d, hop - 1], p * HALF)]
            todo.append((d, p, (4 - hop) if d == 0 else (4 + hop), messages))
        pieces = [gather_piece(0, c, p * HALF, HALF, messages) for d, p, c, messages in todo]
        for (d, p, _, _), piece in zip(todo, pieces):
            write_piece(sb0.at[d, hop], p * HALF, HALF, *piece)
        for d, p, _, _ in todo:
            o_copy(d, hop, p).start()

    def p_copy(name):
        i, a, n = MSG[name]
        dev = y_dev if name[0] == "y" else x_dev[0 if "u" in name else 1]
        return remote(sb1.at[a:a + n], mb1.at[a:a + n], sent.at[7], p_recv.at[i], dev)

    def arrived(name, skip=0):
        return (mb1, MSG[name][1] + skip)

    def tree(name, c, r0, n, *needs):
        _, a, _ = MSG[name]
        write_piece(sb1, a, n, *gather_piece(1, c, r0, n, [arrived(*need) for need in needs]))
        p_copy(name).start()

    def split(name, c, parts):
        _, a, _ = MSG[name]
        for r0, needs in parts:
            write_piece(sb1, a + r0, 16, *gather_piece(1, c, r0, 16, needs))
        p_copy(name).start()

    def tree_y7():
        tree("y7", 7, 32, 32)

    def tree_xx1():
        tree("xx1u", 7, 0, 16)
        tree("xx1d", 7, 16, 16)

    def tree_x1():
        tree("x1u", 4, 0, 32)
        need("y7")
        tree("x1d", 4, 32, 32, ("y7",))

    def tree_y56():
        tree("y5", 5, 32, 32)
        tree("y6", 6, 32, 32)

    def tree_xx2():
        need("xx1")
        split("xx2u", 6, ((0, [arrived("xx1u")]), (16, [])))
        split("xx2d", 5, ((0, []), (16, [arrived("xx1d")])))

    def tree_x2():
        need("x1", "y56")
        tree("x2u0", 2, 0, 32, ("x1u",))
        tree("x2u1", 2, 32, 32, ("y6",))
        tree("x2d0", 1, 0, 32)
        tree("x2d1", 1, 32, 32, ("y5",), ("x1d",))

    def tree_yf():
        need("xx2")
        tree("yf", 3, 0, 32, ("xx2u",), ("xx2d",))

    def tree_y3():
        tree("y3", 3, 32, 32)

    trees = {
        "y7": tree_y7, "xx1": tree_xx1, "x1": tree_x1, "y56": tree_y56, "xx2": tree_xx2, "x2": tree_x2, "yf": tree_yf,
        "y3": tree_y3,
    }

    def finish(g, p, messages):
        out, _ = gather_piece(g, 0, p * HALF, HALF, messages)
        squares = jnp.zeros((HALF, HEAD), F32)
        for h in range(SHARE):
            o_ref[p * HALF:(p + 1) * HALF, g * GW + h * HEAD:g * GW + (h + 1) * HEAD] = out[h]
            squares = squares + out[h] * out[h]
        rows = slice(p * HALF, (p + 1) * HALF)
        if g == 0:
            sq_p[rows, :] = squares
        else:
            total = jnp.sum(squares + sq_p[rows, :], axis=1, keepdims=True)
            sq_p[rows, :] = jnp.broadcast_to(total, (HALF, HEAD))

    def o_out(g):
        cols = slice(g * GW, (g + 1) * GW)
        return pltpu.make_async_copy(o_ref.at[:, cols], o_hbm.at[:, cols], out_sem.at[g])

    def finish0():
        need("o3T", "o3F")
        for p in (0, 1):
            finish(0, p, [(mb0.at[d, 3], p * HALF) for d in (0, 1)])

    def retire():
        rz_copy.wait_recv()
        group = y * 2 + zhi
        for i in (0, 1):
            got = jnp.where(section_ref[group] == 0, tokens(i, group).astype(F32), 0.0)
            for source, ref, a in (
                ((1 - y) * 2 + zhi, rt_y, 0),
                (y * 2 + 1 - zhi, rz_r, 0),
                ((1 - y) * 2 + 1 - zhi, rz_r, 32),
            ):
                got = jnp.where(section_ref[source] == 0, ref[a + 16 * i:a + 16 * i + 16].astype(F32), got)
            fresh_ref[i] = got.astype(BF16)

    ready = set()

    def unit_needs(u):
        g, half, j = UNITS[u]
        if g == 0:
            need(*[f"zq{k}{p}" for k in range(j + 1) for p in "TF" if k < 3 or p == "T"])
            need("xkown_x", "xkown_y")
            if half:
                need("xkfwd", "xky12", "xkyx", "xkyf", "xky3")
        else:
            need("xqown_x", "xqown_y")
            if j < 2:
                need("xqfwd", "xqy12", "xqyx", "xqyf", "xqy3")
            need(*[f"zk{k}{p}" for k in range(4 if half else 2) for p in "TF" if k < 3 or p == "T"])
        if 2 * g + half not in ready:
            ready.add(2 * g + half)
            make_bias(2 * g + half)

    scored = done = 0
    for op in PLAN:
        if op == "S":
            unit_needs(scored)
            score_alone(scored)
            scored += 1
        elif op == "P":
            step(done, done % 2, False)
            done += 1
        elif op == "PS":
            unit_needs(scored)
            step(done, done % 2, True)
            scored += 1
            done += 1
        elif op == "clear_l":
            l_st[...] = jnp.zeros(l_st.shape, F32)
        elif op == "clear_acc":
            acc[...] = jnp.zeros(acc.shape, F32)
        elif op == "rt":
            rt_copy.start()
        elif op == "far":
            need("zq3T")
            far_retire()
        elif op in trees:
            trees[op]()
        elif op[0] == "o":
            ring(int(op[1]), op[2] == "T")
        else:
            begin(op)
    finish0()
    o_out(0).start()
    retire()
    need("x2", "y3", "yf")
    for p in (0, 1):
        finish(1, p, [arrived(f"x2u{p}"), arrived(f"x2d{p}"), arrived("yf" if p == 0 else "y3")])
    o_out(1).start()
    rows = jnp.concatenate([sq_p[...], jnp.zeros((HEAD - TOK, HEAD), F32)], 0)
    sq_s[...] = rows.T[0:8]
    sc = [remote(sq_s, sq_r.at[i], sent.at[8], h_recv.at[i], head_dev[i]) for i in range(3)]
    for copy in sc:
        copy.start()
    total = sq_s[...]
    for i, copy in enumerate(sc):
        copy.wait_recv()
        total = total + sq_r[i]
    total_ref[...] = total
    for g in (0, 1):
        o_out(g).wait()

    for i, refs in enumerate((
        (qg.at[0, 0:7],),
        (kv.at[0], kv.at[1, 0:3]),
        (kv.at[0], kv.at[1, 0:3]),
        (qg.at[0, 0:7],),
        (rt_s,),
        (rz_s,),
        (sb0.at[0], sb0.at[1, 0:3]),
        (sb1,),
        (sq_r,),
    )):
        for ref in refs:
            pltpu.make_async_copy(ref, ref, sent.at[i]).wait()


def finish_kernel(
    count_ref, o_hbm, total_ref, gain_ref, ck_hbm, cv_hbm, fresh_ref, out_hbm, nck_hbm, ncv_hbm,
    o_ref, out_ref, old_ref, new_ref, in_sem, out_sem,
):
    blocks = [slice(g * GW, (g + 1) * GW) for g in (0, 1)]
    loads = [pltpu.make_async_copy(a, old_ref.at[i], in_sem.at[i]) for i, a in enumerate((ck_hbm, cv_hbm))]
    loads += [pltpu.make_async_copy(o_hbm.at[:, b], o_ref.at[g], in_sem.at[2 + g]) for g, b in enumerate(blocks)]
    stores = [pltpu.make_async_copy(new_ref.at[i], a, out_sem.at[i]) for i, a in enumerate((nck_hbm, ncv_hbm))]
    stores += [pltpu.make_async_copy(out_ref.at[g], out_hbm.at[:, b], out_sem.at[2 + g]) for g, b in enumerate(blocks)]
    for copy in loads:
        copy.start()
    total = jnp.concatenate([total_ref[...]] * 16, 0).T[0:TOK]
    scale = lax.rsqrt(total / (HEADS * HEAD) + 1e-06)
    spot = lax.broadcasted_iota(jnp.int32, (CACHE, 16), 0) - lax.broadcasted_iota(jnp.int32, (CACHE, 16), 1)
    chosen = jnp.where(spot == count_ref[0], 1.0, 0.0).astype(BF16)
    row = lax.broadcasted_iota(jnp.int32, (CACHE, 256), 0) - count_ref[0]
    inside = (row >= 0) & (row < 16)
    for i in (0, 1):
        loads[i].wait()
        moved = jnp.dot(chosen, fresh_ref[i], preferred_element_type=F32)
        new_ref[i] = jnp.where(inside, moved, old_ref[i].astype(F32)).astype(BF16)
        stores[i].start()
    for g in (0, 1):
        loads[2 + g].wait()
        for h in range(SHARE):
            cols = slice(h * HEAD, (h + 1) * HEAD)
            gain = gain_ref[g * GW + h * HEAD:g * GW + (h + 1) * HEAD].reshape(1, HEAD)
            out_ref[g, :, cols] = o_ref[g, :, cols] * scale * gain
        stores[2 + g].start()
    for copy in stores:
        copy.wait()


def on_device(queries, keys, values, cache_keys, cache_values, cache_count, span_section, norm_gain):
    vmem = pl.BlockSpec(memory_space=pltpu.VMEM)
    smem = pl.BlockSpec(memory_space=pltpu.SMEM)
    hbm = pl.BlockSpec(memory_space=pl.ANY)
    dma = pltpu.SemaphoreType.DMA
    state = pltpu.VMEM((2, NZ, TOK, GW), F32)
    o, total, fresh = pl.pallas_call(
        kernel,
        out_shape=[
            jax.ShapeDtypeStruct((TOK, 2 * GW), F32),
            jax.ShapeDtypeStruct((8, HEAD), F32),
            jax.ShapeDtypeStruct((2, 16, 256), BF16),
        ],
        in_specs=[hbm] * 7,
        out_specs=[hbm, vmem, vmem],
        scratch_shapes=[
            pltpu.VMEM((2, NZ, TOK, GW), BF16),
            pltpu.VMEM((4, 4, KVR, HEAD), BF16),
            pltpu.VMEM((4, 2, 1, SPAN), F32),
            state, state, state,
            pltpu.VMEM((PAIR, SPAN), F32), pltpu.VMEM((PAIR, SPAN), F32),
            pltpu.VMEM((PAIR, HEAD), F32), pltpu.VMEM((PAIR, HEAD), F32),
            pltpu.VMEM((PAIR, HEAD), F32), pltpu.VMEM((PAIR, HEAD), F32),
            pltpu.VMEM((2, 4, TOK, MW), BF16), pltpu.VMEM((2, 4, TOK, MW), BF16),
            pltpu.VMEM((MSG_ROWS, MW), BF16), pltpu.VMEM((MSG_ROWS, MW), BF16),
            pltpu.VMEM((64, 256), BF16), pltpu.VMEM((64, 256), BF16),
            pltpu.VMEM((64, 256), BF16), pltpu.VMEM((64, 256), BF16),
            pltpu.VMEM((TOK, HEAD), F32),
            pltpu.VMEM((8, HEAD), F32),
            pltpu.VMEM((3, 8, HEAD), F32),
            pltpu.VMEM((TOK, 2 * GW), F32),
            pltpu.SMEM((1,), jnp.int32),
            pltpu.SMEM((4,), jnp.int32),
            dma((12,)), dma((2,)),
            dma((9,)), dma((2, 4, 2)), dma((2, 4, 2)), dma((12,)), dma((12,)), dma((2,)), dma((2, 4, 2)), dma((len(MSG),)),
            dma((3,)),
        ],
        compiler_params=pltpu.CompilerParams(
            collective_id=0, has_side_effects=True, vmem_limit_bytes=56 * 2**20
        ),
    )(queries, keys, values, cache_keys, cache_values, cache_count, span_section)
    return pl.pallas_call(
        finish_kernel,
        out_shape=[
            jax.ShapeDtypeStruct((TOK, 2 * GW), F32),
            jax.ShapeDtypeStruct((CACHE, 256), BF16),
            jax.ShapeDtypeStruct((CACHE, 256), BF16),
        ],
        in_specs=[smem, hbm, vmem, vmem, hbm, hbm, vmem],
        out_specs=[hbm] * 3,
        scratch_shapes=[
            pltpu.VMEM((2, TOK, GW), F32), pltpu.VMEM((2, TOK, GW), F32),
            pltpu.VMEM((2, CACHE, 256), BF16), pltpu.VMEM((2, CACHE, 256), BF16),
            dma((4,)), dma((4,)),
        ],
        compiler_params=pltpu.CompilerParams(vmem_limit_bytes=56 * 2**20),
    )(cache_count, o, total, norm_gain, cache_keys, cache_values, fresh)


def solution(mesh):
    placed = (
        P("slot", "head"),
        P("slot", "head"),
        P("slot", "head"),
        P("slot", "head"),
        P("slot", "head"),
        P("slot"),
        P(),
        P("head"),
    )
    return jax.shard_map(
        on_device,
        mesh=mesh,
        in_specs=placed,
        out_specs=(P("slot", "head"), P("slot", "head"), P("slot", "head")),
        check_vma=False,
    )
```
